32 devices in a mesh: replica: 4 (over y, x), shard: 8 (over z, core).
Axes of the slice: x: 2, y: 2, z: 4, core: 2. Of those that a mesh axis runs over, the one named last changes fastest.
Arguments:
- hidden: bfloat16 [2, 32, 256, 768], P(None, ('replica', 'shard')), may hold values from -6 to 6
- encoded: bfloat16 [2, 32, 256, 768], P(None, ('replica', 'shard')), may hold values from -6 to 6
- out_grad: bfloat16 [2, 32, 256, 768], P(None, ('replica', 'shard')), may hold values from -6 to 6
- seg_start: int32 [2, 32, 13], P(None, ('replica', 'shard')), may hold values from 0 to 240, as said below
- seg_parent: int32 [2, 32, 13], P(None, ('replica', 'shard')), may hold values from 0 to 4, as said below
- bucket_of_distance: int32 [256], replicated, may hold values from 0 to 31, as said below
- norm_self: bfloat16 [768], P('shard'), may hold values from 0.5 to 1.5
- self_query: bfloat16 [768, 768], P('shard'), may hold values from -0.109375 to 0.109375
- self_key: bfloat16 [768, 768], P('shard'), may hold values from -0.109375 to 0.109375
- self_value: bfloat16 [768, 768], P('shard'), may hold values from -0.21875 to 0.21875
- self_out: bfloat16 [768, 768], P('shard'), may hold values from -0.875 to 0.875
- rel_bias: bfloat16 [32, 12], P('shard'), may hold values from -4 to 4
- norm_cross: bfloat16 [768], P('shard'), may hold values from 0.5 to 1.5
- cross_query: bfloat16 [768, 768], P('shard'), may hold values from -0.109375 to 0.109375
- cross_key: bfloat16 [768, 768], P('shard'), may hold values from -0.109375 to 0.109375
- cross_value: bfloat16 [768, 768], P('shard'), may hold values from -0.21875 to 0.21875
- cross_out: bfloat16 [768, 768], P('shard'), may hold values from -0.875 to 0.875
- norm_ff: bfloat16 [768], P('shard'), may hold values from 0.5 to 1.5
- ff_gate: bfloat16 [768, 2048], P('shard'), may hold values from -0.21875 to 0.21875
- ff_up: bfloat16 [768, 2048], P('shard'), may hold values from -0.21875 to 0.21875
- ff_down: bfloat16 [2048, 768], P('shard'), may hold values from -0.125 to 0.125
Outputs:
- layer_out: bfloat16 [2, 32, 256, 768], P(None, ('replica', 'shard'))
- grad_hidden: bfloat16 [2, 32, 256, 768], P(None, ('replica', 'shard'))
- grad_encoded: bfloat16 [2, 32, 256, 768], P(None, ('replica', 'shard'))
- grad_norm_self: float32 [768], P('shard')
- grad_self_query: float32 [768, 768], P('shard')
- grad_self_key: float32 [768, 768], P('shard')
- grad_self_value: float32 [768, 768], P('shard')
- grad_self_out: float32 [768, 768], P('shard')
- grad_rel_bias: float32 [32, 12], P('shard')
- grad_norm_cross: float32 [768], P('shard')
- grad_cross_query: float32 [768, 768], P('shard')
- grad_cross_key: float32 [768, 768], P('shard')
- grad_cross_value: float32 [768, 768], P('shard')
- grad_cross_out: float32 [768, 768], P('shard')
- grad_norm_ff: float32 [768], P('shard')
- grad_ff_gate: float32 [768, 2048], P('shard')
- grad_ff_up: float32 [768, 2048], P('shard')
- grad_ff_down: float32 [2048, 768], P('shard')
The draws below stay inside these ranges and needn't reach their ends.
Inputs may be any that keep to these rules, and one draw needn't show every extreme that they name: `seg_start`: segment 0 is the trunk and starts at 0; the twelve other segments lie end to end after it in some order, each once. `seg_parent`: segments 0 to 4 have parent 0; each of segments 1 to 4 is the parent of exactly two of segments 5 to 12. `bucket_of_distance`: entry 0 is 0; from one distance to the next it rises by 1 or 2 until it reaches 31, and then stays.
All inputs are finite; a program needn't handle non-finite values.
Results may differ from the reference program's by a relative error of at most 0.03.
The reference program's roundings to bfloat16 on the way count: a program that leaves them out, or rounds other values in their place, can miss the bound.
Values may be sent and summed in bfloat16 or wider, within the bound.
A program may use at most 192 MiB of HBM per device.

```python
import jax
import jax.numpy as jnp
from jax import lax

D = 768
H = 12
DH = 64
FF = 2048
NB = 32
NSEG = 13
TRUNK = 64
BRANCH = 16
LEAF = 16
ENC = 256
MB = 2
TREE = 256
TREES = 32


def tree_draws(key):
    base_key = jax.random.fold_in(key, 7)
    tree_keys = jax.random.split(base_key, MB * TREES)

    def one_tree(tree_key):
        order_key, parent_key = jax.random.split(tree_key)
        order = (jax.random.permutation(order_key, NSEG - 1) + 1).astype(jnp.int32)
        seg_index = jnp.arange(NSEG, dtype=jnp.int32)
        seg_len = jnp.where(seg_index == 0, TRUNK, jnp.where(seg_index <= 4, BRANCH, LEAF)).astype(jnp.int32)
        lengths = jnp.take(seg_len, order)
        starts_in_order = (TRUNK + jnp.cumsum(lengths) - lengths).astype(jnp.int32)
        start = jnp.zeros((NSEG,), jnp.int32).at[order].set(starts_in_order)
        leaf_parent = jax.random.permutation(parent_key, jnp.arange(8, dtype=jnp.int32) // 2 + 1).astype(jnp.int32)
        parent = jnp.concatenate([jnp.zeros((5,), jnp.int32), leaf_parent])
        return (start, parent)
    starts, parents = jax.vmap(one_tree)(tree_keys)
    return (starts.reshape(MB, TREES, NSEG), parents.reshape(MB, TREES, NSEG))


def draw_seg_start(key, part):
    return tree_draws(key)[0]


def draw_seg_parent(key, part):
    return tree_draws(key)[1]


def draw_bucket_of_distance(key, part):
    steps = jax.random.randint(jax.random.fold_in(key, 11), (TREE,), 1, 3).astype(jnp.int32)
    steps = steps.at[0].set(0)
    return jnp.minimum(jnp.cumsum(steps), NB - 1).astype(jnp.int32)


def level_of(stream_key, dims, cuts, smallest, largest):
    loudness, own = 1.0, jax.random.fold_in(stream_key, 6)
    for position, parts in cuts:
        steps = jnp.exp(jax.random.uniform(jax.random.fold_in(own, position), (parts,), jnp.float32, smallest / len(cuts), largest / len(cuts)))
        loudness = loudness * jnp.repeat(steps, dims[position] // parts).reshape([-1 if axis == position else 1 for axis in range(len(dims))])
    return loudness


def normal_values(own_key, dims, spread, reach, cuts=(), kind=jnp.bfloat16):
    drawn = spread * jax.random.normal(own_key, dims, jnp.float32)
    if cuts:
        drawn = drawn * level_of(own_key, dims, cuts, -0.22, 0.18)
    return jnp.clip(drawn, -reach, reach).astype(kind)


def setup_inputs(seed: int = 0) -> dict:
    splits = jax.random.split(jax.random.key(seed), 22)
    return {
        "hidden": normal_values(splits[0], (MB, TREES, TREE, D), 1.0, 6.0, ((1, 32),)),
        "encoded": normal_values(splits[1], (MB, TREES, ENC, D), 1.0, 6.0, ((1, 32),)),
        "out_grad": normal_values(splits[2], (MB, TREES, TREE, D), 1.0, 6.0, ((1, 32),)),
        "seg_start": draw_seg_start(jax.random.fold_in(splits[21], 71), 0),
        "seg_parent": draw_seg_parent(jax.random.fold_in(splits[21], 71), 0),
        "bucket_of_distance": draw_bucket_of_distance(jax.random.fold_in(splits[21], 71), 0),
        "norm_self": jnp.clip(1.0 + 0.1 * jax.random.normal(splits[6], (D,), jnp.float32), 0.5, 1.5).astype(jnp.bfloat16),
        "self_query": normal_values(splits[7], (D, D), (4 * D) ** -0.5, 0.109375, ((0, 8),)),
        "self_key": normal_values(splits[8], (D, D), (4 * D) ** -0.5, 0.109375, ((0, 8),)),
        "self_value": normal_values(splits[9], (D, D), D ** -0.5, 0.21875, ((0, 8),)),
        "self_out": normal_values(splits[10], (D, D), (D // 16) ** -0.5, 0.875, ((0, 8),)),
        "rel_bias": normal_values(splits[11], (NB, H), 1.0, 4.0, ((0, 8),)),
        "norm_cross": jnp.clip(1.0 + 0.1 * jax.random.normal(splits[12], (D,), jnp.float32), 0.5, 1.5).astype(jnp.bfloat16),
        "cross_query": normal_values(splits[13], (D, D), (4 * D) ** -0.5, 0.109375, ((0, 8),)),
        "cross_key": normal_values(splits[14], (D, D), (4 * D) ** -0.5, 0.109375, ((0, 8),)),
        "cross_value": normal_values(splits[15], (D, D), D ** -0.5, 0.21875, ((0, 8),)),
        "cross_out": normal_values(splits[16], (D, D), (D // 16) ** -0.5, 0.875, ((0, 8),)),
        "norm_ff": jnp.clip(1.0 + 0.1 * jax.random.normal(splits[17], (D,), jnp.float32), 0.5, 1.5).astype(jnp.bfloat16),
        "ff_gate": normal_values(splits[18], (D, FF), D ** -0.5, 0.21875, ((0, 8),)),
        "ff_up": normal_values(splits[19], (D, FF), D ** -0.5, 0.21875, ((0, 8),)),
        "ff_down": normal_values(splits[20], (FF, D), FF ** -0.5, 0.125, ((0, 8),)),
    }


EPSILON = 1e-06
NEGATIVE = -1000000000.0
PRECISE = lax.Precision.HIGHEST

@jax.custom_vjp
def low(v):
    return lax.optimization_barrier(v.astype(jnp.bfloat16)).astype(jnp.float32)

@jax.custom_vjp
def low_back(v):
    return v

def low_keep(v):
    return (low(v), None)

def low_pass(kept, grad):
    return (grad,)

def back_keep(v):
    return (v, None)

def back_low(kept, grad):
    return (low(grad),)
low.defvjp(low_keep, low_pass)
low_back.defvjp(back_keep, back_low)

def tree_layout(start, parent, bucket_of_distance):
    seg_index = jnp.arange(NSEG, dtype=jnp.int32)
    seg_len = jnp.where(seg_index == 0, TRUNK, jnp.where(seg_index <= 4, BRANCH, LEAF)).astype(jnp.int32)
    seg_depth = jnp.where(seg_index == 0, 0, jnp.where(seg_index <= 4, TRUNK, TRUNK + BRANCH)).astype(jnp.int32)
    token_place = jnp.arange(TREE, dtype=jnp.int32)
    member = ((token_place[:, None] >= start[None, :]) & (token_place[:, None] < (start + seg_len)[None, :])).astype(jnp.int32)
    token_depth = lax.optimization_barrier(jnp.sum(member * (seg_depth - start)[None, :], axis=1)) + token_place
    parent_hot = (parent[:, None] == seg_index[None, :]).astype(jnp.int32)
    grand_parent = jnp.dot(parent_hot, parent_hot)
    ancestry = jnp.eye(NSEG, dtype=jnp.int32) + parent_hot + grand_parent
    seg_reach = jnp.dot(jnp.dot(member, ancestry), member.T)
    allowed = (seg_reach > 0) & (token_depth[None, :] <= token_depth[:, None])
    distance = jnp.clip(token_depth[:, None] - token_depth[None, :], 0, TREE - 1).astype(jnp.int32)
    bucket = jnp.take(bucket_of_distance, distance)
    onehot = bucket[:, :, None] == jnp.arange(NB, dtype=jnp.int32)[None, None, :]
    return (allowed, onehot)

def rms_norm(values_in, gain):
    return values_in * lax.rsqrt(lax.optimization_barrier(jnp.mean(values_in * values_in, axis=-1, keepdims=True)) + EPSILON) * gain

def product(left, right):
    return jnp.dot(left, right, precision=PRECISE)

def attend(queries, keys_in, values_in, score_bias, allowed):
    split_q = queries.reshape(queries.shape[0], H, DH)
    split_k = keys_in.reshape(keys_in.shape[0], H, DH)
    split_v = values_in.reshape(values_in.shape[0], H, DH)
    scores = jnp.einsum('ihd,jhd->hij', split_q, split_k, precision=PRECISE)
    if score_bias is not None:
        scores = jnp.where(allowed[None], scores + score_bias, NEGATIVE)
    scores = low_back(scores)
    soft_weights = low(jax.nn.softmax(scores, axis=-1))
    context = jnp.einsum('hij,jhd->ihd', soft_weights, split_v, precision=PRECISE)
    return low(low_back(context.reshape(queries.shape[0], D)))

def tree_layer(params, inputs, encoder, start, parent, bucket_of_distance):
    gain_self, w_query, w_key, w_value, w_out, bias_table, gain_cross, c_query, c_key, c_value, c_out, gain_ff, w_gate, w_up, w_down = params
    allowed, onehot = tree_layout(start, parent, bucket_of_distance)
    score_bias = jnp.einsum('ijb,bh->hij', onehot.astype(jnp.float32), bias_table, precision=PRECISE)
    normed_self = low(rms_norm(inputs, gain_self))
    self_queries = low(low_back(product(normed_self, w_query)))
    self_keys = low(low_back(product(normed_self, w_key)))
    self_values = low(low_back(product(normed_self, w_value)))
    self_context = attend(self_queries, self_keys, self_values, score_bias, allowed)
    after_self = inputs + low_back(product(self_context, w_out))
    normed_cross = low(rms_norm(after_self, gain_cross))
    cross_queries = low(low_back(product(normed_cross, c_query)))
    cross_keys = low(low_back(product(encoder, c_key)))
    cross_values = low(low_back(product(encoder, c_value)))
    cross_context = attend(cross_queries, cross_keys, cross_values, None, None)
    after_cross = after_self + low_back(product(cross_context, c_out))
    normed_ff = low(rms_norm(after_cross, gain_ff))
    gate = low_back(product(normed_ff, w_gate))
    up_proj = low_back(product(normed_ff, w_up))
    inner = low(jax.nn.gelu(gate, approximate=True) * up_proj)
    return after_cross + low_back(product(inner, w_down))

def reference(hidden, encoded, out_grad, seg_start, seg_parent, bucket_of_distance, norm_self, self_query, self_key, self_value, self_out, rel_bias, norm_cross, cross_query, cross_key, cross_value, cross_out, norm_ff, ff_gate, ff_up, ff_down):
    params = tuple((weight.astype(jnp.float32) for weight in (norm_self, self_query, self_key, self_value, self_out, rel_bias, norm_cross, cross_query, cross_key, cross_value, cross_out, norm_ff, ff_gate, ff_up, ff_down)))
    count = MB * TREES
    inputs_flat = hidden.astype(jnp.float32).reshape(count, TREE, D)
    encoder_flat = encoded.astype(jnp.float32).reshape(count, ENC, D)
    starts_flat = seg_start.reshape(count, NSEG).astype(jnp.int32)
    parents_flat = seg_parent.reshape(count, NSEG).astype(jnp.int32)
    cotangent = out_grad.astype(jnp.float32).reshape(count, TREE, D)

    def forward(weights, inputs_all, encoder_all):
        tree_fn = jax.checkpoint(lambda p_w, x_in, e_in, s_in, r_in: tree_layer(p_w, x_in, e_in, s_in, r_in, bucket_of_distance))
        return lax.map(lambda tree_item: tree_fn(weights, tree_item[0], tree_item[1], tree_item[2], tree_item[3]), (inputs_all, encoder_all, starts_flat, parents_flat))
    outputs, pullback = jax.vjp(forward, params, inputs_flat, encoder_flat)
    grads, grad_inputs, grad_encoder = pullback(cotangent)
    g_norm_self, g_self_query, g_self_key, g_self_value, g_self_out, g_rel_bias, g_norm_cross, g_cross_query, g_cross_key, g_cross_value, g_cross_out, g_norm_ff, g_ff_gate, g_ff_up, g_ff_down = grads
    return (outputs.astype(jnp.bfloat16).reshape(MB, TREES, TREE, D), grad_inputs.astype(jnp.bfloat16).reshape(MB, TREES, TREE, D), grad_encoder.astype(jnp.bfloat16).reshape(MB, TREES, ENC, D), g_norm_self, g_self_query, g_self_key, g_self_value, g_self_out, g_rel_bias, g_norm_cross, g_cross_query, g_cross_key, g_cross_value, g_cross_out, g_norm_ff, g_ff_gate, g_ff_up, g_ff_down)
```

```python
import functools
import jax
import jax.numpy as jnp
from jax import lax
from jax.experimental import pallas as pl
from jax.experimental.pallas import tpu as pltpu
from jax.sharding import PartitionSpec as P

D = 768
H = 12
DH = 64
NB = 32
NSEG = 13
TRUNK = 64
BRANCH = 16
LEAF = 16
TREE = 256


EPSILON = 1e-06
NEGATIVE = -1000000000.0


def bucket_bounds(bucket_of_distance):
    levels = jnp.arange(NB + 1, dtype=jnp.int32)
    below = (bucket_of_distance[:, None] < levels[None, :]).astype(jnp.int32)
    return jnp.sum(below, axis=0)


def tree_layout(start, parent, bounds):
    seg_index = jnp.arange(NSEG, dtype=jnp.int32)
    seg_len = jnp.where(seg_index == 0, TRUNK, jnp.where(seg_index <= 4, BRANCH, LEAF)).astype(
        jnp.int32
    )
    seg_depth = jnp.where(
        seg_index == 0, 0, jnp.where(seg_index <= 4, TRUNK, TRUNK + BRANCH)
    ).astype(jnp.int32)
    token_place = jnp.arange(TREE, dtype=jnp.int32)
    member = (
        (token_place[:, None] >= start[None, :])
        & (token_place[:, None] < (start + seg_len)[None, :])
    ).astype(jnp.int32)
    token_depth = jnp.sum(member * (seg_depth - start)[None, :], axis=1) + token_place
    parent_hot = (parent[:, None] == seg_index[None, :]).astype(jnp.int32)
    grand_parent = jnp.dot(parent_hot, parent_hot)
    ancestry = jnp.eye(NSEG, dtype=jnp.int32) + parent_hot + grand_parent
    seg_reach = jnp.dot(jnp.dot(member, ancestry), member.T)
    allowed = (seg_reach > 0) & (token_depth[None, :] <= token_depth[:, None])
    distance = jnp.clip(token_depth[:, None] - token_depth[None, :], 0, TREE - 1)
    lower = bounds[:NB]
    upper = bounds[1:]
    onehot = (
        (distance[:, :, None] >= lower[None, None, :])
        & (distance[:, :, None] < upper[None, None, :])
    ).astype(jnp.bfloat16)
    return (allowed, onehot)


def normed(values_in, gain):
    return (
        values_in
        * lax.rsqrt(jnp.mean(values_in * values_in, axis=-1, keepdims=True) + EPSILON)
        * gain
    )


def project(left, right):
    return jnp.dot(left, right, preferred_element_type=jnp.float32)


def outer_sum(left, right):
    return jnp.einsum("sd,se->de", left, right, preferred_element_type=jnp.float32)


def back_project(grad_rows, weight):
    return jnp.einsum("se,de->sd", grad_rows, weight, preferred_element_type=jnp.float32)


def split_heads(matrix):
    return matrix.reshape(matrix.shape[0], H, DH)


def attend_scores(queries, keys_in, score_bias, allowed):
    scores = jnp.einsum(
        "ihd,jhd->hij",
        split_heads(queries),
        split_heads(keys_in),
        preferred_element_type=jnp.float32,
    )
    if score_bias is not None:
        scores = jnp.where(allowed[None], scores + score_bias, NEGATIVE)
    return scores


def attend_forward(queries, keys_in, values_in, score_bias, allowed):
    scores = attend_scores(queries, keys_in, score_bias, allowed)
    row_max = jnp.max(scores, axis=-1, keepdims=True)
    shifted = jnp.exp(scores - row_max)
    row_sum = jnp.sum(shifted, axis=-1, keepdims=True)
    soft_weights = (shifted / row_sum).astype(jnp.bfloat16)
    context = jnp.einsum(
        "hij,jhd->ihd", soft_weights, split_heads(values_in), preferred_element_type=jnp.float32
    )
    return (context.reshape(queries.shape[0], D).astype(jnp.bfloat16), row_max + jnp.log(row_sum))


def attend_backward(queries, keys_in, values_in, score_bias, allowed, log_sum, grad_context):
    scores = attend_scores(queries, keys_in, score_bias, allowed)
    probs = jnp.exp(scores - log_sum)
    soft_weights = probs.astype(jnp.bfloat16)
    grad_heads = split_heads(grad_context)
    grad_values = jnp.einsum(
        "hij,ihd->jhd", soft_weights, grad_heads, preferred_element_type=jnp.float32
    )
    grad_probs = jnp.einsum(
        "ihd,jhd->hij", grad_heads, split_heads(values_in), preferred_element_type=jnp.float32
    )
    grad_scores = (
        probs * (grad_probs - jnp.sum(grad_probs * probs, axis=-1, keepdims=True))
    ).astype(jnp.bfloat16)
    grad_queries = jnp.einsum(
        "hij,jhd->ihd", grad_scores, split_heads(keys_in), preferred_element_type=jnp.float32
    )
    grad_keys = jnp.einsum(
        "hij,ihd->jhd", grad_scores, split_heads(queries), preferred_element_type=jnp.float32
    )
    return (
        grad_queries.reshape(queries.shape[0], D).astype(jnp.bfloat16),
        grad_keys.reshape(keys_in.shape[0], D).astype(jnp.bfloat16),
        grad_values.reshape(values_in.shape[0], D).astype(jnp.bfloat16),
        grad_scores,
    )


def tree_forward(weights, inputs_bf, encoder, start, parent, bounds):
    (
        gain_self,
        w_query,
        w_key,
        w_value,
        w_out,
        bias_table,
        gain_cross,
        c_query,
        c_key,
        c_value,
        c_out,
        gain_ff,
        w_gate,
        w_up,
        w_down,
    ) = weights
    allowed, onehot = tree_layout(start, parent, bounds)
    score_bias = jnp.einsum("ijb,bh->hij", onehot, bias_table, preferred_element_type=jnp.float32)
    inputs = inputs_bf.astype(jnp.float32)
    normed_self = normed(inputs, gain_self.astype(jnp.float32)).astype(jnp.bfloat16)
    self_queries = project(normed_self, w_query).astype(jnp.bfloat16)
    self_keys = project(normed_self, w_key).astype(jnp.bfloat16)
    self_values = project(normed_self, w_value).astype(jnp.bfloat16)
    self_context, self_lse = attend_forward(
        self_queries, self_keys, self_values, score_bias, allowed
    )
    after_self = inputs + project(self_context, w_out)
    normed_cross = normed(after_self, gain_cross.astype(jnp.float32)).astype(jnp.bfloat16)
    cross_queries = project(normed_cross, c_query).astype(jnp.bfloat16)
    cross_keys = project(encoder, c_key).astype(jnp.bfloat16)
    cross_values = project(encoder, c_value).astype(jnp.bfloat16)
    cross_context, cross_lse = attend_forward(cross_queries, cross_keys, cross_values, None, None)
    after_cross = after_self + project(cross_context, c_out)
    normed_ff = normed(after_cross, gain_ff.astype(jnp.float32)).astype(jnp.bfloat16)
    gate = project(normed_ff, w_gate)
    up_proj = project(normed_ff, w_up)
    inner = (jax.nn.gelu(gate, approximate=True) * up_proj).astype(jnp.bfloat16)
    layer_out = (after_cross + project(inner, w_down)).astype(jnp.bfloat16)
    saved = (
        after_self,
        after_cross,
        normed_self,
        self_queries,
        self_keys,
        self_values,
        self_context,
        self_lse,
        normed_cross,
        cross_queries,
        cross_keys,
        cross_values,
        cross_context,
        cross_lse,
        normed_ff,
        gate,
        up_proj,
        inner,
        allowed,
        onehot,
        score_bias,
    )
    return (layer_out, saved)


def tree_backward(weights, inputs_bf, encoder, grad_out, saved):
    (
        gain_self,
        w_query,
        w_key,
        w_value,
        w_out,
        bias_table,
        gain_cross,
        c_query,
        c_key,
        c_value,
        c_out,
        gain_ff,
        w_gate,
        w_up,
        w_down,
    ) = weights
    (
        after_self,
        after_cross,
        normed_self,
        self_queries,
        self_keys,
        self_values,
        self_context,
        self_lse,
        normed_cross,
        cross_queries,
        cross_keys,
        cross_values,
        cross_context,
        cross_lse,
        normed_ff,
        gate,
        up_proj,
        inner,
        allowed,
        onehot,
        score_bias,
    ) = saved
    inputs = inputs_bf.astype(jnp.float32)
    grad_w_down = outer_sum(inner, grad_out)
    grad_inner = back_project(grad_out, w_down)
    _, gelu_pull = jax.vjp(
        lambda gate_in, up_in: jax.nn.gelu(gate_in, approximate=True) * up_in, gate, up_proj
    )
    grad_gate, grad_up = gelu_pull(grad_inner)
    grad_gate = grad_gate.astype(jnp.bfloat16)
    grad_up = grad_up.astype(jnp.bfloat16)
    grad_w_gate = outer_sum(normed_ff, grad_gate)
    grad_w_up = outer_sum(normed_ff, grad_up)
    grad_normed_ff = back_project(grad_gate, w_gate) + back_project(grad_up, w_up)
    _, norm_pull = jax.vjp(normed, after_cross, gain_ff.astype(jnp.float32))
    grad_part, grad_gain_ff = norm_pull(grad_normed_ff)
    grad_after_cross = grad_out.astype(jnp.float32) + grad_part
    cross_branch = grad_after_cross.astype(jnp.bfloat16)
    grad_c_out = outer_sum(cross_context, cross_branch)
    grad_cross_context = back_project(cross_branch, c_out).astype(jnp.bfloat16)
    grad_cq, grad_ck, grad_cv, _ = attend_backward(
        cross_queries, cross_keys, cross_values, None, None, cross_lse, grad_cross_context
    )
    grad_c_query = outer_sum(normed_cross, grad_cq)
    grad_c_key = outer_sum(encoder, grad_ck)
    grad_c_value = outer_sum(encoder, grad_cv)
    grad_encoder = (back_project(grad_ck, c_key) + back_project(grad_cv, c_value)).astype(
        jnp.bfloat16
    )
    _, norm_pull = jax.vjp(normed, after_self, gain_cross.astype(jnp.float32))
    grad_part, grad_gain_cross = norm_pull(back_project(grad_cq, c_query))
    grad_after_self = grad_after_cross + grad_part
    self_branch = grad_after_self.astype(jnp.bfloat16)
    grad_w_out = outer_sum(self_context, self_branch)
    grad_self_context = back_project(self_branch, w_out).astype(jnp.bfloat16)
    grad_sq, grad_sk, grad_sv, grad_scores = attend_backward(
        self_queries, self_keys, self_values, score_bias, allowed, self_lse, grad_self_context
    )
    grad_bias_table = jnp.einsum(
        "hij,ijb->bh", grad_scores, onehot, preferred_element_type=jnp.float32
    )
    grad_w_query = outer_sum(normed_self, grad_sq)
    grad_w_key = outer_sum(normed_self, grad_sk)
    grad_w_value = outer_sum(normed_self, grad_sv)
    grad_normed_self = (
        back_project(grad_sq, w_query)
        + back_project(grad_sk, w_key)
        + back_project(grad_sv, w_value)
    )
    _, norm_pull = jax.vjp(normed, inputs, gain_self.astype(jnp.float32))
    grad_part, grad_gain_self = norm_pull(grad_normed_self)
    grad_inputs = (grad_after_self + grad_part).astype(jnp.bfloat16)
    grads = (
        grad_gain_self,
        grad_w_query,
        grad_w_key,
        grad_w_value,
        grad_w_out,
        grad_bias_table,
        grad_gain_cross,
        grad_c_query,
        grad_c_key,
        grad_c_value,
        grad_c_out,
        grad_gain_ff,
        grad_w_gate,
        grad_w_up,
        grad_w_down,
    )
    return (grad_inputs, grad_encoder, grads)


MESH = pl.DeviceIdType.MESH
SQ, FFN = 768, 2048
TEAM_R, TEAM_S = 4, 8
NZ = TEAM_S // 2

class Team:
    def __init__(self, shard_count):
        self.fold = shard_count // TEAM_S
        r = lax.axis_index("replica")
        s = lax.axis_index("shard")
        self.base_r = (r // TEAM_R) * TEAM_R
        self.q = r % TEAM_R
        self.off_s = s % self.fold
        self.s = s // self.fold
        self.z = self.s // 2
        self.c = self.s % 2
    def dev(self, q, s):
        return (self.base_r + q, s * self.fold + self.off_s)
    def flip(self, q, bit):
        if bit == 1:
            return q + 1 - 2 * (q % 2)
        return q + 2 - 4 * (q // 2)
    @property
    def qx(self): return self.flip(self.q, 1)
    @property
    def qy(self): return self.flip(self.q, 2)
    @property
    def qd(self): return 3 - self.q

def rcopy(src, dst, ss, rs, dev):
    return pltpu.make_async_remote_copy(src_ref=src, dst_ref=dst, send_sem=ss, recv_sem=rs, device_id=dev, device_id_type=MESH)

def enter(devs):
    b = pltpu.get_barrier_semaphore()
    for d in devs:
        pl.semaphore_signal(b, inc=1, device_id=d, device_id_type=MESH)
    pl.semaphore_wait(b, len(devs))


PH = 4
def piece(bufs, p, q, z, c, half=None):
    sq, gu, dn = bufs
    if p < 2:
        ref = sq.at[p * 4 + q, z, c]; n = SQ
    elif p == 2:
        ref = gu.at[q // 2, z, c, q % 2]; n = FFN
    else:
        ref = dn.at[z, c, q]; n = SQ
    if half is not None:
        ref = ref.at[:, pl.ds(half * (n // 2), n // 2)]
    return ref
def own_all(bufs, p, z, c):
    sq, gu, dn = bufs
    if p < 2: return sq.at[pl.ds(p * 4, 4), z, c]
    if p == 2: return gu.at[:, z, c]
    return dn.at[z, c]
def sib_all(bufs, p, c):
    sq, gu, dn = bufs
    if p < 2: return sq.at[pl.ds(p * 4, 4), :, c]
    if p == 2: return gu.at[:, :, c]
    return dn.at[:, c]

def gather_kernel(sharded, *refs):
    shards = refs[:11]
    sq, gu, dn = bufs = refs[11:14]
    (lsem, zs, zr, xs, xr, ys, yr, dxs, dxr, dys, dyr, cs, cr) = refs[14:]
    t = Team(sharded)
    q, z, c = t.q, t.z, t.c
    sib = t.dev(q, z * 2 + 1 - c)
    xn, yn = t.dev(t.qx, t.s), t.dev(t.qy, t.s)
    def zdev(k): return t.dev(q, ((z + k) % NZ) * 2 + c)
    def zsrc(k): return (z + NZ - k) % NZ
    loc = []
    for i in range(8):
        loc.append(pltpu.make_async_copy(shards[i], sq.at[i, z, c], lsem.at[i]))
    for i in range(2):
        for h in range(2):
            loc.append(pltpu.make_async_copy(shards[8 + i].at[pl.ds(h*48,48)], gu.at[i, z, c, h], lsem.at[8 + 2*i+h]))
    for h in range(4):
        loc.append(pltpu.make_async_copy(shards[10].at[pl.ds(h*64,64)], dn.at[z, c, h], lsem.at[12+h]))
    for l in loc: l.start()
    enter([sib, xn, yn] + [zdev(k) for k in range(1, NZ)])
    for l in loc: l.wait()
    sends = []
    def go(cp):
        cp.start(); sends.append(cp)
    def s1(p):
        for k in range(1, NZ):
            go(rcopy(piece(bufs, p, q, z, c), piece(bufs, p, q, z, c), zs.at[p, k], zr.at[p, k], zdev(k)))
    def s0(p):
        a = own_all(bufs, p, z, c)
        go(rcopy(a, a, cs.at[p, 0], cr.at[p], sib))
    def wrecv(ref, sem):
        rcopy(ref, ref, sem, sem, sib).wait_recv()
    def zstep(p, k):
        ref = piece(bufs, p, q, zsrc(k), c)
        wrecv(ref, zr.at[p, k])
        go(rcopy(ref, ref, xs.at[p, k], xr.at[p, k], xn))
        go(rcopy(ref, ref, ys.at[p, k], yr.at[p, k], yn))
        go(rcopy(ref, ref, cs.at[p, 5 * k - 4], cr.at[p], sib))
    def xystep(p, k):
        ref = piece(bufs, p, t.qx, zsrc(k), c)
        wrecv(ref, xr.at[p, k])
        h = piece(bufs, p, t.qx, zsrc(k), c, 0)
        go(rcopy(h, h, dys.at[p, k], dyr.at[p, k], yn))
        go(rcopy(ref, ref, cs.at[p, 5 * k - 3], cr.at[p], sib))
        ref = piece(bufs, p, t.qy, zsrc(k), c)
        wrecv(ref, yr.at[p, k])
        h = piece(bufs, p, t.qy, zsrc(k), c, 1)
        go(rcopy(h, h, dxs.at[p, k], dxr.at[p, k], xn))
        go(rcopy(ref, ref, cs.at[p, 5 * k - 2], cr.at[p], sib))
    def dstep(p, k):
        h = piece(bufs, p, t.qd, zsrc(k), c, 0)
        wrecv(h, dyr.at[p, k])
        go(rcopy(h, h, cs.at[p, 5 * k - 1], cr.at[p], sib))
        h = piece(bufs, p, t.qd, zsrc(k), c, 1)
        wrecv(h, dxr.at[p, k])
        go(rcopy(h, h, cs.at[p, 5 * k], cr.at[p], sib))
    s1(0); s0(0); s1(1); s0(1)
    steps = [(p, k) for p in range(PH) for k in range(1, NZ)]
    n = len(steps)
    for i in range(n + 2):
        if i < n:
            p, k = steps[i]
            if k == 1 and p + 2 < PH:
                s1(p + 2); s0(p + 2)
            zstep(p, k)
        if 1 <= i < n + 1: xystep(*steps[i - 1])
        if 2 <= i < n + 2: dstep(*steps[i - 2])
    for p in range(PH):
        wrecv(sib_all(bufs, p, 1 - c), cr.at[p])
    for cp in sends: cp.wait_send()


def gather(shards, shard_count):
    D = pltpu.SemaphoreType.DMA
    pair = [D((PH, NZ)), D((PH, NZ))]
    return pl.pallas_call(
        functools.partial(gather_kernel, shard_count),
        out_shape=[jax.ShapeDtypeStruct(s, jnp.bfloat16) for s in (sq_shape(), gu_shape(), dn_shape())],
        in_specs=[pl.BlockSpec(memory_space=pltpu.HBM)] * 11,
        out_specs=[pl.BlockSpec(memory_space=pltpu.VMEM)] * 3,
        scratch_shapes=[D((16,))] + pair * 5 + [D((PH, 16)), D((PH,))],
        compiler_params=pltpu.CompilerParams(collective_id=0, has_side_effects=True, vmem_limit_bytes=50 * 2**20),
        name="gather_weights",
    )(*shards)


BF = jnp.bfloat16
ROWS = (96, 96, 48, 64)
COLS = (SQ, SQ, FFN, SQ)
def gview(bufs, p, q, z, c):
    sq, gu, dn = bufs
    if p < 2: return sq.at[p * 4 + q, z, c]
    if p == 2: return gu.at[q // 2, z, c, q % 2]
    return dn.at[z, c, q]

class Reducer:
    NSTAGE = 7
    def __init__(self, t, g, rc, r1, r2, rz, fin, sems, chunks):
        self.t, self.g = t, g
        self.rc, self.r1, self.r2, self.rz, self.fin = rc, r1, r2, rz, fin
        (self.s_c, self.r_c, self.s_1, self.r_1, self.s_2, self.r_2, self.s_z, self.r_z, self.s_f, self.r_f) = sems
        self.chunks = chunks
        self.sends = []
        q, z, c = t.q, t.z, t.c
        self.sib = t.dev(q, z * 2 + 1 - c)
        self.nb = (t.dev(t.qx, t.s), t.dev(t.qy, t.s))
        self.qn = (t.qx, t.qy)
    def zdev(self, k):
        t = self.t
        return t.dev(t.q, ((t.z + k) % NZ) * 2 + t.c)
    def go(self, src, dst, ss, rs, dev):
        cp = rcopy(src, dst, ss, rs, dev)
        cp.start()
        self.sends.append(cp)
    def wr(self, ref, sem):
        rcopy(ref, ref, sem, sem, self.sib).wait_recv()
    def rows(self, ch):
        p, r0, n = ch
        return pl.ds(r0, n)
    def cols(self, ch, h):
        w = COLS[ch[0]] // 2
        return pl.ds(h * w, w)
    def gp(self, ch, q, z, c, h=None):
        ref = gview(self.g, ch[0], q, z, c).at[self.rows(ch)]
        return ref if h is None else ref.at[:, self.cols(ch, h)]
    def gall(self, ch, c):
        p = ch[0]
        sq, gu, dn = self.g
        if p < 2: return sq.at[pl.ds(p * 4, 4), :, c, self.rows(ch)]
        if p == 2: return gu.at[:, :, c, :, self.rows(ch)]
        return dn.at[:, c, :, self.rows(ch)]
    def gq(self, ch, q, c, h):
        p = ch[0]
        sq, gu, dn = self.g
        if p < 2: return sq.at[p * 4 + q, :, c, self.rows(ch), self.cols(ch, h)]
        if p == 2: return gu.at[q // 2, :, c, q % 2, self.rows(ch), self.cols(ch, h)]
        return dn.at[:, c, q, self.rows(ch), self.cols(ch, h)]
    def rcp(self, ch, q, z):
        p = ch[0]
        b = self.rc[p]
        if p < 2: return b.at[q, z, self.rows(ch)]
        if p == 2: return b.at[q // 2, z, q % 2, self.rows(ch)]
        return b.at[z, q, self.rows(ch)]
    def rcall(self, ch):
        p = ch[0]
        b = self.rc[p]
        if p < 2: return b.at[:, :, self.rows(ch)]
        if p == 2: return b.at[:, :, :, self.rows(ch)]
        return b.at[:, :, self.rows(ch)]
    def stage(self, st, i):
        t, ch = self.t, self.chunks[i]
        q, z, c = t.q, t.z, t.c
        p = ch[0]
        if st == 0:
            self.go(self.gall(ch, 1 - c), self.rcall(ch), self.s_c.at[i], self.r_c.at[i], self.sib)
        elif st == 1:
            self.wr(self.rcall(ch), self.r_c.at[i])
            @pl.loop(0, 4 * NZ)
            def _(j):
                a, b = self.gp(ch, j // NZ, j % NZ, c), self.rcp(ch, j // NZ, j % NZ)
                a[...] = a[...] + b[...]
            for h in range(2):
                for m, qq in enumerate((self.qn[h], t.qd)):
                    slot = (qq // 2) if h == 0 else (qq % 2)
                    self.go(self.gq(ch, qq, c, h), self.r1[p].at[h, slot, :, self.rows(ch)],
                            self.s_1.at[i, h, m], self.r_1.at[i, h, m], self.nb[h])
        elif st == 2:
            for h in range(2):
                for m, qq in ((1, self.qn[1 - h]), (0, q)):
                    slot = (qq // 2) if h == 0 else (qq % 2)
                    land = self.r1[p].at[h, slot, :, self.rows(ch)]
                    self.wr(land, self.r_1.at[i, h, m])
                    @pl.loop(0, NZ)
                    def _(j):
                        a = self.gp(ch, qq, j, c, h)
                        a[...] = a[...] + self.r1[p][h, slot, j, self.rows(ch), :]
                    if m == 1:
                        self.go(self.gq(ch, qq, c, h), self.r2[p].at[h, :, self.rows(ch)],
                                self.s_2.at[i, h], self.r_2.at[i, h], self.nb[1 - h])
        elif st == 3:
            for h in range(2):
                self.wr(self.r2[p].at[h, :, self.rows(ch)], self.r_2.at[i, h])
                @pl.loop(0, NZ)
                def _(j):
                    a = self.gp(ch, q, j, c, h)
                    a[...] = a[...] + self.r2[p][h, j, self.rows(ch), :]
            for k in range(1, NZ):
                self.go(self.gp(ch, q, (z + k) % NZ, c), self.rz[p].at[k, self.rows(ch)],
                        self.s_z.at[i, k], self.r_z.at[i, k], self.zdev(k))
        elif st == 4:
            for k in range(1, NZ):
                self.wr(self.rz[p].at[k, self.rows(ch)], self.r_z.at[i, k])
            v = self.gp(ch, q, z, c)[...].astype(jnp.float32)
            for k in range(1, NZ):
                v = v + self.rz[p][k, self.rows(ch), :].astype(jnp.float32)
            f = self.fin[p].at[q, self.rows(ch)]
            f[...] = v.astype(BF)
            for h in range(2):
                self.go(f, f, self.s_f.at[i, h], self.r_f.at[i, h], self.nb[h])
        elif st == 5:
            for h in range(2):
                f = self.fin[p].at[self.qn[h], self.rows(ch)]
                self.wr(f, self.r_f.at[i, h])
                f = f.at[:, self.cols(ch, h)]
                self.go(f, f, self.s_f.at[i, 2 + h], self.r_f.at[i, 2 + h], self.nb[1 - h])
        elif st == 6:
            for h in range(2):
                f = self.fin[p].at[t.qd, self.rows(ch)].at[:, self.cols(ch, h)]
                self.wr(f, self.r_f.at[i, 2 + h])
    def finish(self):
        for cp in self.sends: cp.wait_send()

def sq_shape(): return (8, NZ, 2, 96, SQ)
def gu_shape(): return (2, NZ, 2, 2, 48, FFN)
def dn_shape(): return (NZ, 2, 4, 64, SQ)
def scratch(nch):
    D = pltpu.SemaphoreType.DMA
    V = lambda s: pltpu.VMEM(s, BF)
    rc = [V((4, NZ, 96, SQ)), V((4, NZ, 96, SQ)), V((2, NZ, 2, 48, FFN)), V((NZ, 4, 64, SQ))]
    r1 = [V((2, 2, NZ, ROWS[p], COLS[p] // 2)) for p in range(4)]
    r2 = [V((2, NZ, ROWS[p], COLS[p] // 2)) for p in range(4)]
    rz = [V((NZ, ROWS[p], COLS[p])) for p in range(4)]
    sems = [D((nch,)), D((nch,)), D((nch, 2, 2)), D((nch, 2, 2)), D((nch, 2)), D((nch, 2)), D((nch, NZ)), D((nch, NZ)), D((nch, 4)), D((nch, 4))]
    return rc, r1, r2, rz, sems
CHUNKS = [(3, 0, 64), (2, 0, 48), (1, 0, 96), (0, 0, 96)]
def reduce_kernel(sharded, chunks, *refs):
    g = refs[0:3]
    fin = refs[3:7]
    rest = refs[7:]
    rc, r1, r2, rz, sems = rest[0:4], rest[4:8], rest[8:12], rest[12:16], rest[16:26]
    t = Team(sharded)
    R = Reducer(t, g, rc, r1, r2, rz, fin, sems, chunks)
    enter([R.sib, R.nb[0], R.nb[1]] + [R.zdev(k) for k in range(1, NZ)])
    n = len(chunks)
    for i in range(n + R.NSTAGE - 1):
        for st in range(R.NSTAGE):
            if 0 <= i - st < n:
                R.stage(st, i - st)
    R.finish()

def reduce(g, shard_count, chunks=CHUNKS):
    rc, r1, r2, rz, sems = scratch(len(chunks))
    V = pl.BlockSpec(memory_space=pltpu.VMEM)
    return pl.pallas_call(
        functools.partial(reduce_kernel, shard_count, chunks),
        out_shape=[jax.ShapeDtypeStruct((4, ROWS[p], COLS[p]), BF) for p in range(4)],
        in_specs=[V] * 3, out_specs=[V] * 4,
        scratch_shapes=rc + r1 + r2 + rz + sems,
        compiler_params=pltpu.CompilerParams(collective_id=1, has_side_effects=True, vmem_limit_bytes=60 * 2**20),
        name="reduce_grads",
    )(*g)


def team_rows(weight, fold):
    if fold == 1:
        return weight
    n = TEAM_S * fold
    groups = [[a * fold + b for b in range(fold)] for a in range(TEAM_S)]
    return lax.all_gather(weight, "shard", axis=0, tiled=True, axis_index_groups=groups)


def team_sum(grad, fold, teams_r):
    if fold > 1:
        groups = [[a * fold + b for b in range(fold)] for a in range(TEAM_S)]
        grad = lax.psum_scatter(grad, "shard", scatter_dimension=0, tiled=True, axis_index_groups=groups)
    if teams_r > 1:
        groups = [[a * TEAM_R + b for a in range(teams_r)] for b in range(TEAM_R)]
        grad = lax.psum(grad, "replica", axis_index_groups=groups)
    return grad


def body(
    replicas, shards,
    hidden, encoded, out_grad, seg_start, seg_parent, bucket_of_distance,
    norm_self, self_query, self_key, self_value, self_out, rel_bias,
    norm_cross, cross_query, cross_key, cross_value, cross_out,
    norm_ff, ff_gate, ff_up, ff_down,
):
    bounds = bucket_bounds(bucket_of_distance)
    fold, teams_r = shards // TEAM_S, replicas // TEAM_R
    big = (self_query, self_key, self_value, self_out, cross_query, cross_key, cross_value, cross_out, ff_gate, ff_up, ff_down)
    sq, gu, dn = gather([team_rows(w, fold) for w in big], shards)
    sq, gu, dn = sq.reshape(8, SQ, SQ), gu.reshape(2, SQ, FFN), dn.reshape(FFN, SQ)
    small = jnp.concatenate([norm_self, norm_cross, norm_ff, rel_bias.reshape(-1)])
    small = lax.all_gather(small, "shard", axis=0)
    rows, brows = norm_self.shape[0], rel_bias.shape[0]
    gains = [small[:, i * rows:(i + 1) * rows].reshape(-1) for i in range(3)]
    bias = small[:, 3 * rows:].reshape(NB, H)
    weights = (gains[0], sq[0], sq[1], sq[2], sq[3], bias, gains[1], sq[4], sq[5], sq[6], sq[7], gains[2], gu[0], gu[1], dn)

    def one_tree(running, item):
        layer_out, saved = tree_forward(weights, item[0], item[1], item[3], item[4], bounds)
        grad_inputs, grad_encoder, grads = tree_backward(weights, item[0], item[1], item[2], saved)
        return (jax.tree.map(jnp.add, running, grads), (layer_out, grad_inputs, grad_encoder))

    flat = lambda v: v.reshape((-1,) + v.shape[2:])
    zeros = tuple(jnp.zeros(w.shape, jnp.float32) for w in weights)
    grads, outs = lax.scan(one_tree, zeros, tuple(map(flat, (hidden, encoded, out_grad, seg_start, seg_parent))))
    layer_out, grad_hidden, grad_encoded = (v.reshape(hidden.shape) for v in outs)
    (g_ns, g_q, g_k, g_v, g_o, g_rb, g_nc, g_cq, g_ck, g_cv, g_co, g_nf, g_g, g_u, g_d) = grads
    gsq = jnp.stack([w.astype(BF) for w in (g_q, g_k, g_v, g_o, g_cq, g_ck, g_cv, g_co)]).reshape(sq_shape())
    ggu = jnp.stack([g_g.astype(BF), g_u.astype(BF)]).reshape(gu_shape())
    fin = reduce((gsq, ggu, g_d.astype(BF).reshape(dn_shape())), shards)
    f0, f1 = fin[0], fin[1]
    f2 = fin[2].reshape(2, 96, FFN)
    f3 = fin[3].reshape(256, SQ)
    parts = [f0[0], f0[1], f0[2], f0[3], f1[0], f1[1], f1[2], f1[3], f2[0], f2[1], f3]
    (o_q, o_k, o_v, o_o, o_cq, o_ck, o_cv, o_co, o_g, o_u, o_d) = [team_sum(v.astype(jnp.float32), fold, teams_r) for v in parts]
    gsmall = lax.psum(jnp.concatenate([g_ns, g_nc, g_nf, g_rb.reshape(-1)]), ("replica", "shard"))
    s = lax.axis_index("shard")
    o_ns, o_nc, o_nf = (lax.dynamic_slice(gsmall, (i * D + s * rows,), (rows,)) for i in range(3))
    o_rb = lax.dynamic_slice(gsmall[3 * D:].reshape(NB, H), (s * brows, 0), (brows, H))
    return (layer_out, grad_hidden, grad_encoded, o_ns, o_q, o_k, o_v, o_o, o_rb, o_nc, o_cq, o_ck, o_cv, o_co, o_nf, o_g, o_u, o_d)


def solution(mesh):
    placed = (
        P(None, ("replica", "shard"), None, None),
        P(None, ("replica", "shard"), None, None),
        P(None, ("replica", "shard"), None, None),
        P(None, ("replica", "shard"), None),
        P(None, ("replica", "shard"), None),
        P(),
        P("shard"),
        P("shard", None),
        P("shard", None),
        P("shard", None),
        P("shard", None),
        P("shard", None),
        P("shard"),
        P("shard", None),
        P("shard", None),
        P("shard", None),
        P("shard", None),
        P("shard"),
        P("shard", None),
        P("shard", None),
        P("shard", None),
    )
    return jax.shard_map(
        functools.partial(body, mesh.shape["replica"], mesh.shape["shard"]),
        mesh=mesh,
        in_specs=placed,
        out_specs=(
            P(None, ("replica", "shard"), None, None),
            P(None, ("replica", "shard"), None, None),
            P(None, ("replica", "shard"), None, None),
            P("shard"),
            P("shard", None),
            P("shard", None),
            P("shard", None),
            P("shard", None),
            P("shard", None),
            P("shard"),
            P("shard", None),
            P("shard", None),
            P("shard", None),
            P("shard", None),
            P("shard"),
            P("shard", None),
            P("shard", None),
            P("shard", None),
        ),
        check_vma=False,
    )
```

```python
import functools
import math

import jax
import jax.numpy as jnp
from jax import lax
from jax.experimental import pallas as pl
from jax.experimental.pallas import tpu as pltpu
from jax.sharding import PartitionSpec as P

SQ, FFN, H, DH, TREE, NSEG, NB = 768, 2048, 12, 64, 256, 13, 32
TRUNK, BRANCH, LEAF = 64, 16, 16
BF, F32 = jnp.bfloat16, jnp.float32
EPSILON, NEGATIVE = 1e-6, -1e9
DEPTHS = 128
SEG_LEN = (TRUNK,) + (BRANCH,) * 4 + (LEAF,) * 8
SEG_DEPTH = (0,) + (TRUNK,) * 4 + (TRUNK + BRANCH,) * 8

def nn(a, b): return lax.dot_general(a, b, (((1,), (0,)), ((), ())), preferred_element_type=F32)
def nt(a, b): return lax.dot_general(a, b, (((1,), (1,)), ((), ())), preferred_element_type=F32)
def tn(a, b): return lax.dot_general(a, b, (((0,), (0,)), ((), ())), preferred_element_type=F32)

class Layer:
    def __init__(self, refs, trees):
        self.__dict__.update(refs)
        self.trees = trees
        self.tokens = trees * TREE

    def layout(self):
        for t in range(self.trees):
            def place(shape, axis):
                pos = lax.broadcasted_iota(jnp.int32, shape, axis)
                dep, sid, pid, gid = pos, jnp.zeros_like(pos), jnp.zeros_like(pos), jnp.zeros_like(pos)
                for s in range(NSEG):
                    at = self.seg_start[t, s]
                    inside = (pos >= at) & (pos < at + SEG_LEN[s])
                    dep = dep + jnp.where(inside, SEG_DEPTH[s] - at, 0)
                    sid = jnp.where(inside, s, sid)
                    pid = jnp.where(inside, self.seg_parent[t, s], pid)
                    gid = jnp.where(inside, self.seg_parent[t, self.seg_parent[t, s]], gid)
                return dep, sid, pid, gid
            dep_j, sid_j, _, _ = place((TREE, 1), 0)
            dep_i, sid_i, pid_i, gid_i = place((1, TREE), 1)
            ok = ((sid_j == sid_i) | (sid_j == pid_i) | (sid_j == gid_i)) & (dep_j <= dep_i)
            self.mask[t] = jnp.where(ok, 0.0, NEGATIVE).astype(F32)
            lanes = lax.broadcasted_iota(jnp.int32, (TREE, DEPTHS), 1)
            self.hot[t] = jnp.where(lanes == dep_j, 1.0, 0.0).astype(BF)
            rows = lax.broadcasted_iota(jnp.int32, (DEPTHS, TREE), 0)
            self.hot_t[t] = jnp.where(rows == DEPTHS - 1 - dep_i, 1.0, 0.0).astype(BF)

    def bucket_hot(self):
        row = lax.broadcasted_iota(jnp.int32, (128, DEPTHS), 0)
        inner = row % 16
        bucket = jnp.where((inner >= 4) & (inner < 8), 4 * (row // 16) + inner - 4, -1)
        return jnp.where(self.bucket[...][:1] == bucket, 1.0, 0.0).astype(BF)

    def spread(self, s):
        i = lax.broadcasted_iota(jnp.int32, (128, SQ), 0)
        j = lax.broadcasted_iota(jnp.int32, (128, SQ), 1)
        return jnp.where((j == i + 96 * s) & (i < 96), 1.0, 0.0).astype(BF)

    def small_params(self):
        total = jnp.zeros((16, SQ), F32)
        for s in range(8):
            total = total + nn(self.small[s], self.spread(s))
        self.gains[...] = total
        table = tn(self.small[...].reshape(128, 128), self.bucket_hot())
        for h in range(H):
            row = jnp.broadcast_to(table[h:h + 1], (DEPTHS, DEPTHS))
            self.toep[h] = pltpu.roll(row, 0, 1, stride=1, stride_axis=0).astype(BF)
        self.gain_grads[...] = jnp.zeros_like(self.gain_grads)
        self.bias_grads[...] = jnp.zeros_like(self.bias_grads)

    def small_grads(self):
        hot = self.bucket_hot()
        sums = self.bias_grads[...]
        high = sums.astype(BF)
        low = (sums - high.astype(F32)).astype(BF)
        out = nt(hot, high) + nt(hot, low)
        gains = self.gain_grads[...].astype(BF)
        for s in range(8):
            self.small_out[s] = (out[16 * s:16 * s + 16] + nt(gains, self.spread(s))).astype(BF)

    def norm(self, src, dst, gain):
        g = self.gains[gain:gain + 1, :]
        @pl.loop(0, self.tokens // 64, unroll=4)
        def _(b):
            rows = pl.ds(b * 64, 64)
            v = src[rows, :].astype(F32)
            r = lax.rsqrt(jnp.mean(v * v, axis=-1, keepdims=True) + EPSILON)
            dst[rows, :] = (v * r * g).astype(BF)

    def norm_back(self, src, gain, store):
        g = self.gains[gain:gain + 1, :]
        @pl.loop(0, self.tokens // 64, unroll=4)
        def _(b):
            rows = pl.ds(b * 64, 64)
            v = src[rows, :].astype(F32)
            r = lax.rsqrt(jnp.mean(v * v, axis=-1, keepdims=True) + EPSILON)
            n = v * r
            dh = self.gn[rows, :]
            dg = dh * g
            self.gain_grads[gain:gain + 1, :] += jnp.sum(dh * n, axis=0, keepdims=True)
            store(rows, r * (dg - n * jnp.mean(dg * n, axis=-1, keepdims=True)))

    def wsq(self, w): return self.sq[w].reshape(SQ, SQ)
    def project(self, src, w, dst):
        @pl.loop(0, 3, unroll=3)
        def _(n):
            cols = pl.ds(pl.multiple_of(n * 256, 256), 256)
            wt = self.sq[w, :, :, :, cols].reshape(SQ, 256)
            for t in range(self.trees):
                rows = pl.ds(t * TREE, TREE)
                dst[rows, cols] = nn(src[rows, :], wt).astype(BF)
    def project_add(self, src, w, base, dst):
        @pl.loop(0, 3, unroll=3)
        def _(n):
            cols = pl.ds(pl.multiple_of(n * 256, 256), 256)
            wt = self.sq[w, :, :, :, cols].reshape(SQ, 256)
            for t in range(self.trees):
                rows = pl.ds(t * TREE, TREE)
                dst[rows, cols] = base[rows, cols].astype(F32) + nn(src[rows, :], wt)
    def back(self, pairs, dst, dtype):
        @pl.loop(0, 2, unroll=2)
        def _(n):
            cols = pl.ds(pl.multiple_of(n * 384, 384), 384)
            for t in range(self.trees):
                rows = pl.ds(t * TREE, TREE)
                total = None
                for src, w in pairs:
                    part = nt(src[rows, :], self.sq[w, pl.ds(n * 2, 2)].reshape(384, SQ))
                    total = part if total is None else total + part
                dst[rows, cols] = total.astype(dtype)
    def weight_grad(self, left, right, w):
        @pl.loop(0, 2, unroll=2)
        def _(n):
            cols = pl.ds(pl.multiple_of(n * 384, 384), 384)
            lt = left[:, cols]
            for m in range(3):
                part = tn(lt, right[:, m * 256:(m + 1) * 256])
                self.sq[w, pl.ds(n * 2, 2), :, :, m * 256:(m + 1) * 256] = part.astype(BF).reshape(2, 2, 96, 256)

    def lanes(self):
        low = lax.broadcasted_iota(jnp.int32, (TREE, 128), 1) < DH
        return low, jnp.logical_not(low)
    def attend(self, q, k, v, ctx, probs, masked, first, last):
        halves = self.lanes()
        @pl.loop(first * self.trees // 2, last * self.trees // 2, unroll=3)
        def _(i):
            t, p = i // (H // 2), i % (H // 2)
            rows = pl.ds(pl.multiple_of(t * TREE, TREE), TREE)
            cols = pl.ds(pl.multiple_of(p * 128, 128), 128)
            qp, kp, vt = q[rows, cols], k[rows, cols], v[rows, cols].T
            if masked:
                hot = self.hot[t]
                kp = jnp.concatenate([kp, hot], axis=1)
            outs = []
            for e in range(2):
                qe = jnp.where(halves[e], qp, jnp.zeros_like(qp))
                if masked:
                    qe = jnp.concatenate([qe, nt(hot, self.toep[2 * p + e]).astype(BF)], axis=1)
                s = nt(kp, qe)
                if masked:
                    s = s + self.mask[t]
                x = jnp.exp(s - jnp.max(s, axis=0, keepdims=True))
                pr = (x * (1.0 / jnp.sum(x, axis=0, keepdims=True))).astype(BF)
                probs[2 * i + e] = pr
                outs.append(nn(vt[e * DH:(e + 1) * DH], pr))
            ctx[rows, cols] = jnp.concatenate(outs, axis=0).astype(BF).T
    def attend_back(self, q, k, v, dctx, probs, masked, first, last):
        halves = self.lanes()
        @pl.loop(first * self.trees // 2, last * self.trees // 2, unroll=3)
        def _(i):
            t, p = i // (H // 2), i % (H // 2)
            rows = pl.ds(pl.multiple_of(t * TREE, TREE), TREE)
            cols = pl.ds(pl.multiple_of(p * 128, 128), 128)
            qp, kt, vp, dp = q[rows, cols], k[rows, cols].T, v[rows, cols], dctx[rows, cols]
            dq, dk, dv = [], [], []
            for e in range(2):
                pr = probs[2 * i + e]
                prf = pr.astype(F32)
                g = nt(vp, jnp.where(halves[e], dp, jnp.zeros_like(dp)))
                ds = (prf * (g - jnp.sum(g * prf, axis=0, keepdims=True))).astype(BF)
                dv.append(nn(pr, dp))
                dq.append(nn(kt[e * DH:(e + 1) * DH], ds))
                dk.append(nn(ds, qp))
                if masked:
                    m = nn(nn(self.hot_t[t], ds).astype(BF), self.hot[t])
                    m = pltpu.roll(m, 1, 1, stride=1, stride_axis=0)
                    self.bias_grads[pl.ds(2 * p + e, 1), :] += jnp.sum(m, axis=0, keepdims=True)
            q[rows, cols] = jnp.concatenate(dq, axis=0).astype(BF).T
            k[rows, cols] = jnp.where(halves[0], dk[0], dk[1]).astype(BF)
            v[rows, cols] = jnp.where(halves[0], dv[0], dv[1]).astype(BF)

    def feed_forward(self, m):
        base = pl.multiple_of(m * 512, 512)
        for hf in range(2):
            cols = pl.ds(pl.multiple_of(base + hf * 256, 256), 256)
            wg = self.gu[0, :, :, :, :, cols].reshape(SQ, 256)
            wu = self.gu[1, :, :, :, :, cols].reshape(SQ, 256)
            wd = self.dn[m, hf].reshape(256, SQ)
            here = slice(hf * 256, hf * 256 + 256)
            @pl.loop(0, self.trees, unroll=2)
            def _(t):
                rows = pl.ds(pl.multiple_of(t * TREE, TREE), TREE)
                x = self.nf[rows, :]
                g, u, gi = nn(x, wg), nn(x, wu), nt(self.dy[rows, :], wd)
                c = math.sqrt(2.0 / math.pi)
                th = jnp.tanh(c * (g + 0.044715 * (g * g * g)))
                half = 0.5 * (1.0 + th)
                gelu = g * half
                slope = half + 0.5 * g * (1.0 - th * th) * c * (1.0 + 3 * 0.044715 * (g * g))
                self.inner[rows, here] = (gelu * u).astype(BF)
                self.ggate[rows, here] = (gi * u * slope).astype(BF)
                self.gup[rows, here] = (gi * gelu).astype(BF)
        @pl.loop(0, 3, unroll=3)
        def _(n):
            cols = pl.ds(pl.multiple_of(n * 256, 256), 256)
            wd = self.dn[m, :, :, :, cols].reshape(512, 256)
            for t in range(self.trees):
                rows = pl.ds(t * TREE, TREE)
                self.oacc[rows, cols] += nn(self.inner[rows, :], wd)
        @pl.loop(0, 2, unroll=2)
        def _(n):
            cols = pl.ds(pl.multiple_of(n * 384, 384), 384)
            hid = pl.ds(base, 512)
            wg = self.gu[0, pl.ds(n * 2, 2), :, :, :, hid].reshape(384, 512)
            wu = self.gu[1, pl.ds(n * 2, 2), :, :, :, hid].reshape(384, 512)
            for t in range(self.trees):
                rows = pl.ds(t * TREE, TREE)
                self.gn[rows, cols] += nt(self.ggate[rows, :], wg) + nt(self.gup[rows, :], wu)
        @pl.loop(0, 2, unroll=2)
        def _(n):
            hid = pl.ds(base, 512)
            cols = pl.ds(pl.multiple_of(n * 384, 384), 384)
            lt = self.nf[:, cols]
            self.gu[0, pl.ds(n * 2, 2), :, :, :, hid] = tn(lt, self.ggate[...]).astype(BF).reshape(2, 2, 2, 48, 512)
            self.gu[1, pl.ds(n * 2, 2), :, :, :, hid] = tn(lt, self.gup[...]).astype(BF).reshape(2, 2, 2, 48, 512)
        @pl.loop(0, 3, unroll=3)
        def _(n):
            cols = pl.ds(pl.multiple_of(n * 256, 256), 256)
            self.dn[m, :, :, :, cols] = tn(self.inner[...], self.dy[:, cols]).astype(BF).reshape(2, 4, 64, 256)

    def start_ff(self):
        self.norm(self.after_cross, self.nf, 2)
        self.oacc[...] = self.after_cross[...]
        self.gn[...] = jnp.zeros_like(self.gn)
    def end_ff(self):
        self.stage[...] = self.oacc[...].astype(BF)
    def back_ff_norm(self):
        def store(rows, dv):
            total = self.dy[rows, :].astype(F32) + dv
            self.oacc[rows, :] = total
            self.gb[rows, :] = total.astype(BF)
        self.norm_back(self.after_cross, 2, store)
    def back_cross_a(self):
        self.weight_grad_after(self.cctx, self.gb, 7, self.cctx)
    def weight_grad_after(self, ctx, grad, w, dst):
        self.back([(grad, w)], self.stage, BF)
        self.weight_grad(ctx, grad, w)
        dst[...] = self.stage[...]
    def back_cross_norm(self):
        def store(rows, dv):
            total = self.oacc[rows, :] + dv
            self.oacc[rows, :] = total
            self.gb[rows, :] = total.astype(BF)
        self.norm_back(self.after_self, 1, store)
    def back_self_a(self):
        self.weight_grad_after(self.ctx, self.gb, 3, self.ctx)
    def back_self_norm(self):
        def store(rows, dv):
            self.gb[rows, :] = (self.oacc[rows, :] + dv).astype(BF)
        self.norm_back(self.hid, 0, store)

def layer_scratch(trees):
    T = trees * TREE
    V = pltpu.VMEM
    b = lambda: V((T, SQ), BF)
    f = lambda: V((T, SQ), F32)
    d = {k: b() for k in ("ns", "q", "k", "v", "ctx", "nc", "cq", "ck", "cv", "cctx", "nf", "gb", "stage")}
    d.update({k: f() for k in ("after_self", "after_cross", "oacc", "gn")})
    d.update(ps=V((trees * H, TREE, TREE), BF), pc=V((trees * H, TREE, TREE), BF),
             mask=V((trees, TREE, TREE), F32), hot=V((trees, TREE, DEPTHS), BF), hot_t=V((trees, DEPTHS, TREE), BF),
             toep=V((H, DEPTHS, DEPTHS), BF), gains=V((16, SQ), F32), gain_grads=V((16, SQ), F32),
             bias_grads=V((128, 128), F32), inner=V((T, 512), BF), ggate=V((T, 512), BF), gup=V((T, 512), BF))
    return d


MESH = pl.DeviceIdType.MESH
TEAM_R, TEAM_S = 4, 8
NZ = TEAM_S // 2


class Team:
    def __init__(self, shard_count):
        self.fold = shard_count // TEAM_S
        r = lax.axis_index("replica")
        s = lax.axis_index("shard")
        self.base_r = (r // TEAM_R) * TEAM_R
        self.q = r % TEAM_R
        self.off_s = s % self.fold
        self.s = s // self.fold
        self.z = self.s // 2
        self.c = self.s % 2
        self.qx = self.q + 1 - 2 * (self.q % 2)
        self.qy = self.q + 2 - 4 * (self.q // 2)
        self.qd = 3 - self.q
        self.sib = self.dev(self.q, self.z * 2 + 1 - self.c)
        self.nb = (self.dev(self.qx, self.s), self.dev(self.qy, self.s))
        self.diag = self.dev(self.qd, self.s)
        self.qn = (self.qx, self.qy)

    def dev(self, q, s):
        return (self.base_r + q, s * self.fold + self.off_s)

    def zdev(self, k):
        return self.dev(self.q, ((self.z + k) % NZ) * 2 + self.c)

    def zsrc(self, k):
        return (self.z + NZ - k) % NZ


def rcopy(src, dst, send_sem, recv_sem, device):
    return pltpu.make_async_remote_copy(
        src_ref=src, dst_ref=dst, send_sem=send_sem, recv_sem=recv_sem, device_id=device, device_id_type=MESH
    )


class Sender:
    def __init__(self, team):
        self.t = team
        self.sends = {}

    def go(self, src, dst, send_sem, recv_sem, device, key=0):
        cp = rcopy(src, dst, send_sem, recv_sem, device)
        cp.start()
        self.sends.setdefault(key, []).append(cp)

    def got(self, ref, sem):
        rcopy(ref, ref, sem, sem, self.t.sib).wait_recv()

    def sent(self, key=0):
        for cp in self.sends.pop(key, ()):
            cp.wait_send()


PHASES = (("sq", 0, SQ), ("sq", 4, SQ), ("gu", 0, 1024), ("dn", 0, SQ), ("gu", 1024, 1024))


class Gather(Sender):
    def __init__(self, team, bufs, sems):
        super().__init__(team)
        self.sq, self.gu, self.dn = bufs
        (self.zs, self.zr, self.xs, self.xr, self.ys, self.yr, self.dxs, self.dxr, self.dys, self.dyr, self.cs, self.cr) = sems

    def piece(self, p, q, z, half=None):
        kind, first, n = PHASES[p]
        c = self.t.c
        lo = 0 if half is None else half * (n // 2)
        w = n if half is None else n // 2
        if kind == "sq":
            ref = self.sq.at[first + q, z, c]
        elif kind == "gu":
            ref, lo = self.gu.at[q // 2, z, c, q % 2], lo + first
        else:
            ref = self.dn.at[z, c, q]
        return ref.at[:, pl.ds(lo, w)]

    def all_of(self, p, z, c):
        kind, first, n = PHASES[p]
        if kind == "sq":
            return self.sq.at[pl.ds(first, 4), z, c]
        if kind == "gu":
            return self.gu.at[:, z, c, :, :, pl.ds(first, n)]
        return self.dn.at[z, c]

    def begin(self, p):
        t = self.t
        ref = self.piece(p, t.q, t.z)
        for k in range(1, NZ):
            self.go(ref, ref, self.zs.at[p, k], self.zr.at[p, k], t.zdev(k), p)
        own = self.all_of(p, t.z, t.c)
        self.go(own, own, self.cs.at[p, 0], self.cr.at[p], t.sib, p)

    def zstep(self, p, k):
        t = self.t
        ref = self.piece(p, t.q, t.zsrc(k))
        self.got(ref, self.zr.at[p, k])
        self.go(ref, ref, self.xs.at[p, k], self.xr.at[p, k], t.nb[0], p)
        self.go(ref, ref, self.ys.at[p, k], self.yr.at[p, k], t.nb[1], p)
        self.go(ref, ref, self.cs.at[p, 5 * k - 4], self.cr.at[p], t.sib, p)

    def xystep(self, p, k):
        t = self.t
        z = t.zsrc(k)
        ref = self.piece(p, t.qx, z)
        self.got(ref, self.xr.at[p, k])
        h = self.piece(p, t.qx, z, 0)
        self.go(h, h, self.dys.at[p, k], self.dyr.at[p, k], t.nb[1], p)
        self.go(ref, ref, self.cs.at[p, 5 * k - 3], self.cr.at[p], t.sib, p)
        ref = self.piece(p, t.qy, z)
        self.got(ref, self.yr.at[p, k])
        h = self.piece(p, t.qy, z, 1)
        self.go(h, h, self.dxs.at[p, k], self.dxr.at[p, k], t.nb[0], p)
        self.go(ref, ref, self.cs.at[p, 5 * k - 2], self.cr.at[p], t.sib, p)

    def dstep(self, p, k):
        t = self.t
        z = t.zsrc(k)
        for half, sem, i in ((0, self.dyr, 1), (1, self.dxr, 0)):
            h = self.piece(p, t.qd, z, half)
            self.got(h, sem.at[p, k])
            self.go(h, h, self.cs.at[p, 5 * k - i], self.cr.at[p], t.sib, p)

    def tick(self, i):
        steps = [(p, k) for p in range(len(PHASES)) for k in range(1, NZ)]
        n = len(steps)
        if i < n:
            p, k = steps[i]
            if k == 1 and p + 2 < len(PHASES):
                self.begin(p + 2)
            self.zstep(p, k)
        if 1 <= i < n + 1:
            self.xystep(*steps[i - 1])
        if 2 <= i < n + 2:
            self.dstep(*steps[i - 2])

    def whole(self, p):
        self.got(self.all_of(p, slice(None), 1 - self.t.c), self.cr.at[p])


CHUNKS = (
    ("gu", 0, 0, 48, 0, 512),
    ("gu", 0, 0, 48, 512, 512),
    ("gu", 0, 0, 48, 1024, 512),
    ("gu", 0, 0, 48, 1536, 512),
    ("dn", 0, 0, 64, 0, SQ),
    ("sq", 4, 0, 48, 0, SQ),
    ("sq", 4, 48, 48, 0, SQ),
    ("sq", 0, 0, 48, 0, SQ),
    ("sq", 0, 48, 48, 0, SQ),
)
ENTRY = (0, 1, 2, 3, 4, 6, 7, 9, 10)
KINDS = {"sq": 0, "gu": 1, "dn": 2}
ROWS = (96, 48, 64)
LAND = (SQ, 1024, SQ)
STAGES = 7


class Reduce(Sender):
    def __init__(self, team, bufs, rc, r1, r2, rz, fin, sems):
        super().__init__(team)
        self.sq, self.gu, self.dn = bufs
        self.rc, self.r1, self.r2, self.rz, self.fin = rc, r1, r2, rz, fin
        (self.s_c, self.r_c, self.s_1, self.r_1, self.s_2, self.r_2, self.s_z, self.r_z, self.s_f, self.r_f) = sems

    def rows(self, ch):
        return pl.ds(ch[2], ch[3])

    def cols(self, ch, h=None):
        if h is None:
            return pl.ds(ch[4], ch[5])
        return pl.ds(ch[4] + h * (ch[5] // 2), ch[5] // 2)

    def land(self, ch):
        return pl.ds((ch[4] % LAND[KINDS[ch[0]]]) // 2, ch[5] // 2)

    def spot(self, ch):
        return pl.ds(ch[4] % LAND[KINDS[ch[0]]], ch[5])

    def view(self, ch, q, z, c, h=None):
        kind, w = ch[0], ch[1]
        rows, cols = self.rows(ch), self.cols(ch, h)
        if kind == "sq":
            return self.sq.at[w + q, z, c, rows, cols]
        if kind == "gu":
            return self.gu.at[q // 2, z, c, q % 2, rows, cols]
        return self.dn.at[z, c, q, rows, cols]

    def half(self, ch, c):
        kind, w = ch[0], ch[1]
        rows, cols = self.rows(ch), self.cols(ch)
        if kind == "sq":
            return self.sq.at[pl.ds(w, 4), :, c, rows, cols]
        if kind == "gu":
            return self.gu.at[:, :, c, :, rows, cols]
        return self.dn.at[:, c, :, rows, cols]

    def from_core(self, ch, q=None, z=None):
        b = self.rc[KINDS[ch[0]]]
        rows, cols = self.rows(ch), self.spot(ch)
        if ch[0] == "sq":
            return b.at[:, :, rows, cols] if q is None else b.at[q, z, rows, cols]
        if ch[0] == "gu":
            return b.at[:, :, :, rows, cols] if q is None else b.at[q // 2, z, q % 2, rows, cols]
        return b.at[:, :, rows, cols] if q is None else b.at[z, q, rows, cols]

    def final(self, ch):
        return self.fin[0 if ch[1] == 0 else 1] if ch[0] == "sq" else self.fin[1 + KINDS[ch[0]]]

    def stage(self, st, i):
        t, ch = self.t, CHUNKS[i]
        q, z, c = t.q, t.z, t.c
        kd = KINDS[ch[0]]
        rows, land = self.rows(ch), self.land(ch)
        if st == 0:
            self.go(self.half(ch, 1 - c), self.from_core(ch), self.s_c.at[i], self.r_c.at[i], t.sib)
        elif st == 1:
            self.got(self.from_core(ch), self.r_c.at[i])

            @pl.loop(0, 4 * NZ)
            def _(j):
                a, b = self.view(ch, j // NZ, j % NZ, c), self.from_core(ch, j // NZ, j % NZ)
                a[...] = a[...] + b[...]

            for h in range(2):
                for m, qq in enumerate((t.qn[h], t.qd)):
                    slot = (qq // 2) if h == 0 else (qq % 2)
                    self.go(
                        self.view(ch, qq, slice(None), c, h), self.r1[kd].at[h, slot, :, rows, land],
                        self.s_1.at[i, h, m], self.r_1.at[i, h, m], t.nb[h],
                    )
        elif st == 2:
            for h in range(2):
                for m, qq in ((1, t.qn[1 - h]), (0, q)):
                    slot = (qq // 2) if h == 0 else (qq % 2)
                    self.got(self.r1[kd].at[h, slot, :, rows, land], self.r_1.at[i, h, m])

                    @pl.loop(0, NZ)
                    def _(j):
                        a = self.view(ch, qq, j, c, h)
                        a[...] = a[...] + self.r1[kd][h, slot, j, rows, land]

                    if m == 1:
                        self.go(
                            self.view(ch, qq, slice(None), c, h), self.r2[kd].at[h, :, rows, land],
                            self.s_2.at[i, h], self.r_2.at[i, h], t.nb[1 - h],
                        )
        elif st == 3:
            for h in range(2):
                self.got(self.r2[kd].at[h, :, rows, land], self.r_2.at[i, h])

                @pl.loop(0, NZ)
                def _(j):
                    a = self.view(ch, q, j, c, h)
                    a[...] = a[...] + self.r2[kd][h, j, rows, land]

            for k in range(1, NZ):
                self.go(
                    self.view(ch, q, (z + k) % NZ, c), self.rz[kd].at[k - 1, rows, self.spot(ch)],
                    self.s_z.at[i, k], self.r_z.at[i, k], t.zdev(k),
                )
        elif st == 4:
            v = self.view(ch, q, z, c)[...].astype(F32)
            for k in range(1, NZ):
                self.got(self.rz[kd].at[k - 1, rows, self.spot(ch)], self.r_z.at[i, k])
                v = v + self.rz[kd][k - 1, rows, self.spot(ch)].astype(F32)
            f = self.final(ch).at[q, rows, self.cols(ch)]
            f[...] = v.astype(BF)
            for h in range(2):
                self.go(f, f, self.s_f.at[i, h], self.r_f.at[i, h], t.nb[h])
        elif st == 5:
            for h in range(2):
                self.got(self.final(ch).at[t.qn[h], rows, self.cols(ch)], self.r_f.at[i, h])
                f = self.final(ch).at[t.qn[h], rows, self.cols(ch, h)]
                self.go(f, f, self.s_f.at[i, 2 + h], self.r_f.at[i, 2 + h], t.nb[1 - h])
        else:
            for h in range(2):
                self.got(self.final(ch).at[t.qd, rows, self.cols(ch, h)], self.r_f.at[i, 2 + h])

    def tick(self, n):
        for st in reversed(range(STAGES)):
            for i, entry in enumerate(ENTRY):
                if n - entry == st:
                    self.stage(st, i)


def layer_kernel(names, shards, trees, *refs):
    seg_start, seg_parent, bucket, *gains_in, bias_in, hid_in, enc_in, dy_in = refs[:10]
    weights = refs[10:21]
    lo, gh, ge, f0, f1, f2, f3, small_fin = refs[21:29]
    r = dict(zip(names, refs[29:]))
    bufs = (r["sq"], r["gu"], r["dn"])
    t = Team(shards)
    L = Layer(dict(r, seg_start=seg_start, seg_parent=seg_parent, bucket=bucket), trees)
    G = Gather(t, bufs, [r["g%d" % i] for i in range(12)])
    R = Reduce(
        t, bufs, [r["rc0"], r["rc1"], r["rc2"]], [r["ra0"], r["ra1"], r["ra2"]], [r["rb0"], r["rb1"], r["rb2"]],
        [r["rz0"], r["rz1"], r["rz2"]], (f0, f1, f2, f3), [r["r%d" % i] for i in range(10)],
    )
    S = Sender(t)

    loc, lsem = [], r["local"]

    def fetch(src, dst):
        cp = pltpu.make_async_copy(src, dst, lsem.at[len(loc)])
        cp.start()
        loc.append(cp)

    z, c = t.z, t.c
    for i in range(8):
        fetch(weights[i], r["sq"].at[i, z, c])
    for i in range(2):
        for h in range(2):
            fetch(weights[8 + i].at[pl.ds(h * 48, 48)], r["gu"].at[i, z, c, h])
    for h in range(4):
        fetch(weights[10].at[pl.ds(h * 64, 64)], r["dn"].at[z, c, h])
    fetch(hid_in, r["hid"])
    fetch(enc_in, r["enc"])
    fetch(dy_in, r["dy"])

    others = [t.dev(t.q, (t.s + k) % TEAM_S) for k in range(1, TEAM_S)]
    greet = others + list(t.nb) + [t.diag]
    barrier = pltpu.get_barrier_semaphore()
    for d in greet:
        pl.semaphore_signal(barrier, inc=1, device_id=d, device_id_type=MESH)
    pl.semaphore_wait(barrier, len(greet))
    for cp in loc:
        cp.wait()

    small, mix = r["small"], r["mix"]
    mix[...] = jnp.zeros_like(mix)
    for i in range(3):
        mix[i:i + 1, :96] = gains_in[i][...].astype(F32)
    mix[4:8, :H] = bias_in[...].astype(F32)
    small[t.s] = mix[...].astype(BF)
    for k in range(1, TEAM_S):
        S.go(small.at[t.s], small.at[t.s], r["ss"].at[0, k], r["sr"].at[0, k], others[k - 1])
    G.begin(0)
    G.begin(1)
    L.layout()
    G.tick(0)
    for k in range(1, TEAM_S):
        S.got(small.at[(t.s + TEAM_S - k) % TEAM_S], r["sr"].at[0, k])
    L.small_params()
    G.tick(1)
    L.norm(r["hid"], r["ns"], 0)
    for i in range(2, 6):
        G.tick(i)
    own = (r["q"], r["k"], r["v"], r["ctx"], r["ps"], True)
    cross = (r["cq"], r["ck"], r["cv"], r["cctx"], r["pc"], False)
    G.whole(0)
    for w in range(3):
        L.project(r["ns"], w, own[w])
    for n in range(4):
        G.tick(6 + n)
        L.attend(*own, 3 * n, 3 * n + 3)
    G.tick(10)
    L.project_add(r["ctx"], 3, r["hid"], r["after_self"])
    L.norm(r["after_self"], r["nc"], 1)
    G.whole(1)
    L.project(r["nc"], 4, r["cq"])
    G.tick(11)
    L.project(r["enc"], 5, r["ck"])
    L.project(r["enc"], 6, r["cv"])
    L.attend(*cross, 0, 3)
    G.tick(12)
    L.attend(*cross, 3, 9)
    G.tick(13)
    L.attend(*cross, 9, 12)
    L.project_add(r["cctx"], 7, r["after_self"], r["after_cross"])
    G.tick(14)
    L.start_ff()
    G.tick(15)
    for p in (2, 3):
        G.whole(p)
        G.sent(p)

    L.feed_forward(0)
    G.tick(16)
    R.tick(0)
    L.feed_forward(1)
    R.tick(1)
    G.whole(4)
    for p in (4, 0, 1):
        G.sent(p)
    S.sent()
    for m in (2, 3):
        L.feed_forward(m)
        R.tick(m)
    R.tick(4)
    L.end_ff()
    out0 = pltpu.make_async_copy(r["stage"], lo, lsem.at[0])
    out0.start()
    L.back_ff_norm()
    out0.wait()
    L.back_cross_a()
    L.attend_back(*cross, 0, 12)
    R.tick(5)
    L.back([(r["ck"], 5), (r["cv"], 6)], r["stage"], BF)
    out1 = pltpu.make_async_copy(r["stage"], ge, lsem.at[1])
    out1.start()
    L.back([(r["cq"], 4)], r["gn"], F32)
    L.weight_grad(r["nc"], r["cq"], 4)
    L.weight_grad(r["enc"], r["ck"], 5)
    L.weight_grad(r["enc"], r["cv"], 6)
    R.tick(6)
    L.back_cross_norm()
    R.tick(7)
    out1.wait()
    L.back_self_a()
    L.attend_back(*own, 0, 12)
    R.tick(8)
    L.back([(r["q"], 0), (r["k"], 1), (r["v"], 2)], r["gn"], F32)
    L.weight_grad(r["ns"], r["q"], 0)
    L.weight_grad(r["ns"], r["k"], 1)
    L.weight_grad(r["ns"], r["v"], 2)
    R.tick(9)
    L.back_self_norm()
    out2 = pltpu.make_async_copy(r["gb"], gh, lsem.at[2])
    out2.start()
    L.small_grads()
    so, sa, sb = r["small_out"], r["small_a"], r["small_b"]
    for k in range(1, TEAM_S):
        S.go(so.at[(t.s + k) % TEAM_S], sa.at[t.s], r["ss"].at[1, k], r["sr"].at[1, k], others[k - 1])
    sa[t.s] = so[t.s]
    R.tick(10)
    for k in range(1, TEAM_S):
        S.got(sa.at[(t.s + TEAM_S - k) % TEAM_S], r["sr"].at[1, k])
    sb[t.q] = jnp.sum(sa[...].astype(F32), axis=0).astype(BF)
    for k, (qq, d) in enumerate(((t.qx, t.nb[0]), (t.qy, t.nb[1]), (t.qd, t.diag))):
        S.go(sb.at[t.q], sb.at[t.q], r["ss"].at[2, k], r["sr"].at[2, k], d)
    last = max(ENTRY) + STAGES
    R.tick(11)
    for k, qq in enumerate((t.qx, t.qy, t.qd)):
        S.got(sb.at[qq], r["sr"].at[2, k])
    small_fin[...] = jnp.sum(sb[...].astype(F32), axis=0)
    for n in range(12, last):
        R.tick(n)
    R.sent()
    S.sent()
    out2.wait()


def layer(seg_start, seg_parent, bucket, gains, bias, hid, enc, dy, weights, shards):
    trees = seg_start.shape[0]
    tokens = trees * TREE
    V, D = pltpu.VMEM, pltpu.SemaphoreType.DMA
    act = lambda: V((tokens, SQ), BF)
    n, p = len(CHUNKS), len(PHASES)
    scratch = dict(
        sq=V((8, NZ, 2, 96, SQ), BF), gu=V((2, NZ, 2, 2, 48, FFN), BF), dn=V((NZ, 2, 4, 64, SQ), BF),
        rc0=V((4, NZ, 96, SQ), BF), rc1=V((2, NZ, 2, 48, LAND[1]), BF), rc2=V((NZ, 4, 64, SQ), BF),
        hid=act(), enc=act(), dy=act(), local=D((20,)),
        small=V((8, 16, 128), BF), small_out=V((8, 16, 128), BF), small_a=V((8, 16, 128), BF), small_b=V((4, 16, 128), BF),
        ss=D((3, 8)), sr=D((3, 8)), mix=V((16, 128), F32),
    )
    for i in range(3):
        scratch["ra%d" % i] = V((2, 2, NZ, ROWS[i], LAND[i] // 2), BF)
        scratch["rb%d" % i] = V((2, NZ, ROWS[i], LAND[i] // 2), BF)
        scratch["rz%d" % i] = V((NZ - 1, ROWS[i], LAND[i]), BF)
    for i in range(12):
        scratch["g%d" % i] = D((p, 16)) if i == 10 else D((p,)) if i == 11 else D((p, NZ))
    for i, shape in enumerate([(n,), (n,), (n, 2, 2), (n, 2, 2), (n, 2), (n, 2), (n, NZ), (n, NZ), (n, 4), (n, 4)]):
        scratch["r%d" % i] = D(shape)
    scratch.update(layer_scratch(trees))
    hbm, vmem, smem = (pl.BlockSpec(memory_space=m) for m in (pltpu.HBM, pltpu.VMEM, pltpu.SMEM))
    sd = jax.ShapeDtypeStruct
    return pl.pallas_call(
        functools.partial(layer_kernel, list(scratch), shards, trees),
        out_shape=[sd((tokens, SQ), BF)] * 3
        + [sd((4, 96, SQ), BF), sd((4, 96, SQ), BF), sd((4, 48, FFN), BF), sd((4, 64, SQ), BF), sd((16, 128), F32)],
        in_specs=[smem, smem] + [vmem] * 5 + [hbm] * 14,
        out_specs=[hbm] * 3 + [vmem] * 5,
        scratch_shapes=list(scratch.values()),
        compiler_params=pltpu.CompilerParams(collective_id=0, has_side_effects=True, vmem_limit_bytes=64 * 2**20 - 65536),
        name="decoder_layer",
    )(seg_start, seg_parent, bucket, *gains, bias, hid, enc, dy, *weights)


def finish_kernel(lo, gh, ge, f0, f1, f2, f3, small, *refs):
    o_lo, o_gh, o_ge = refs[:3]
    squares, gate, up, down = refs[3:11], refs[11], refs[12], refs[13]
    norms, table = refs[14:17], refs[17]
    a0, a1, a2, b0, b1, b2, b3, w0, w1, w2, w3, sem_in, sem_out = refs[18:]
    pairs = ((f0, b0), (f1, b1), (f2, b2), (f3, b3), (lo, a0), (gh, a1), (ge, a2))
    ins = [pltpu.make_async_copy(a, b, sem_in.at[i]) for i, (a, b) in enumerate(pairs)]
    for cp in ins:
        cp.start()
    for i in range(3):
        norms[i][...] = small[i:i + 1, :96]
    table[...] = small[4:8, :H]
    outs = []

    def out(src, dst):
        cp = pltpu.make_async_copy(src, dst, sem_out.at[len(outs)])
        cp.start()
        outs.append(cp)

    for n, (b, w) in enumerate(((b0, w0), (b1, w1))):
        ins[n].wait()
        for i in range(4):
            w[i] = b[i].astype(F32)
            out(w.at[i], squares[4 * n + i])
    ins[2].wait()
    for i, dst in enumerate((gate, up)):
        w2[i] = b2[2 * i:2 * i + 2].reshape(96, FFN).astype(F32)
        out(w2.at[i], dst)
    ins[3].wait()
    w3[...] = b3[...].reshape(256, SQ).astype(F32)
    out(w3, down)
    for i, dst in enumerate((o_lo, o_gh, o_ge)):
        ins[4 + i].wait()
        out((a0, a1, a2)[i], dst)
    for cp in outs:
        cp.wait()


def finish(outs):
    hbm, vmem = pl.BlockSpec(memory_space=pltpu.HBM), pl.BlockSpec(memory_space=pltpu.VMEM)
    V, sd = pltpu.VMEM, jax.ShapeDtypeStruct
    res = pl.pallas_call(
        finish_kernel,
        out_shape=[sd(o.shape, BF) for o in outs[:3]] + [sd((96, SQ), F32)] * 8 + [sd((96, FFN), F32)] * 2
        + [sd((256, SQ), F32)] + [sd((1, 96), F32)] * 3 + [sd((4, H), F32)],
        in_specs=[hbm] * 7 + [vmem],
        out_specs=[hbm] * 14 + [vmem] * 4,
        scratch_shapes=[V(o.shape, BF) for o in outs[:7]]
        + [V((4, 96, SQ), F32), V((4, 96, SQ), F32), V((2, 96, FFN), F32), V((256, SQ), F32)]
        + [pltpu.SemaphoreType.DMA((7,)), pltpu.SemaphoreType.DMA((14,))],
        compiler_params=pltpu.CompilerParams(vmem_limit_bytes=63 * 2**20),
        name="finish",
    )(*outs)
    return (*res[:3], res[3:11], res[11], res[12], res[13], res[14:17], res[17])


def team_rows(weight, fold):
    if fold == 1:
        return weight
    groups = [[a * fold + b for b in range(fold)] for a in range(TEAM_S)]
    return lax.all_gather(weight, "shard", axis=0, tiled=True, axis_index_groups=groups)


def team_sum(grad, fold, teams_r):
    if fold > 1:
        groups = [[a * fold + b for b in range(fold)] for a in range(TEAM_S)]
        grad = lax.psum_scatter(grad, "shard", scatter_dimension=0, tiled=True, axis_index_groups=groups)
    if teams_r > 1:
        groups = [[a * TEAM_R + b for a in range(teams_r)] for b in range(TEAM_R)]
        grad = lax.psum(grad, "replica", axis_index_groups=groups)
    return grad


def body(
    replicas, shards,
    hidden, encoded, out_grad, seg_start, seg_parent, bucket_of_distance,
    norm_self, self_query, self_key, self_value, self_out, rel_bias,
    norm_cross, cross_query, cross_key, cross_value, cross_out,
    norm_ff, ff_gate, ff_up, ff_down,
):
    fold, teams_r = shards // TEAM_S, replicas // TEAM_R
    big = (self_query, self_key, self_value, self_out, cross_query, cross_key, cross_value, cross_out, ff_gate, ff_up, ff_down)
    flat = lambda v: v.reshape(-1, v.shape[-1])
    outs = layer(
        flat(seg_start), flat(seg_parent), bucket_of_distance.reshape(2, 128),
        [team_rows(g, fold).reshape(1, -1) for g in (norm_self, norm_cross, norm_ff)], team_rows(rel_bias, fold),
        flat(hidden), flat(encoded), flat(out_grad), [team_rows(w, fold) for w in big], shards,
    )
    lo, gh, ge, squares, gate, up, down, norms, table = finish(outs)
    squares = [team_sum(v, fold, teams_r) for v in squares]
    gate, up, down, table = (team_sum(v, fold, teams_r) for v in (gate, up, down, table))
    norms = [team_sum(v.reshape(-1), fold, teams_r) for v in norms]
    lo, gh, ge = (v.reshape(hidden.shape) for v in (lo, gh, ge))
    return (
        lo, gh, ge, norms[0], *squares[:4], table, norms[1], *squares[4:], norms[2], gate, up, down,
    )


def solution(mesh):
    placed = (
        P(None, ("replica", "shard"), None, None),
        P(None, ("replica", "shard"), None, None),
        P(None, ("replica", "shard"), None, None),
        P(None, ("replica", "shard"), None),
        P(None, ("replica", "shard"), None),
        P(),
        P("shard"),
        P("shard", None),
        P("shard", None),
        P("shard", None),
        P("shard", None),
        P("shard", None),
        P("shard"),
        P("shard", None),
        P("shard", None),
        P("shard", None),
        P("shard", None),
        P("shard"),
        P("shard", None),
        P("shard", None),
        P("shard", None),
    )
    return jax.shard_map(
        functools.partial(body, mesh.shape["replica"], mesh.shape["shard"]),
        mesh=mesh,
        in_specs=placed,
        out_specs=(
            P(None, ("replica", "shard"), None, None),
            P(None, ("replica", "shard"), None, None),
            P(None, ("replica", "shard"), None, None),
            P("shard"),
            P("shard", None),
            P("shard", None),
            P("shard", None),
            P("shard", None),
            P("shard", None),
            P("shard"),
            P("shard", None),
            P("shard", None),
            P("shard", None),
            P("shard", None),
            P("shard"),
            P("shard", None),
            P("shard", None),
            P("shard", None),
        ),
        check_vma=False,
    )
```

```python
import functools
import math

import jax
import jax.numpy as jnp
from jax import lax
from jax.experimental import pallas as pl
from jax.experimental.pallas import tpu as pltpu
from jax.sharding import PartitionSpec as P

SQ, FFN, H, DH, TREE, NSEG, NB = 768, 2048, 12, 64, 256, 13, 32
TRUNK, BRANCH, LEAF = 64, 16, 16
BF, F32 = jnp.bfloat16, jnp.float32
EPSILON, NEGATIVE = 1e-6, -1e9
DEPTHS = 128
SEG_LEN = (TRUNK,) + (BRANCH,) * 4 + (LEAF,) * 8
SEG_DEPTH = (0,) + (TRUNK,) * 4 + (TRUNK + BRANCH,) * 8

def nn(a, b): return lax.dot_general(a, b, (((1,), (0,)), ((), ())), preferred_element_type=F32)
def nt(a, b): return lax.dot_general(a, b, (((1,), (1,)), ((), ())), preferred_element_type=F32)
def tn(a, b): return lax.dot_general(a, b, (((0,), (0,)), ((), ())), preferred_element_type=F32)

class Layer:
    def __init__(self, refs, trees):
        self.__dict__.update(refs)
        self.trees = trees
        self.tokens = trees * TREE

    def layout(self):
        for t in range(self.trees):
            def place(shape, axis):
                pos = lax.broadcasted_iota(jnp.int32, shape, axis)
                dep, sid, pid, gid = pos, jnp.zeros_like(pos), jnp.zeros_like(pos), jnp.zeros_like(pos)
                for s in range(NSEG):
                    at = self.seg_start[t, s]
                    inside = (pos >= at) & (pos < at + SEG_LEN[s])
                    dep = dep + jnp.where(inside, SEG_DEPTH[s] - at, 0)
                    sid = jnp.where(inside, s, sid)
                    pid = jnp.where(inside, self.seg_parent[t, s], pid)
                    gid = jnp.where(inside, self.seg_parent[t, self.seg_parent[t, s]], gid)
                return dep, sid, pid, gid
            dep_j, sid_j, _, _ = place((TREE, 1), 0)
            dep_i, sid_i, pid_i, gid_i = place((1, TREE), 1)
            ok = ((sid_j == sid_i) | (sid_j == pid_i) | (sid_j == gid_i)) & (dep_j <= dep_i)
            self.mask[t] = jnp.where(ok, 0.0, NEGATIVE).astype(F32)
            lanes = lax.broadcasted_iota(jnp.int32, (TREE, DEPTHS), 1)
            self.hot[t] = jnp.where(lanes == dep_j, 1.0, 0.0).astype(BF)
            rows = lax.broadcasted_iota(jnp.int32, (DEPTHS, TREE), 0)
            self.hot_t[t] = jnp.where(rows == DEPTHS - 1 - dep_i, 1.0, 0.0).astype(BF)

    def bucket_hot(self):
        row = lax.broadcasted_iota(jnp.int32, (128, DEPTHS), 0)
        inner = row % 16
        bucket = jnp.where((inner >= 4) & (inner < 8), 4 * (row // 16) + inner - 4, -1)
        return jnp.where(self.bucket[...][:1] == bucket, 1.0, 0.0).astype(BF)

    def spread(self, s):
        i = lax.broadcasted_iota(jnp.int32, (128, SQ), 0)
        j = lax.broadcasted_iota(jnp.int32, (128, SQ), 1)
        return jnp.where((j == i + 96 * s) & (i < 96), 1.0, 0.0).astype(BF)

    def small_params(self):
        total = jnp.zeros((16, SQ), F32)
        for s in range(8):
            total = total + nn(self.small[s], self.spread(s))
        self.gains[...] = total
        table = tn(self.small[...].reshape(128, 128), self.bucket_hot())
        for h in range(H):
            row = jnp.broadcast_to(table[h:h + 1], (DEPTHS, DEPTHS))
            self.toep[h] = pltpu.roll(row, 0, 1, stride=1, stride_axis=0).astype(BF)
        self.gain_grads[...] = jnp.zeros_like(self.gain_grads)
        self.bias_grads[...] = jnp.zeros_like(self.bias_grads)

    def small_grads(self):
        hot = self.bucket_hot()
        sums = self.bias_grads[...]
        high = sums.astype(BF)
        low = (sums - high.astype(F32)).astype(BF)
        out = nt(hot, high) + nt(hot, low)
        gains = self.gain_grads[...].astype(BF)
        for s in range(8):
            self.small_out[s] = (out[16 * s:16 * s + 16] + nt(gains, self.spread(s))).astype(BF)

    def norm(self, src, dst, gain):
        g = self.gains[gain:gain + 1, :]
        @pl.loop(0, self.tokens // 64, unroll=4)
        def _(b):
            rows = pl.ds(b * 64, 64)
            v = src[rows, :].astype(F32)
            r = lax.rsqrt(jnp.mean(v * v, axis=-1, keepdims=True) + EPSILON)
            dst[rows, :] = (v * r * g).astype(BF)

    def norm_back(self, src, gain, store):
        g = self.gains[gain:gain + 1, :]
        @pl.loop(0, self.tokens // 64, unroll=4)
        def _(b):
            rows = pl.ds(b * 64, 64)
            v = src[rows, :].astype(F32)
            r = lax.rsqrt(jnp.mean(v * v, axis=-1, keepdims=True) + EPSILON)
            n = v * r
            dh = self.gn[rows, :]
            dg = dh * g
            self.gain_grads[gain:gain + 1, :] += jnp.sum(dh * n, axis=0, keepdims=True)
            store(rows, r * (dg - n * jnp.mean(dg * n, axis=-1, keepdims=True)))

    def wsq(self, w): return self.sq[w].reshape(SQ, SQ)
    def project(self, src, w, dst):
        @pl.loop(0, 3, unroll=3)
        def _(n):
            cols = pl.ds(pl.multiple_of(n * 256, 256), 256)
            wt = self.sq[w, :, :, :, cols].reshape(SQ, 256)
            for t in range(self.trees):
                rows = pl.ds(t * TREE, TREE)
                dst[rows, cols] = nn(src[rows, :], wt).astype(BF)
    def project_add(self, src, w, base, dst):
        @pl.loop(0, 3, unroll=3)
        def _(n):
            cols = pl.ds(pl.multiple_of(n * 256, 256), 256)
            wt = self.sq[w, :, :, :, cols].reshape(SQ, 256)
            for t in range(self.trees):
                rows = pl.ds(t * TREE, TREE)
                dst[rows, cols] = base[rows, cols].astype(F32) + nn(src[rows, :], wt)
    def back(self, pairs, dst, dtype):
        @pl.loop(0, 2, unroll=2)
        def _(n):
            cols = pl.ds(pl.multiple_of(n * 384, 384), 384)
            for t in range(self.trees):
                rows = pl.ds(t * TREE, TREE)
                total = None
                for src, w in pairs:
                    part = nt(src[rows, :], self.sq[w, pl.ds(n * 2, 2)].reshape(384, SQ))
                    total = part if total is None else total + part
                dst[rows, cols] = total.astype(dtype)
    def weight_grad(self, left, right, w):
        @pl.loop(0, 2, unroll=2)
        def _(n):
            cols = pl.ds(pl.multiple_of(n * 384, 384), 384)
            lt = left[:, cols]
            for m in range(3):
                part = tn(lt, right[:, m * 256:(m + 1) * 256])
                self.sq[w, pl.ds(n * 2, 2), :, :, m * 256:(m + 1) * 256] = part.astype(BF).reshape(2, 2, 96, 256)

    def lanes(self):
        low = lax.broadcasted_iota(jnp.int32, (TREE, 128), 1) < DH
        return low, jnp.logical_not(low)
    def attend(self, q, k, v, ctx, probs, masked, first, last):
        halves = self.lanes()
        @pl.loop(first * self.trees // 2, last * self.trees // 2, unroll=3)
        def _(i):
            t, p = i // (H // 2), i % (H // 2)
            rows = pl.ds(pl.multiple_of(t * TREE, TREE), TREE)
            cols = pl.ds(pl.multiple_of(p * 128, 128), 128)
            qp, kp, vt = q[rows, cols], k[rows, cols], v[rows, cols].T
            if masked:
                hot = self.hot[t]
                kp = jnp.concatenate([kp, hot], axis=1)
            outs = []
            for e in range(2):
                qe = jnp.where(halves[e], qp, jnp.zeros_like(qp))
                if masked:
                    qe = jnp.concatenate([qe, nt(hot, self.toep[2 * p + e]).astype(BF)], axis=1)
                s = nt(kp, qe)
                if masked:
                    s = s + self.mask[t]
                x = jnp.exp(s - jnp.max(s, axis=0, keepdims=True))
                pr = (x * (1.0 / jnp.sum(x, axis=0, keepdims=True))).astype(BF)
                probs[2 * i + e] = pr
                outs.append(nn(vt[e * DH:(e + 1) * DH], pr))
            ctx[rows, cols] = jnp.concatenate(outs, axis=0).astype(BF).T
    def attend_back(self, q, k, v, dctx, probs, masked, first, last):
        halves = self.lanes()
        @pl.loop(first * self.trees // 2, last * self.trees // 2, unroll=3)
        def _(i):
            t, p = i // (H // 2), i % (H // 2)
            rows = pl.ds(pl.multiple_of(t * TREE, TREE), TREE)
            cols = pl.ds(pl.multiple_of(p * 128, 128), 128)
            qp, kt, vp, dp = q[rows, cols], k[rows, cols].T, v[rows, cols], dctx[rows, cols]
            dq, dk, dv = [], [], []
            for e in range(2):
                pr = probs[2 * i + e]
                prf = pr.astype(F32)
                g = nt(vp, jnp.where(halves[e], dp, jnp.zeros_like(dp)))
                ds = (prf * (g - jnp.sum(g * prf, axis=0, keepdims=True))).astype(BF)
                dv.append(nn(pr, dp))
                dq.append(nn(kt[e * DH:(e + 1) * DH], ds))
                dk.append(nn(ds, qp))
                if masked:
                    m = nn(nn(self.hot_t[t], ds).astype(BF), self.hot[t])
                    m = pltpu.roll(m, 1, 1, stride=1, stride_axis=0)
                    self.bias_grads[pl.ds(2 * p + e, 1), :] += jnp.sum(m, axis=0, keepdims=True)
            q[rows, cols] = jnp.concatenate(dq, axis=0).astype(BF).T
            k[rows, cols] = jnp.where(halves[0], dk[0], dk[1]).astype(BF)
            v[rows, cols] = jnp.where(halves[0], dv[0], dv[1]).astype(BF)

    def feed_forward(self, m):
        base = pl.multiple_of(m * 512, 512)
        for hf in range(2):
            cols = pl.ds(pl.multiple_of(base + hf * 256, 256), 256)
            wg = self.gu[0, :, :, :, :, cols].reshape(SQ, 256)
            wu = self.gu[1, :, :, :, :, cols].reshape(SQ, 256)
            wd = self.dn[m, hf].reshape(256, SQ)
            here = slice(hf * 256, hf * 256 + 256)
            @pl.loop(0, self.trees, unroll=2)
            def _(t):
                rows = pl.ds(pl.multiple_of(t * TREE, TREE), TREE)
                x = self.nf[rows, :]
                g, u, gi = nn(x, wg), nn(x, wu), nt(self.dy[rows, :], wd)
                c = math.sqrt(2.0 / math.pi)
                th = jnp.tanh(c * (g + 0.044715 * (g * g * g)))
                half = 0.5 * (1.0 + th)
                gelu = g * half
                slope = half + 0.5 * g * (1.0 - th * th) * c * (1.0 + 3 * 0.044715 * (g * g))
                self.inner[rows, here] = (gelu * u).astype(BF)
                self.ggate[rows, here] = (gi * u * slope).astype(BF)
                self.gup[rows, here] = (gi * gelu).astype(BF)
        @pl.loop(0, 3, unroll=3)
        def _(n):
            cols = pl.ds(pl.multiple_of(n * 256, 256), 256)
            wd = self.dn[m, :, :, :, cols].reshape(512, 256)
            for t in range(self.trees):
                rows = pl.ds(t * TREE, TREE)
                self.oacc[rows, cols] += nn(self.inner[rows, :], wd)
        @pl.loop(0, 2, unroll=2)
        def _(n):
            cols = pl.ds(pl.multiple_of(n * 384, 384), 384)
            hid = pl.ds(base, 512)
            wg = self.gu[0, pl.ds(n * 2, 2), :, :, :, hid].reshape(384, 512)
            wu = self.gu[1, pl.ds(n * 2, 2), :, :, :, hid].reshape(384, 512)
            for t in range(self.trees):
                rows = pl.ds(t * TREE, TREE)
                self.gn[rows, cols] += nt(self.ggate[rows, :], wg) + nt(self.gup[rows, :], wu)
        @pl.loop(0, 2, unroll=2)
        def _(n):
            hid = pl.ds(base, 512)
            cols = pl.ds(pl.multiple_of(n * 384, 384), 384)
            lt = self.nf[:, cols]
            self.gu[0, pl.ds(n * 2, 2), :, :, :, hid] = tn(lt, self.ggate[...]).astype(BF).reshape(2, 2, 2, 48, 512)
            self.gu[1, pl.ds(n * 2, 2), :, :, :, hid] = tn(lt, self.gup[...]).astype(BF).reshape(2, 2, 2, 48, 512)
        @pl.loop(0, 3, unroll=3)
        def _(n):
            cols = pl.ds(pl.multiple_of(n * 256, 256), 256)
            self.dn[m, :, :, :, cols] = tn(self.inner[...], self.dy[:, cols]).astype(BF).reshape(2, 4, 64, 256)

    def start_ff(self):
        self.norm(self.after_cross, self.nf, 2)
        self.oacc[...] = self.after_cross[...]
        self.gn[...] = jnp.zeros_like(self.gn)
    def end_ff(self):
        self.stage[...] = self.oacc[...].astype(BF)
    def back_ff_norm(self):
        def store(rows, dv):
            total = self.dy[rows, :].astype(F32) + dv
            self.oacc[rows, :] = total
            self.gb[rows, :] = total.astype(BF)
        self.norm_back(self.after_cross, 2, store)
    def back_cross_a(self):
        self.weight_grad_after(self.cctx, self.gb, 7, self.cctx)
    def weight_grad_after(self, ctx, grad, w, dst):
        self.back([(grad, w)], self.stage, BF)
        self.weight_grad(ctx, grad, w)
        dst[...] = self.stage[...]
    def back_cross_norm(self):
        def store(rows, dv):
            total = self.oacc[rows, :] + dv
            self.oacc[rows, :] = total
            self.gb[rows, :] = total.astype(BF)
        self.norm_back(self.after_self, 1, store)
    def back_self_a(self):
        self.weight_grad_after(self.ctx, self.gb, 3, self.ctx)
    def back_self_norm(self):
        def store(rows, dv):
            self.gb[rows, :] = (self.oacc[rows, :] + dv).astype(BF)
        self.norm_back(self.hid, 0, store)

def layer_scratch(trees):
    T = trees * TREE
    V = pltpu.VMEM
    b = lambda: V((T, SQ), BF)
    f = lambda: V((T, SQ), F32)
    d = {k: b() for k in ("ns", "q", "k", "v", "ctx", "nc", "cq", "ck", "cv", "cctx", "nf", "gb", "stage")}
    d.update({k: f() for k in ("after_self", "after_cross", "oacc", "gn")})
    d.update(ps=V((trees * H, TREE, TREE), BF), pc=V((trees * H, TREE, TREE), BF),
             mask=V((trees, TREE, TREE), F32), hot=V((trees, TREE, DEPTHS), BF), hot_t=V((trees, DEPTHS, TREE), BF),
             toep=V((H, DEPTHS, DEPTHS), BF), gains=V((16, SQ), F32), gain_grads=V((16, SQ), F32),
             bias_grads=V((128, 128), F32), inner=V((T, 512), BF), ggate=V((T, 512), BF), gup=V((T, 512), BF))
    return d


MESH = pl.DeviceIdType.MESH
TEAM_R, TEAM_S = 4, 8
NZ = TEAM_S // 2


class Team:
    def __init__(self, shard_count):
        self.fold = shard_count // TEAM_S
        r = lax.axis_index("replica")
        s = lax.axis_index("shard")
        self.base_r = (r // TEAM_R) * TEAM_R
        self.q = r % TEAM_R
        self.off_s = s % self.fold
        self.s = s // self.fold
        self.z = self.s // 2
        self.c = self.s % 2
        self.qx = self.q + 1 - 2 * (self.q % 2)
        self.qy = self.q + 2 - 4 * (self.q // 2)
        self.qd = 3 - self.q
        self.sib = self.dev(self.q, self.z * 2 + 1 - self.c)
        self.nb = (self.dev(self.qx, self.s), self.dev(self.qy, self.s))
        self.diag = self.dev(self.qd, self.s)
        self.qn = (self.qx, self.qy)

    def dev(self, q, s):
        return (self.base_r + q, s * self.fold + self.off_s)

    def zdev(self, k):
        return self.dev(self.q, ((self.z + k) % NZ) * 2 + self.c)

    def zsrc(self, k):
        return (self.z + NZ - k) % NZ


def rcopy(src, dst, send_sem, recv_sem, device):
    return pltpu.make_async_remote_copy(
        src_ref=src, dst_ref=dst, send_sem=send_sem, recv_sem=recv_sem, device_id=device, device_id_type=MESH
    )


class Sender:
    def __init__(self, team):
        self.t = team
        self.sends = {}

    def go(self, src, dst, send_sem, recv_sem, device, key=0):
        cp = rcopy(src, dst, send_sem, recv_sem, device)
        cp.start()
        self.sends.setdefault(key, []).append(cp)

    def got(self, ref, sem):
        rcopy(ref, ref, sem, sem, self.t.sib).wait_recv()

    def sent(self, key=0):
        for cp in self.sends.pop(key, ()):
            cp.wait_send()


PHASES = (("sq", 0, SQ), ("sq", 4, SQ), ("gu", 0, 1024), ("dn", 0, SQ), ("gu", 1024, 1024))


class Gather(Sender):
    def __init__(self, team, bufs, sems):
        super().__init__(team)
        self.done = [0, 0, 0]
        self.sq, self.gu, self.dn = bufs
        (self.zs, self.zr, self.xs, self.xr, self.ys, self.yr, self.dxs, self.dxr, self.dys, self.dyr, self.cs, self.cr) = sems

    def piece(self, p, q, z, half=None):
        kind, first, n = PHASES[p]
        c = self.t.c
        lo = 0 if half is None else half * (n // 2)
        w = n if half is None else n // 2
        if kind == "sq":
            ref = self.sq.at[first + q, z, c]
        elif kind == "gu":
            ref, lo = self.gu.at[q // 2, z, c, q % 2], lo + first
        else:
            ref = self.dn.at[z, c, q]
        return ref.at[:, pl.ds(lo, w)]

    def all_of(self, p, z, c):
        kind, first, n = PHASES[p]
        if kind == "sq":
            return self.sq.at[pl.ds(first, 4), z, c]
        if kind == "gu":
            return self.gu.at[:, z, c, :, :, pl.ds(first, n)]
        return self.dn.at[z, c]

    def begin(self, p):
        t = self.t
        ref = self.piece(p, t.q, t.z)
        for k in range(1, NZ):
            self.go(ref, ref, self.zs.at[p, k], self.zr.at[p, k], t.zdev(k), p)
        own = self.all_of(p, t.z, t.c)
        self.go(own, own, self.cs.at[p, 0], self.cr.at[p], t.sib, p)

    def zstep(self, p, k):
        t = self.t
        ref = self.piece(p, t.q, t.zsrc(k))
        self.got(ref, self.zr.at[p, k])
        self.go(ref, ref, self.xs.at[p, k], self.xr.at[p, k], t.nb[0], p)
        self.go(ref, ref, self.ys.at[p, k], self.yr.at[p, k], t.nb[1], p)
        self.go(ref, ref, self.cs.at[p, 5 * k - 4], self.cr.at[p], t.sib, p)

    def xystep(self, p, k):
        t = self.t
        z = t.zsrc(k)
        ref = self.piece(p, t.qx, z)
        self.got(ref, self.xr.at[p, k])
        h = self.piece(p, t.qx, z, 0)
        self.go(h, h, self.dys.at[p, k], self.dyr.at[p, k], t.nb[1], p)
        self.go(ref, ref, self.cs.at[p, 5 * k - 3], self.cr.at[p], t.sib, p)
        ref = self.piece(p, t.qy, z)
        self.got(ref, self.yr.at[p, k])
        h = self.piece(p, t.qy, z, 1)
        self.go(h, h, self.dxs.at[p, k], self.dxr.at[p, k], t.nb[0], p)
        self.go(ref, ref, self.cs.at[p, 5 * k - 2], self.cr.at[p], t.sib, p)

    def dstep(self, p, k):
        t = self.t
        z = t.zsrc(k)
        for half, sem, i in ((0, self.dyr, 1), (1, self.dxr, 0)):
            h = self.piece(p, t.qd, z, half)
            self.got(h, sem.at[p, k])
            self.go(h, h, self.cs.at[p, 5 * k - i], self.cr.at[p], t.sib, p)

    def run(self, nz, nx, nd):
        for i in range(max(self.done[0], nz)):
            for step, (what, upto) in enumerate(((self.zstep, nz), (self.xystep, nx), (self.dstep, nd))):
                n = self.done[step]
                if n < upto:
                    p, k = n // (NZ - 1), n % (NZ - 1) + 1
                    if step == 0 and k == 1 and p + 2 < len(PHASES):
                        self.begin(p + 2)
                    what(p, k)
                    self.done[step] += 1

    def whole(self, p):
        self.got(self.all_of(p, slice(None), 1 - self.t.c), self.cr.at[p])


CHUNKS = (
    ("gu", 0, 0, 48, 0, 512),
    ("gu", 0, 0, 48, 512, 512),
    ("gu", 0, 0, 48, 1024, 512),
    ("gu", 0, 0, 48, 1536, 512),
    ("dn", 0, 0, 64, 0, SQ),
    ("sq", 4, 0, 48, 0, SQ),
    ("sq", 4, 48, 48, 0, SQ),
    ("sq", 0, 0, 48, 0, SQ),
    ("sq", 0, 48, 48, 0, SQ),
)
ENTRY = (0, 1, 2, 3, 4, 6, 7, 9, 10)
KINDS = {"sq": 0, "gu": 1, "dn": 2}
ROWS = (96, 48, 64)
LAND = (SQ, 1536, SQ)
STAGES = 7


class Reduce(Sender):
    def __init__(self, team, bufs, rc, r1, r2, rz, fin, sems):
        super().__init__(team)
        self.sq, self.gu, self.dn = bufs
        self.rc, self.r1, self.r2, self.rz, self.fin = rc, r1, r2, rz, fin
        (self.s_c, self.r_c, self.s_1, self.r_1, self.s_2, self.r_2, self.s_z, self.r_z, self.s_f, self.r_f) = sems

    def rows(self, ch):
        return pl.ds(ch[2], ch[3])

    def cols(self, ch, h=None):
        if h is None:
            return pl.ds(ch[4], ch[5])
        return pl.ds(ch[4] + h * (ch[5] // 2), ch[5] // 2)

    def land(self, ch):
        return pl.ds((ch[4] % LAND[KINDS[ch[0]]]) // 2, ch[5] // 2)

    def spot(self, ch):
        return pl.ds(ch[4] % LAND[KINDS[ch[0]]], ch[5])

    def view(self, ch, q, z, c, h=None):
        kind, w = ch[0], ch[1]
        rows, cols = self.rows(ch), self.cols(ch, h)
        if kind == "sq":
            return self.sq.at[w + q, z, c, rows, cols]
        if kind == "gu":
            return self.gu.at[q // 2, z, c, q % 2, rows, cols]
        return self.dn.at[z, c, q, rows, cols]

    def half(self, ch, c):
        kind, w = ch[0], ch[1]
        rows, cols = self.rows(ch), self.cols(ch)
        if kind == "sq":
            return self.sq.at[pl.ds(w, 4), :, c, rows, cols]
        if kind == "gu":
            return self.gu.at[:, :, c, :, rows, cols]
        return self.dn.at[:, c, :, rows, cols]

    def from_core(self, ch, q=None, z=None):
        b = self.rc[KINDS[ch[0]]]
        rows, cols = self.rows(ch), self.spot(ch)
        if ch[0] == "sq":
            return b.at[:, :, rows, cols] if q is None else b.at[q, z, rows, cols]
        if ch[0] == "gu":
            return b.at[:, :, :, rows, cols] if q is None else b.at[q // 2, z, q % 2, rows, cols]
        return b.at[:, :, rows, cols] if q is None else b.at[z, q, rows, cols]

    def final(self, ch):
        return self.fin[0 if ch[1] == 0 else 1] if ch[0] == "sq" else self.fin[1 + KINDS[ch[0]]]

    def stage(self, st, i):
        t, ch = self.t, CHUNKS[i]
        q, z, c = t.q, t.z, t.c
        kd = KINDS[ch[0]]
        rows, land = self.rows(ch), self.land(ch)
        if st == 0:
            self.go(self.half(ch, 1 - c), self.from_core(ch), self.s_c.at[i], self.r_c.at[i], t.sib)
        elif st == 1:
            self.got(self.from_core(ch), self.r_c.at[i])

            @pl.loop(0, 4 * NZ)
            def _(j):
                a, b = self.view(ch, j // NZ, j % NZ, c), self.from_core(ch, j // NZ, j % NZ)
                a[...] = a[...] + b[...]

            for h in range(2):
                for m, qq in enumerate((t.qn[h], t.qd)):
                    slot = (qq // 2) if h == 0 else (qq % 2)
                    self.go(
                        self.view(ch, qq, slice(None), c, h), self.r1[kd].at[h, slot, :, rows, land],
                        self.s_1.at[i, h, m], self.r_1.at[i, h, m], t.nb[h],
                    )
        elif st == 2:
            for h in range(2):
                for m, qq in ((1, t.qn[1 - h]), (0, q)):
                    slot = (qq // 2) if h == 0 else (qq % 2)
                    self.got(self.r1[kd].at[h, slot, :, rows, land], self.r_1.at[i, h, m])

                    @pl.loop(0, NZ)
                    def _(j):
                        a = self.view(ch, qq, j, c, h)
                        a[...] = a[...] + self.r1[kd][h, slot, j, rows, land]

            for h in range(2):
                self.go(
                    self.view(ch, t.qn[1 - h], slice(None), c, h), self.r2[kd].at[h, :, rows, land],
                    self.s_2.at[i, h], self.r_2.at[i, h], t.nb[1 - h],
                )
        elif st == 3:
            for h in range(2):
                self.got(self.r2[kd].at[h, :, rows, land], self.r_2.at[i, h])

                @pl.loop(0, NZ)
                def _(j):
                    a = self.view(ch, q, j, c, h)
                    a[...] = a[...] + self.r2[kd][h, j, rows, land]

            for k in range(1, NZ):
                self.go(
                    self.view(ch, q, (z + k) % NZ, c), self.rz[kd].at[k - 1, rows, self.spot(ch)],
                    self.s_z.at[i, k], self.r_z.at[i, k], t.zdev(k),
                )
        elif st == 4:
            v = self.view(ch, q, z, c)[...].astype(F32)
            for k in range(1, NZ):
                self.got(self.rz[kd].at[k - 1, rows, self.spot(ch)], self.r_z.at[i, k])
                v = v + self.rz[kd][k - 1, rows, self.spot(ch)].astype(F32)
            f = self.final(ch).at[q, rows, self.cols(ch)]
            f[...] = v.astype(BF)
            for h in range(2):
                self.go(f, f, self.s_f.at[i, h], self.r_f.at[i, h], t.nb[h])
        elif st == 5:
            for h in range(2):
                self.got(self.final(ch).at[t.qn[h], rows, self.cols(ch)], self.r_f.at[i, h])
                f = self.final(ch).at[t.qn[h], rows, self.cols(ch, h)]
                self.go(f, f, self.s_f.at[i, 2 + h], self.r_f.at[i, 2 + h], t.nb[1 - h])
        else:
            for h in range(2):
                self.got(self.final(ch).at[t.qd, rows, self.cols(ch, h)], self.r_f.at[i, 2 + h])

    def tick(self, n):
        for st in (1, 0, 6, 5, 4, 3, 2):
            for i, entry in enumerate(ENTRY):
                if n - entry == st:
                    self.stage(st, i)


def layer_kernel(names, shards, trees, *refs):
    seg_start, seg_parent, bucket, *gains_in, bias_in, hid_in, enc_in, dy_in = refs[:10]
    weights = refs[10:21]
    lo, gh, ge, f0, f1, f2, f3, small_fin = refs[21:29]
    r = dict(zip(names, refs[29:]))
    bufs = (r["sq"], r["gu"], r["dn"])
    t = Team(shards)
    L = Layer(dict(r, seg_start=seg_start, seg_parent=seg_parent, bucket=bucket), trees)
    G = Gather(t, bufs, [r["g%d" % i] for i in range(12)])
    R = Reduce(
        t, bufs, [r["rc0"], r["rc1"], r["rc2"]], [r["ra0"], r["ra1"], r["ra2"]], [r["rb0"], r["rb1"], r["rb2"]],
        [r["rz0"], r["rz1"], r["rz2"]], (f0, f1, f2, f3), [r["r%d" % i] for i in range(10)],
    )
    S = Sender(t)

    loc, lsem = [], r["local"]

    def fetch(src, dst):
        cp = pltpu.make_async_copy(src, dst, lsem.at[len(loc)])
        cp.start()
        loc.append(cp)

    z, c = t.z, t.c
    for i in range(8):
        fetch(weights[i], r["sq"].at[i, z, c])
    for i in range(2):
        for h in range(2):
            fetch(weights[8 + i].at[pl.ds(h * 48, 48)], r["gu"].at[i, z, c, h])
    for h in range(4):
        fetch(weights[10].at[pl.ds(h * 64, 64)], r["dn"].at[z, c, h])
    fetch(hid_in, r["hid"])
    fetch(enc_in, r["enc"])
    fetch(dy_in, r["dy"])

    others = [t.dev(t.q, (t.s + k) % TEAM_S) for k in range(1, TEAM_S)]
    greet = others + list(t.nb) + [t.diag]
    barrier = pltpu.get_barrier_semaphore()
    for d in greet:
        pl.semaphore_signal(barrier, inc=1, device_id=d, device_id_type=MESH)
    pl.semaphore_wait(barrier, len(greet))
    for cp in loc:
        cp.wait()

    small, mix = r["small"], r["mix"]
    mix[...] = jnp.zeros_like(mix)
    for i in range(3):
        mix[i:i + 1, :96] = gains_in[i][...].astype(F32)
    mix[4:8, :H] = bias_in[...].astype(F32)
    small[t.s] = mix[...].astype(BF)
    for k in range(1, TEAM_S):
        S.go(small.at[t.s], small.at[t.s], r["ss"].at[0, k], r["sr"].at[0, k], others[k - 1])
    G.begin(0)
    G.begin(1)
    L.layout()
    G.run(1, 0, 0)
    for k in range(1, TEAM_S):
        S.got(small.at[(t.s + TEAM_S - k) % TEAM_S], r["sr"].at[0, k])
    L.small_params()
    G.run(2, 1, 0)
    L.norm(r["hid"], r["ns"], 0)
    G.run(3, 2, 1)
    G.run(4, 3, 2)
    G.run(5, 4, 3)
    G.run(6, 4, 3)
    own = (r["q"], r["k"], r["v"], r["ctx"], r["ps"], True)
    cross = (r["cq"], r["ck"], r["cv"], r["cctx"], r["pc"], False)
    G.whole(0)
    for w in range(3):
        L.project(r["ns"], w, own[w])
    for n in range(4):
        G.run(7 + n, 5 + n, 3 + n)
        L.attend(*own, 3 * n, 3 * n + 3)
    G.run(11, 9, 7)
    L.project_add(r["ctx"], 3, r["hid"], r["after_self"])
    L.norm(r["after_self"], r["nc"], 1)
    G.whole(1)
    L.project(r["nc"], 4, r["cq"])
    G.run(12, 10, 8)
    L.project(r["enc"], 5, r["ck"])
    L.project(r["enc"], 6, r["cv"])
    L.attend(*cross, 0, 3)
    G.run(13, 11, 9)
    L.attend(*cross, 3, 9)
    G.run(14, 12, 10)
    L.attend(*cross, 9, 12)
    L.project_add(r["cctx"], 7, r["after_self"], r["after_cross"])
    G.run(15, 13, 11)
    L.start_ff()
    G.run(15, 14, 12)
    for p in (2, 3):
        G.whole(p)
    G.run(15, 15, 13)
    for p in (2, 3):
        G.sent(p)

    L.feed_forward(0)
    G.run(15, 15, 15)
    R.tick(0)
    L.feed_forward(1)
    R.tick(1)
    G.whole(4)
    for p in (4, 0, 1):
        G.sent(p)
    S.sent()
    for m in (2, 3):
        L.feed_forward(m)
        R.tick(m)
    L.end_ff()
    out0 = pltpu.make_async_copy(r["stage"], lo, lsem.at[0])
    out0.start()
    L.back_ff_norm()
    out0.wait()
    L.back_cross_a()
    R.tick(4)
    L.attend_back(*cross, 0, 6)
    R.tick(5)
    L.attend_back(*cross, 6, 12)
    L.back([(r["ck"], 5), (r["cv"], 6)], r["stage"], BF)
    out1 = pltpu.make_async_copy(r["stage"], ge, lsem.at[1])
    out1.start()
    L.back([(r["cq"], 4)], r["gn"], F32)
    L.weight_grad(r["nc"], r["cq"], 4)
    L.weight_grad(r["enc"], r["ck"], 5)
    L.weight_grad(r["enc"], r["cv"], 6)
    R.tick(6)
    L.back_cross_norm()
    out1.wait()
    L.back_self_a()
    L.attend_back(*own, 0, 3)
    R.tick(7)
    L.attend_back(*own, 3, 9)
    R.tick(8)
    L.attend_back(*own, 9, 12)
    L.back([(r["q"], 0), (r["k"], 1), (r["v"], 2)], r["gn"], F32)
    L.weight_grad(r["ns"], r["q"], 0)
    L.weight_grad(r["ns"], r["k"], 1)
    L.weight_grad(r["ns"], r["v"], 2)
    R.tick(9)
    L.back_self_norm()
    out2 = pltpu.make_async_copy(r["gb"], gh, lsem.at[2])
    out2.start()
    L.small_grads()
    so, sa, sb = r["small_out"], r["small_a"], r["small_b"]
    for k in range(1, TEAM_S):
        S.go(so.at[(t.s + k) % TEAM_S], sa.at[t.s], r["ss"].at[1, k], r["sr"].at[1, k], others[k - 1])
    sa[t.s] = so[t.s]
    R.tick(10)
    for k in range(1, TEAM_S):
        S.got(sa.at[(t.s + TEAM_S - k) % TEAM_S], r["sr"].at[1, k])
    sb[t.q] = jnp.sum(sa[...].astype(F32), axis=0).astype(BF)
    for k, (qq, d) in enumerate(((t.qx, t.nb[0]), (t.qy, t.nb[1]), (t.qd, t.diag))):
        S.go(sb.at[t.q], sb.at[t.q], r["ss"].at[2, k], r["sr"].at[2, k], d)
    last = max(ENTRY) + STAGES
    R.tick(11)
    for k, qq in enumerate((t.qx, t.qy, t.qd)):
        S.got(sb.at[qq], r["sr"].at[2, k])
    small_fin[...] = jnp.sum(sb[...].astype(F32), axis=0)
    for n in range(12, last):
        R.tick(n)
    R.sent()
    S.sent()
    out2.wait()


def layer(seg_start, seg_parent, bucket, gains, bias, hid, enc, dy, weights, shards):
    trees = seg_start.shape[0]
    tokens = trees * TREE
    V, D = pltpu.VMEM, pltpu.SemaphoreType.DMA
    act = lambda: V((tokens, SQ), BF)
    n, p = len(CHUNKS), len(PHASES)
    scratch = dict(
        sq=V((8, NZ, 2, 96, SQ), BF), gu=V((2, NZ, 2, 2, 48, FFN), BF), dn=V((NZ, 2, 4, 64, SQ), BF),
        rc0=V((4, NZ, 96, SQ), BF), rc1=V((2, NZ, 2, 48, LAND[1]), BF), rc2=V((NZ, 4, 64, SQ), BF),
        hid=act(), enc=act(), dy=act(), local=D((20,)),
        small=V((8, 16, 128), BF), small_out=V((8, 16, 128), BF), small_a=V((8, 16, 128), BF), small_b=V((4, 16, 128), BF),
        ss=D((3, 8)), sr=D((3, 8)), mix=V((16, 128), F32),
    )
    for i in range(3):
        scratch["ra%d" % i] = V((2, 2, NZ, ROWS[i], LAND[i] // 2), BF)
        scratch["rb%d" % i] = V((2, NZ, ROWS[i], LAND[i] // 2), BF)
        scratch["rz%d" % i] = V((NZ - 1, ROWS[i], LAND[i]), BF)
    for i in range(12):
        scratch["g%d" % i] = D((p, 16)) if i == 10 else D((p,)) if i == 11 else D((p, NZ))
    for i, shape in enumerate([(n,), (n,), (n, 2, 2), (n, 2, 2), (n, 2), (n, 2), (n, NZ), (n, NZ), (n, 4), (n, 4)]):
        scratch["r%d" % i] = D(shape)
    scratch.update(layer_scratch(trees))
    hbm, vmem, smem = (pl.BlockSpec(memory_space=m) for m in (pltpu.HBM, pltpu.VMEM, pltpu.SMEM))
    sd = jax.ShapeDtypeStruct
    return pl.pallas_call(
        functools.partial(layer_kernel, list(scratch), shards, trees),
        out_shape=[sd((tokens, SQ), BF)] * 3
        + [sd((4, 96, SQ), BF), sd((4, 96, SQ), BF), sd((4, 48, FFN), BF), sd((4, 64, SQ), BF), sd((16, 128), F32)],
        in_specs=[smem, smem] + [vmem] * 5 + [hbm] * 14,
        out_specs=[hbm] * 3 + [vmem] * 5,
        scratch_shapes=list(scratch.values()),
        compiler_params=pltpu.CompilerParams(collective_id=0, has_side_effects=True, vmem_limit_bytes=64 * 2**20 - 65536),
        name="decoder_layer",
    )(seg_start, seg_parent, bucket, *gains, bias, hid, enc, dy, *weights)


def finish_kernel(lo, gh, ge, f0, f1, f2, f3, small, *refs):
    o_lo, o_gh, o_ge = refs[:3]
    squares, gate, up, down = refs[3:11], refs[11], refs[12], refs[13]
    norms, table = refs[14:17], refs[17]
    a0, a1, a2, b0, b1, b2, b3, w0, w1, w2, w3, sem_in, sem_out = refs[18:]
    pairs = ((f0, b0), (f1, b1), (f2, b2), (f3, b3), (lo, a0), (gh, a1), (ge, a2))
    ins = [pltpu.make_async_copy(a, b, sem_in.at[i]) for i, (a, b) in enumerate(pairs)]
    for cp in ins:
        cp.start()
    for i in range(3):
        norms[i][...] = small[i:i + 1, :96]
    table[...] = small[4:8, :H]
    outs = []

    def out(src, dst):
        cp = pltpu.make_async_copy(src, dst, sem_out.at[len(outs)])
        cp.start()
        outs.append(cp)

    for n, (b, w) in enumerate(((b0, w0), (b1, w1))):
        ins[n].wait()
        for i in range(4):
            w[i] = b[i].astype(F32)
            out(w.at[i], squares[4 * n + i])
    ins[2].wait()
    for i, dst in enumerate((gate, up)):
        w2[i] = b2[2 * i:2 * i + 2].reshape(96, FFN).astype(F32)
        out(w2.at[i], dst)
    ins[3].wait()
    w3[...] = b3[...].reshape(256, SQ).astype(F32)
    out(w3, down)
    for i, dst in enumerate((o_lo, o_gh, o_ge)):
        ins[4 + i].wait()
        out((a0, a1, a2)[i], dst)
    for cp in outs:
        cp.wait()


def finish(outs):
    hbm, vmem = pl.BlockSpec(memory_space=pltpu.HBM), pl.BlockSpec(memory_space=pltpu.VMEM)
    V, sd = pltpu.VMEM, jax.ShapeDtypeStruct
    res = pl.pallas_call(
        finish_kernel,
        out_shape=[sd(o.shape, BF) for o in outs[:3]] + [sd((96, SQ), F32)] * 8 + [sd((96, FFN), F32)] * 2
        + [sd((256, SQ), F32)] + [sd((1, 96), F32)] * 3 + [sd((4, H), F32)],
        in_specs=[hbm] * 7 + [vmem],
        out_specs=[hbm] * 14 + [vmem] * 4,
        scratch_shapes=[V(o.shape, BF) for o in outs[:7]]
        + [V((4, 96, SQ), F32), V((4, 96, SQ), F32), V((2, 96, FFN), F32), V((256, SQ), F32)]
        + [pltpu.SemaphoreType.DMA((7,)), pltpu.SemaphoreType.DMA((14,))],
        compiler_params=pltpu.CompilerParams(vmem_limit_bytes=63 * 2**20),
        name="finish",
    )(*outs)
    return (*res[:3], res[3:11], res[11], res[12], res[13], res[14:17], res[17])


def team_rows(weight, fold):
    if fold == 1:
        return weight
    groups = [[a * fold + b for b in range(fold)] for a in range(TEAM_S)]
    return lax.all_gather(weight, "shard", axis=0, tiled=True, axis_index_groups=groups)


def team_sum(grad, fold, teams_r):
    if fold > 1:
        groups = [[a * fold + b for b in range(fold)] for a in range(TEAM_S)]
        grad = lax.psum_scatter(grad, "shard", scatter_dimension=0, tiled=True, axis_index_groups=groups)
    if teams_r > 1:
        groups = [[a * TEAM_R + b for a in range(teams_r)] for b in range(TEAM_R)]
        grad = lax.psum(grad, "replica", axis_index_groups=groups)
    return grad


def body(
    replicas, shards,
    hidden, encoded, out_grad, seg_start, seg_parent, bucket_of_distance,
    norm_self, self_query, self_key, self_value, self_out, rel_bias,
    norm_cross, cross_query, cross_key, cross_value, cross_out,
    norm_ff, ff_gate, ff_up, ff_down,
):
    fold, teams_r = shards // TEAM_S, replicas // TEAM_R
    big = (self_query, self_key, self_value, self_out, cross_query, cross_key, cross_value, cross_out, ff_gate, ff_up, ff_down)
    flat = lambda v: v.reshape(-1, v.shape[-1])
    outs = layer(
        flat(seg_start), flat(seg_parent), bucket_of_distance.reshape(2, 128),
        [team_rows(g, fold).reshape(1, -1) for g in (norm_self, norm_cross, norm_ff)], team_rows(rel_bias, fold),
        flat(hidden), flat(encoded), flat(out_grad), [team_rows(w, fold) for w in big], shards,
    )
    lo, gh, ge, squares, gate, up, down, norms, table = finish(outs)
    squares = [team_sum(v, fold, teams_r) for v in squares]
    gate, up, down, table = (team_sum(v, fold, teams_r) for v in (gate, up, down, table))
    norms = [team_sum(v.reshape(-1), fold, teams_r) for v in norms]
    lo, gh, ge = (v.reshape(hidden.shape) for v in (lo, gh, ge))
    return (
        lo, gh, ge, norms[0], *squares[:4], table, norms[1], *squares[4:], norms[2], gate, up, down,
    )


def solution(mesh):
    placed = (
        P(None, ("replica", "shard"), None, None),
        P(None, ("replica", "shard"), None, None),
        P(None, ("replica", "shard"), None, None),
        P(None, ("replica", "shard"), None),
        P(None, ("replica", "shard"), None),
        P(),
        P("shard"),
        P("shard", None),
        P("shard", None),
        P("shard", None),
        P("shard", None),
        P("shard", None),
        P("shard"),
        P("shard", None),
        P("shard", None),
        P("shard", None),
        P("shard", None),
        P("shard"),
        P("shard", None),
        P("shard", None),
        P("shard", None),
    )
    return jax.shard_map(
        functools.partial(body, mesh.shape["replica"], mesh.shape["shard"]),
        mesh=mesh,
        in_specs=placed,
        out_specs=(
            P(None, ("replica", "shard"), None, None),
            P(None, ("replica", "shard"), None, None),
            P(None, ("replica", "shard"), None, None),
            P("shard"),
            P("shard", None),
            P("shard", None),
            P("shard", None),
            P("shard", None),
            P("shard", None),
            P("shard"),
            P("shard", None),
            P("shard", None),
            P("shard", None),
            P("shard", None),
            P("shard"),
            P("shard", None),
            P("shard", None),
            P("shard", None),
        ),
        check_vma=False,
    )
```

```python
import functools
import math

import jax
import jax.numpy as jnp
from jax import lax
from jax.experimental import pallas as pl
from jax.experimental.pallas import tpu as pltpu
from jax.sharding import PartitionSpec as P

SQ, FFN, H, DH, TREE, NSEG, NB = 768, 2048, 12, 64, 256, 13, 32
TRUNK, BRANCH, LEAF = 64, 16, 16
BF, F32 = jnp.bfloat16, jnp.float32
EPSILON, NEGATIVE = 1e-6, -1e9
DEPTHS = 128
SEG_LEN = (TRUNK,) + (BRANCH,) * 4 + (LEAF,) * 8
SEG_DEPTH = (0,) + (TRUNK,) * 4 + (TRUNK + BRANCH,) * 8

def nn(a, b): return lax.dot_general(a, b, (((1,), (0,)), ((), ())), preferred_element_type=F32)
def nt(a, b): return lax.dot_general(a, b, (((1,), (1,)), ((), ())), preferred_element_type=F32)
def tn(a, b): return lax.dot_general(a, b, (((0,), (0,)), ((), ())), preferred_element_type=F32)

class Layer:
    def __init__(self, refs, trees):
        self.__dict__.update(refs)
        self.trees = trees
        self.tokens = trees * TREE

    def layout(self):
        for t in range(self.trees):
            def place(shape, axis):
                pos = lax.broadcasted_iota(jnp.int32, shape, axis)
                dep, sid, pid, gid = pos, jnp.zeros_like(pos), jnp.zeros_like(pos), jnp.zeros_like(pos)
                for s in range(NSEG):
                    at = self.seg_start[t, s]
                    inside = (pos >= at) & (pos < at + SEG_LEN[s])
                    dep = dep + jnp.where(inside, SEG_DEPTH[s] - at, 0)
                    sid = jnp.where(inside, s, sid)
                    pid = jnp.where(inside, self.seg_parent[t, s], pid)
                    gid = jnp.where(inside, self.seg_parent[t, self.seg_parent[t, s]], gid)
                return dep, sid, pid, gid
            dep_j, sid_j, _, _ = place((TREE, 1), 0)
            dep_i, sid_i, pid_i, gid_i = place((1, TREE), 1)
            ok = ((sid_j == sid_i) | (sid_j == pid_i) | (sid_j == gid_i)) & (dep_j <= dep_i)
            self.mask[t] = jnp.where(ok, 0.0, NEGATIVE).astype(F32)
            lanes = lax.broadcasted_iota(jnp.int32, (TREE, DEPTHS), 1)
            self.hot[t] = jnp.where(lanes == dep_j, 1.0, 0.0).astype(BF)
            rows = lax.broadcasted_iota(jnp.int32, (DEPTHS, TREE), 0)
            self.hot_t[t] = jnp.where(rows == DEPTHS - 1 - dep_i, 1.0, 0.0).astype(BF)

    def bucket_hot(self):
        row = lax.broadcasted_iota(jnp.int32, (128, DEPTHS), 0)
        inner = row % 16
        bucket = jnp.where((inner >= 4) & (inner < 8), 4 * (row // 16) + inner - 4, -1)
        return jnp.where(self.bucket[...][:1] == bucket, 1.0, 0.0).astype(BF)

    def spread(self, s):
        i = lax.broadcasted_iota(jnp.int32, (128, SQ), 0)
        j = lax.broadcasted_iota(jnp.int32, (128, SQ), 1)
        return jnp.where((j == i + 96 * s) & (i < 96), 1.0, 0.0).astype(BF)

    def small_params(self):
        total = jnp.zeros((16, SQ), F32)
        for s in range(8):
            total = total + nn(self.small[s], self.spread(s))
        self.gains[...] = total
        table = tn(self.small[...].reshape(128, 128), self.bucket_hot())
        for h in range(H):
            row = jnp.broadcast_to(table[h:h + 1], (DEPTHS, DEPTHS))
            self.toep[h] = pltpu.roll(row, 0, 1, stride=1, stride_axis=0).astype(BF)
        self.gain_grads[...] = jnp.zeros_like(self.gain_grads)
        self.bias_grads[...] = jnp.zeros_like(self.bias_grads)

    def small_grads(self):
        hot = self.bucket_hot()
        sums = self.bias_grads[...]
        high = sums.astype(BF)
        low = (sums - high.astype(F32)).astype(BF)
        out = nt(hot, high) + nt(hot, low)
        gains = self.gain_grads[...].astype(BF)
        for s in range(8):
            self.small_out[s] = (out[16 * s:16 * s + 16] + nt(gains, self.spread(s))).astype(BF)

    def norm(self, src, dst, gain):
        g = self.gains[gain:gain + 1, :]
        @pl.loop(0, self.tokens // 64, unroll=4)
        def _(b):
            rows = pl.ds(b * 64, 64)
            v = src[rows, :].astype(F32)
            r = lax.rsqrt(jnp.mean(v * v, axis=-1, keepdims=True) + EPSILON)
            dst[rows, :] = (v * r * g).astype(BF)

    def norm_back(self, src, gain, store):
        g = self.gains[gain:gain + 1, :]
        @pl.loop(0, self.tokens // 64, unroll=4)
        def _(b):
            rows = pl.ds(b * 64, 64)
            v = src[rows, :].astype(F32)
            r = lax.rsqrt(jnp.mean(v * v, axis=-1, keepdims=True) + EPSILON)
            n = v * r
            dh = self.gn[rows, :]
            dg = dh * g
            self.gain_grads[gain:gain + 1, :] += jnp.sum(dh * n, axis=0, keepdims=True)
            store(rows, r * (dg - n * jnp.mean(dg * n, axis=-1, keepdims=True)))

    def wsq(self, w): return self.sq[w].reshape(SQ, SQ)
    def project(self, src, w, dst, first=0, last=3):
        @pl.loop(first, last, unroll=last - first)
        def _(n):
            cols = pl.ds(pl.multiple_of(n * 256, 256), 256)
            wt = self.sq[w, :, :, :, cols].reshape(SQ, 256)
            for t in range(self.trees):
                rows = pl.ds(t * TREE, TREE)
                dst[rows, cols] = nn(src[rows, :], wt).astype(BF)
    def project_add(self, src, w, base, dst):
        @pl.loop(0, 3, unroll=3)
        def _(n):
            cols = pl.ds(pl.multiple_of(n * 256, 256), 256)
            wt = self.sq[w, :, :, :, cols].reshape(SQ, 256)
            for t in range(self.trees):
                rows = pl.ds(t * TREE, TREE)
                dst[rows, cols] = base[rows, cols].astype(F32) + nn(src[rows, :], wt)
    def back(self, pairs, dst, dtype):
        @pl.loop(0, 2, unroll=2)
        def _(n):
            cols = pl.ds(pl.multiple_of(n * 384, 384), 384)
            for t in range(self.trees):
                rows = pl.ds(t * TREE, TREE)
                total = None
                for src, w in pairs:
                    part = nt(src[rows, :], self.sq[w, pl.ds(n * 2, 2)].reshape(384, SQ))
                    total = part if total is None else total + part
                dst[rows, cols] = total.astype(dtype)
    def weight_grad(self, left, right, w):
        @pl.loop(0, 2, unroll=2)
        def _(n):
            cols = pl.ds(pl.multiple_of(n * 384, 384), 384)
            lt = left[:, cols]
            for m in range(3):
                part = tn(lt, right[:, m * 256:(m + 1) * 256])
                self.sq[w, pl.ds(n * 2, 2), :, :, m * 256:(m + 1) * 256] = part.astype(BF).reshape(2, 2, 96, 256)

    def lanes(self):
        low = lax.broadcasted_iota(jnp.int32, (TREE, 128), 1) < DH
        return low, jnp.logical_not(low)
    def block(self, n):
        rows, cols = slice((n % 2) * TREE, (n % 2) * TREE + TREE), slice((n // 2) * TREE, (n // 2) * TREE + TREE)
        return self.gn.at[rows, cols]
    def attend(self, q, k, v, ctx, probs, masked, first, last):
        halves = self.lanes()
        @pl.loop(first * self.trees // 6, last * self.trees // 6)
        def _(n):
            def place(u):
                i = n * 3 + u
                t, p = i % self.trees, i // self.trees
                return t, p, pl.ds(pl.multiple_of(t * TREE, TREE), TREE), pl.ds(pl.multiple_of(p * 128, 128), 128)
            for u in range(3):
                t, p, rows, cols = place(u)
                qp, kp = q[rows, cols], k[rows, cols]
                if masked:
                    hot = self.hot[t]
                    kp = jnp.concatenate([kp, hot], axis=1)
                for e in range(2):
                    qe = jnp.where(halves[e], qp, jnp.zeros_like(qp))
                    if masked:
                        qe = jnp.concatenate([qe, nt(hot, self.toep[2 * p + e]).astype(BF)], axis=1)
                    self.block(2 * u + e)[...] = nt(kp, qe)
            for u in range(3):
                t, p, rows, cols = place(u)
                for e in range(2):
                    s = self.block(2 * u + e)[...]
                    if masked:
                        s = s + self.mask[t]
                    x = jnp.exp(s - jnp.max(s, axis=0, keepdims=True))
                    probs[t * H + 2 * p + e] = (x * (1.0 / jnp.sum(x, axis=0, keepdims=True))).astype(BF)
            for u in range(3):
                t, p, rows, cols = place(u)
                vt = v[rows, cols].T
                outs = [nn(vt[e * DH:(e + 1) * DH], probs[t * H + 2 * p + e]) for e in range(2)]
                ctx[rows, cols] = jnp.concatenate(outs, axis=0).astype(BF).T
    def attend_back(self, q, k, v, dctx, probs, masked, first, last):
        halves = self.lanes()
        @pl.loop(first * self.trees // 6, last * self.trees // 6)
        def _(n):
            def place(u):
                i = n * 3 + u
                t, p = i % self.trees, i // self.trees
                return t, p, pl.ds(pl.multiple_of(t * TREE, TREE), TREE), pl.ds(pl.multiple_of(p * 128, 128), 128)
            for u in range(3):
                t, p, rows, cols = place(u)
                vp, dp = v[rows, cols], dctx[rows, cols]
                dv = []
                for e in range(2):
                    self.block(2 * u + e)[...] = nt(vp, jnp.where(halves[e], dp, jnp.zeros_like(dp)))
                    dv.append(nn(probs[t * H + 2 * p + e], dp))
                v[rows, cols] = jnp.where(halves[0], dv[0], dv[1]).astype(BF)
            for u in range(3):
                t, p, rows, cols = place(u)
                for e in range(2):
                    g = self.block(2 * u + e)[...]
                    prf = probs[t * H + 2 * p + e].astype(F32)
                    ds = prf * (g - jnp.sum(g * prf, axis=0, keepdims=True))
                    probs[t * H + 2 * p + e] = ds.astype(BF)
            for u in range(3):
                t, p, rows, cols = place(u)
                qp, kt = q[rows, cols], k[rows, cols].T
                dq, dk = [], []
                for e in range(2):
                    ds = probs[t * H + 2 * p + e]
                    dq.append(nn(kt[e * DH:(e + 1) * DH], ds))
                    dk.append(nn(ds, qp))
                    if masked:
                        m = nn(nn(self.hot_t[t], ds).astype(BF), self.hot[t])
                        m = pltpu.roll(m, 1, 1, stride=1, stride_axis=0)
                        self.bias_grads[pl.ds(2 * p + e, 1), :] += jnp.sum(m, axis=0, keepdims=True)
                q[rows, cols] = jnp.concatenate(dq, axis=0).astype(BF).T
                k[rows, cols] = jnp.where(halves[0], dk[0], dk[1]).astype(BF)

    def feed_forward(self, m):
        base = pl.multiple_of(m * 512, 512)
        for hf in range(2):
            cols = pl.ds(pl.multiple_of(base + hf * 256, 256), 256)
            wg = self.gu[0, :, :, :, :, cols].reshape(SQ, 256)
            wu = self.gu[1, :, :, :, :, cols].reshape(SQ, 256)
            wd = self.dn[m, hf].reshape(256, SQ)
            here = slice(hf * 256, hf * 256 + 256)
            @pl.loop(0, self.trees, unroll=2)
            def _(t):
                rows = pl.ds(pl.multiple_of(t * TREE, TREE), TREE)
                x = self.nf[rows, :]
                g, u, gi = nn(x, wg), nn(x, wu), nt(self.dy[rows, :], wd)
                c = math.sqrt(2.0 / math.pi)
                th = jnp.tanh(c * (g + 0.044715 * (g * g * g)))
                half = 0.5 * (1.0 + th)
                gelu = g * half
                slope = half + 0.5 * g * (1.0 - th * th) * c * (1.0 + 3 * 0.044715 * (g * g))
                self.inner[rows, here] = (gelu * u).astype(BF)
                self.ggate[rows, here] = (gi * u * slope).astype(BF)
                self.gup[rows, here] = (gi * gelu).astype(BF)
        @pl.loop(0, 3, unroll=3)
        def _(n):
            cols = pl.ds(pl.multiple_of(n * 256, 256), 256)
            wd = self.dn[m, :, :, :, cols].reshape(512, 256)
            for t in range(self.trees):
                rows = pl.ds(t * TREE, TREE)
                self.oacc[rows, cols] += nn(self.inner[rows, :], wd)
        @pl.loop(0, 2, unroll=2)
        def _(n):
            cols = pl.ds(pl.multiple_of(n * 384, 384), 384)
            hid = pl.ds(base, 512)
            wg = self.gu[0, pl.ds(n * 2, 2), :, :, :, hid].reshape(384, 512)
            wu = self.gu[1, pl.ds(n * 2, 2), :, :, :, hid].reshape(384, 512)
            for t in range(self.trees):
                rows = pl.ds(t * TREE, TREE)
                self.gn[rows, cols] += nt(self.ggate[rows, :], wg) + nt(self.gup[rows, :], wu)
        @pl.loop(0, 2, unroll=2)
        def _(n):
            hid = pl.ds(base, 512)
            cols = pl.ds(pl.multiple_of(n * 384, 384), 384)
            lt = self.nf[:, cols]
            self.gu[0, pl.ds(n * 2, 2), :, :, :, hid] = tn(lt, self.ggate[...]).astype(BF).reshape(2, 2, 2, 48, 512)
            self.gu[1, pl.ds(n * 2, 2), :, :, :, hid] = tn(lt, self.gup[...]).astype(BF).reshape(2, 2, 2, 48, 512)
        @pl.loop(0, 3, unroll=3)
        def _(n):
            cols = pl.ds(pl.multiple_of(n * 256, 256), 256)
            self.dn[m, :, :, :, cols] = tn(self.inner[...], self.dy[:, cols]).astype(BF).reshape(2, 4, 64, 256)

    def start_ff(self):
        self.norm(self.after_cross, self.nf, 2)
        self.oacc[...] = self.after_cross[...]
        self.gn[...] = jnp.zeros_like(self.gn)
    def end_ff(self):
        self.stage[...] = self.oacc[...].astype(BF)
    def back_ff_norm(self):
        def store(rows, dv):
            total = self.dy[rows, :].astype(F32) + dv
            self.oacc[rows, :] = total
            self.gb[rows, :] = total.astype(BF)
        self.norm_back(self.after_cross, 2, store)
    def back_cross_a(self):
        self.weight_grad_after(self.cctx, self.gb, 7, self.cctx)
    def weight_grad_after(self, ctx, grad, w, dst):
        self.back([(grad, w)], self.stage, BF)
        self.weight_grad(ctx, grad, w)
        dst[...] = self.stage[...]
    def back_cross_norm(self):
        def store(rows, dv):
            total = self.oacc[rows, :] + dv
            self.oacc[rows, :] = total
            self.gb[rows, :] = total.astype(BF)
        self.norm_back(self.after_self, 1, store)
    def back_self_a(self):
        self.weight_grad_after(self.ctx, self.gb, 3, self.ctx)
    def back_self_norm(self):
        def store(rows, dv):
            self.gb[rows, :] = (self.oacc[rows, :] + dv).astype(BF)
        self.norm_back(self.hid, 0, store)

def layer_scratch(trees):
    T = trees * TREE
    V = pltpu.VMEM
    b = lambda: V((T, SQ), BF)
    f = lambda: V((T, SQ), F32)
    d = {k: b() for k in ("ns", "q", "k", "v", "ctx", "nc", "cq", "ck", "cv", "cctx", "nf", "gb", "stage")}
    d.update({k: f() for k in ("after_self", "after_cross", "oacc", "gn")})
    d.update(ps=V((trees * H, TREE, TREE), BF), pc=V((trees * H, TREE, TREE), BF),
             mask=V((trees, TREE, TREE), F32), hot=V((trees, TREE, DEPTHS), BF), hot_t=V((trees, DEPTHS, TREE), BF),
             toep=V((H, DEPTHS, DEPTHS), BF), gains=V((16, SQ), F32), gain_grads=V((16, SQ), F32),
             bias_grads=V((128, 128), F32), inner=V((T, 512), BF), ggate=V((T, 512), BF), gup=V((T, 512), BF))
    return d


MESH = pl.DeviceIdType.MESH
TEAM_R, TEAM_S = 4, 8
NZ = TEAM_S // 2


class Team:
    def __init__(self, shard_count):
        self.fold = shard_count // TEAM_S
        r = lax.axis_index("replica")
        s = lax.axis_index("shard")
        self.base_r = (r // TEAM_R) * TEAM_R
        self.q = r % TEAM_R
        self.off_s = s % self.fold
        self.s = s // self.fold
        self.z = self.s // 2
        self.c = self.s % 2
        self.qx = self.q + 1 - 2 * (self.q % 2)
        self.qy = self.q + 2 - 4 * (self.q // 2)
        self.qd = 3 - self.q
        self.sib = self.dev(self.q, self.z * 2 + 1 - self.c)
        self.nb = (self.dev(self.qx, self.s), self.dev(self.qy, self.s))
        self.diag = self.dev(self.qd, self.s)
        self.qn = (self.qx, self.qy)

    def dev(self, q, s):
        return (self.base_r + q, s * self.fold + self.off_s)

    def zdev(self, k):
        return self.dev(self.q, ((self.z + k) % NZ) * 2 + self.c)

    def zsrc(self, k):
        return (self.z + NZ - k) % NZ


def rcopy(src, dst, send_sem, recv_sem, device):
    return pltpu.make_async_remote_copy(
        src_ref=src, dst_ref=dst, send_sem=send_sem, recv_sem=recv_sem, device_id=device, device_id_type=MESH
    )


class Sender:
    def __init__(self, team):
        self.t = team
        self.sends = {}

    def go(self, src, dst, send_sem, recv_sem, device, key=0):
        cp = rcopy(src, dst, send_sem, recv_sem, device)
        cp.start()
        self.sends.setdefault(key, []).append(cp)

    def got(self, ref, sem):
        rcopy(ref, ref, sem, sem, self.t.sib).wait_recv()

    def sent(self, key=0):
        for cp in self.sends.pop(key, ()):
            cp.wait_send()


PHASES = (
    ("sq", 0, 0, 256), ("sq", 0, 256, 512), ("sq", 4, 0, SQ), ("gu", 0, 0, 1024), ("dn", 0, 0, SQ), ("gu", 0, 1024, 1024),
)
AHEAD = 1


class Gather(Sender):
    def __init__(self, team, bufs, sems):
        super().__init__(team)
        self.done = [0, 0, 0]
        self.sq, self.gu, self.dn = bufs
        (self.zs, self.zr, self.xs, self.xr, self.ys, self.yr, self.dxs, self.dxr, self.dys, self.dyr, self.cs, self.cr) = sems

    def piece(self, p, q, z, half=None):
        kind, first, col, n = PHASES[p]
        c = self.t.c
        lo = col if half is None else col + half * (n // 2)
        w = n if half is None else n // 2
        if kind == "sq":
            ref = self.sq.at[first + q, z, c]
        elif kind == "gu":
            ref = self.gu.at[q // 2, z, c, q % 2]
        else:
            ref = self.dn.at[z, c, q]
        return ref.at[:, pl.ds(lo, w)]

    def all_of(self, p, z, c):
        kind, first, col, n = PHASES[p]
        cols = pl.ds(col, n)
        if kind == "sq":
            return self.sq.at[pl.ds(first, 4), z, c, :, cols]
        if kind == "gu":
            return self.gu.at[:, z, c, :, :, cols]
        return self.dn.at[z, c, :, :, cols]

    def begin(self, p):
        t = self.t
        ref = self.piece(p, t.q, t.z)
        for k in range(1, NZ):
            self.go(ref, ref, self.zs.at[p, k], self.zr.at[p, k], t.zdev(k), p)
        own = self.all_of(p, t.z, t.c)
        self.go(own, own, self.cs.at[p, 0], self.cr.at[p], t.sib, p)

    def zstep(self, p, k):
        t = self.t
        ref = self.piece(p, t.q, t.zsrc(k))
        self.got(ref, self.zr.at[p, k])
        self.go(ref, ref, self.xs.at[p, k], self.xr.at[p, k], t.nb[0], p)
        self.go(ref, ref, self.ys.at[p, k], self.yr.at[p, k], t.nb[1], p)
        self.go(ref, ref, self.cs.at[p, 5 * k - 4], self.cr.at[p], t.sib, p)

    def xystep(self, p, k):
        t = self.t
        z = t.zsrc(k)
        ref = self.piece(p, t.qx, z)
        self.got(ref, self.xr.at[p, k])
        h = self.piece(p, t.qx, z, 0)
        self.go(h, h, self.dys.at[p, k], self.dyr.at[p, k], t.nb[1], p)
        self.go(ref, ref, self.cs.at[p, 5 * k - 3], self.cr.at[p], t.sib, p)
        ref = self.piece(p, t.qy, z)
        self.got(ref, self.yr.at[p, k])
        h = self.piece(p, t.qy, z, 1)
        self.go(h, h, self.dxs.at[p, k], self.dxr.at[p, k], t.nb[0], p)
        self.go(ref, ref, self.cs.at[p, 5 * k - 2], self.cr.at[p], t.sib, p)

    def dstep(self, p, k):
        t = self.t
        z = t.zsrc(k)
        for half, sem, i in ((0, self.dyr, 1), (1, self.dxr, 0)):
            h = self.piece(p, t.qd, z, half)
            self.got(h, sem.at[p, k])
            self.go(h, h, self.cs.at[p, 5 * k - i], self.cr.at[p], t.sib, p)

    def run(self, nz, nx, nd):
        for i in range(max(self.done[0], nz)):
            for step, (what, upto) in enumerate(((self.zstep, nz), (self.xystep, nx), (self.dstep, nd))):
                n = self.done[step]
                if n < upto:
                    p, k = n // (NZ - 1), n % (NZ - 1) + 1
                    what(p, k)
                    self.done[step] += 1
                    if step == 0 and k == 1 and p + AHEAD < len(PHASES):
                        self.begin(p + AHEAD)

    def whole(self, p):
        self.got(self.all_of(p, slice(None), 1 - self.t.c), self.cr.at[p])


CHUNKS = (
    ("gu", 0, 0, 48, 0, 512),
    ("gu", 0, 0, 48, 512, 512),
    ("gu", 0, 0, 48, 1024, 512),
    ("gu", 0, 0, 48, 1536, 512),
    ("dn", 0, 0, 64, 0, SQ),
    ("sq", 4, 0, 48, 0, SQ),
    ("sq", 4, 48, 48, 0, SQ),
    ("sq", 0, 0, 48, 0, SQ),
    ("sq", 0, 48, 48, 0, SQ),
)
ENTRY = (0, 2, 3, 4, 5, 7, 8, 10, 11)
KINDS = {"sq": 0, "gu": 1, "dn": 2}
ROWS = (96, 48, 64)
LAND = (SQ, 1536, SQ)
STAGES = 7


class Reduce(Sender):
    def __init__(self, team, bufs, rc, r1, r2, rz, fin, sems):
        super().__init__(team)
        self.sq, self.gu, self.dn = bufs
        self.rc, self.r1, self.r2, self.rz, self.fin = rc, r1, r2, rz, fin
        (self.s_c, self.r_c, self.s_1, self.r_1, self.s_2, self.r_2, self.s_z, self.r_z, self.s_f, self.r_f) = sems

    def rows(self, ch):
        return pl.ds(ch[2], ch[3])

    def cols(self, ch, h=None):
        if h is None:
            return pl.ds(ch[4], ch[5])
        return pl.ds(ch[4] + h * (ch[5] // 2), ch[5] // 2)

    def land(self, ch):
        return pl.ds((ch[4] % LAND[KINDS[ch[0]]]) // 2, ch[5] // 2)

    def spot(self, ch):
        return pl.ds(ch[4] % LAND[KINDS[ch[0]]], ch[5])

    def view(self, ch, q, z, c, h=None):
        kind, w = ch[0], ch[1]
        rows, cols = self.rows(ch), self.cols(ch, h)
        if kind == "sq":
            return self.sq.at[w + q, z, c, rows, cols]
        if kind == "gu":
            return self.gu.at[q // 2, z, c, q % 2, rows, cols]
        return self.dn.at[z, c, q, rows, cols]

    def half(self, ch, c):
        kind, w = ch[0], ch[1]
        rows, cols = self.rows(ch), self.cols(ch)
        if kind == "sq":
            return self.sq.at[pl.ds(w, 4), :, c, rows, cols]
        if kind == "gu":
            return self.gu.at[:, :, c, :, rows, cols]
        return self.dn.at[:, c, :, rows, cols]

    def from_core(self, ch, q=None, z=None):
        b = self.rc[KINDS[ch[0]]]
        rows, cols = self.rows(ch), self.spot(ch)
        if ch[0] == "sq":
            return b.at[:, :, rows, cols] if q is None else b.at[q, z, rows, cols]
        if ch[0] == "gu":
            return b.at[:, :, :, rows, cols] if q is None else b.at[q // 2, z, q % 2, rows, cols]
        return b.at[:, :, rows, cols] if q is None else b.at[z, q, rows, cols]

    def final(self, ch):
        return self.fin[0 if ch[1] == 0 else 1] if ch[0] == "sq" else self.fin[1 + KINDS[ch[0]]]

    def stage(self, st, i):
        t, ch = self.t, CHUNKS[i]
        q, z, c = t.q, t.z, t.c
        kd = KINDS[ch[0]]
        rows, land = self.rows(ch), self.land(ch)
        if st == 0:
            self.go(self.half(ch, 1 - c), self.from_core(ch), self.s_c.at[i], self.r_c.at[i], t.sib)
        elif st == 1:
            self.got(self.from_core(ch), self.r_c.at[i])

            @pl.loop(0, 4 * NZ)
            def _(j):
                a, b = self.view(ch, j // NZ, j % NZ, c), self.from_core(ch, j // NZ, j % NZ)
                a[...] = a[...] + b[...]

            for h in range(2):
                for m, qq in enumerate((t.qn[h], t.qd)):
                    slot = (qq // 2) if h == 0 else (qq % 2)
                    self.go(
                        self.view(ch, qq, slice(None), c, h), self.r1[kd].at[h, slot, :, rows, land],
                        self.s_1.at[i, h, m], self.r_1.at[i, h, m], t.nb[h],
                    )
        elif st == 2:
            for h in range(2):
                for m, qq in ((1, t.qn[1 - h]), (0, q)):
                    slot = (qq // 2) if h == 0 else (qq % 2)
                    self.got(self.r1[kd].at[h, slot, :, rows, land], self.r_1.at[i, h, m])

                    @pl.loop(0, NZ)
                    def _(j):
                        a = self.view(ch, qq, j, c, h)
                        a[...] = a[...] + self.r1[kd][h, slot, j, rows, land]

            for h in range(2):
                self.go(
                    self.view(ch, t.qn[1 - h], slice(None), c, h), self.r2[kd].at[h, :, rows, land],
                    self.s_2.at[i, h], self.r_2.at[i, h], t.nb[1 - h],
                )
        elif st == 3:
            for h in range(2):
                self.got(self.r2[kd].at[h, :, rows, land], self.r_2.at[i, h])

                @pl.loop(0, NZ)
                def _(j):
                    a = self.view(ch, q, j, c, h)
                    a[...] = a[...] + self.r2[kd][h, j, rows, land]

            for k in range(1, NZ):
                self.go(
                    self.view(ch, q, (z + k) % NZ, c), self.rz[kd].at[k - 1, rows, self.spot(ch)],
                    self.s_z.at[i, k], self.r_z.at[i, k], t.zdev(k),
                )
        elif st == 4:
            v = self.view(ch, q, z, c)[...].astype(F32)
            for k in range(1, NZ):
                self.got(self.rz[kd].at[k - 1, rows, self.spot(ch)], self.r_z.at[i, k])
                v = v + self.rz[kd][k - 1, rows, self.spot(ch)].astype(F32)
            f = self.final(ch).at[q, rows, self.cols(ch)]
            f[...] = v.astype(BF)
            for h in range(2):
                self.go(f, f, self.s_f.at[i, h], self.r_f.at[i, h], t.nb[h])
        elif st == 5:
            for h in range(2):
                self.got(self.final(ch).at[t.qn[h], rows, self.cols(ch)], self.r_f.at[i, h])
                f = self.final(ch).at[t.qn[h], rows, self.cols(ch, h)]
                self.go(f, f, self.s_f.at[i, 2 + h], self.r_f.at[i, 2 + h], t.nb[1 - h])
        else:
            for h in range(2):
                self.got(self.final(ch).at[t.qd, rows, self.cols(ch, h)], self.r_f.at[i, 2 + h])

    def tick(self, n):
        for st in (1, 0, 6, 5, 4, 3, 2):
            for i, entry in enumerate(ENTRY):
                if n - entry == st:
                    self.stage(st, i)


def layer_kernel(names, shards, trees, *refs):
    seg_start, seg_parent, bucket, *gains_in, bias_in, hid_in, enc_in, dy_in = refs[:10]
    weights = refs[10:21]
    lo, gh, ge, f0, f1, f2, f3, small_fin = refs[21:29]
    r = dict(zip(names, refs[29:]))
    bufs = (r["sq"], r["gu"], r["dn"])
    t = Team(shards)
    L = Layer(dict(r, seg_start=seg_start, seg_parent=seg_parent, bucket=bucket), trees)
    G = Gather(t, bufs, [r["g%d" % i] for i in range(12)])
    R = Reduce(
        t, bufs, [r["rc0"], r["rc1"], r["rc2"]], [r["ra0"], r["ra1"], r["ra2"]], [r["rb0"], r["rb1"], r["rb2"]],
        [r["rz0"], r["rz1"], r["rz2"]], (f0, f1, f2, f3), [r["r%d" % i] for i in range(10)],
    )
    S = Sender(t)

    loc, lsem = [], r["local"]

    def fetch(src, dst):
        cp = pltpu.make_async_copy(src, dst, lsem.at[len(loc)])
        cp.start()
        loc.append(cp)

    z, c = t.z, t.c
    for i in range(8):
        fetch(weights[i], r["sq"].at[i, z, c])
    for i in range(2):
        for h in range(2):
            fetch(weights[8 + i].at[pl.ds(h * 48, 48)], r["gu"].at[i, z, c, h])
    for h in range(4):
        fetch(weights[10].at[pl.ds(h * 64, 64)], r["dn"].at[z, c, h])
    fetch(hid_in, r["hid"])
    fetch(enc_in, r["enc"])
    fetch(dy_in, r["dy"])

    others = [t.dev(t.q, (t.s + k) % TEAM_S) for k in range(1, TEAM_S)]
    greet = others + list(t.nb) + [t.diag]
    barrier = pltpu.get_barrier_semaphore()
    for d in greet:
        pl.semaphore_signal(barrier, inc=1, device_id=d, device_id_type=MESH)
    pl.semaphore_wait(barrier, len(greet))
    for cp in loc:
        cp.wait()

    small, mix = r["small"], r["mix"]
    mix[...] = jnp.zeros_like(mix)
    for i in range(3):
        mix[i:i + 1, :96] = gains_in[i][...].astype(F32)
    mix[4:8, :H] = bias_in[...].astype(F32)
    small[t.s] = mix[...].astype(BF)
    for k in range(1, TEAM_S):
        S.go(small.at[t.s], small.at[t.s], r["ss"].at[0, k], r["sr"].at[0, k], others[k - 1])
    for p in range(AHEAD):
        G.begin(p)
    L.layout()
    G.run(1, 0, 0)
    for k in range(1, TEAM_S):
        S.got(small.at[(t.s + TEAM_S - k) % TEAM_S], r["sr"].at[0, k])
    L.small_params()
    G.run(2, 1, 0)
    L.norm(r["hid"], r["ns"], 0)
    G.run(3, 2, 1)
    G.run(4, 3, 2)
    G.run(5, 4, 3)
    own = (r["q"], r["k"], r["v"], r["ctx"], r["ps"], True)
    cross = (r["cq"], r["ck"], r["cv"], r["cctx"], r["pc"], False)
    G.whole(0)
    for w in range(3):
        L.project(r["ns"], w, own[w], 0, 1)
    G.run(6, 5, 4)
    L.attend(*own, 0, 3)
    G.run(7, 6, 5)
    G.run(8, 7, 6)
    G.run(9, 7, 6)
    G.whole(1)
    for w in range(3):
        L.project(r["ns"], w, own[w], 1, 3)
    L.attend(*own, 3, 6)
    G.run(10, 8, 6)
    L.attend(*own, 6, 12)
    G.run(11, 9, 7)
    L.project_add(r["ctx"], 3, r["hid"], r["after_self"])
    L.norm(r["after_self"], r["nc"], 1)
    G.run(12, 10, 8)
    G.run(13, 11, 9)
    G.whole(2)
    for w, src in enumerate((r["nc"], r["enc"], r["enc"])):
        L.project(src, 4 + w, cross[w])
    G.run(14, 12, 10)
    L.attend(*cross, 0, 6)
    G.run(15, 13, 11)
    L.attend(*cross, 6, 12)
    G.run(16, 14, 12)
    L.project_add(r["cctx"], 7, r["after_self"], r["after_cross"])
    L.start_ff()
    G.run(17, 15, 13)
    G.run(18, 16, 14)
    G.run(18, 17, 15)
    for p in (3, 4):
        G.whole(p)
        G.sent(p)

    L.feed_forward(0)
    G.run(18, 18, 17)
    R.tick(0)
    G.run(18, 18, 18)
    R.tick(1)
    L.feed_forward(1)
    R.tick(2)
    G.whole(5)
    for p in (5, 0, 1, 2):
        G.sent(p)
    S.sent()
    for m in (2, 3):
        L.feed_forward(m)
        R.tick(m + 1)
    L.end_ff()
    out0 = pltpu.make_async_copy(r["stage"], lo, lsem.at[0])
    out0.start()
    L.back_ff_norm()
    out0.wait()
    L.back_cross_a()
    R.tick(5)
    L.attend_back(*cross, 0, 6)
    R.tick(6)
    L.attend_back(*cross, 6, 12)
    L.back([(r["ck"], 5), (r["cv"], 6)], r["stage"], BF)
    out1 = pltpu.make_async_copy(r["stage"], ge, lsem.at[1])
    out1.start()
    L.back([(r["cq"], 4)], r["gn"], F32)
    L.weight_grad(r["nc"], r["cq"], 4)
    L.weight_grad(r["enc"], r["ck"], 5)
    L.weight_grad(r["enc"], r["cv"], 6)
    R.tick(7)
    L.back_cross_norm()
    out1.wait()
    L.back_self_a()
    L.attend_back(*own, 0, 3)
    R.tick(8)
    L.attend_back(*own, 3, 9)
    R.tick(9)
    L.attend_back(*own, 9, 12)
    L.back([(r["q"], 0), (r["k"], 1), (r["v"], 2)], r["gn"], F32)
    L.weight_grad(r["ns"], r["q"], 0)
    L.weight_grad(r["ns"], r["k"], 1)
    L.weight_grad(r["ns"], r["v"], 2)
    R.tick(10)
    L.back_self_norm()
    out2 = pltpu.make_async_copy(r["gb"], gh, lsem.at[2])
    out2.start()
    L.small_grads()
    so, sa, sb = r["small_out"], r["small_a"], r["small_b"]
    for k in range(1, TEAM_S):
        S.go(so.at[(t.s + k) % TEAM_S], sa.at[t.s], r["ss"].at[1, k], r["sr"].at[1, k], others[k - 1])
    sa[t.s] = so[t.s]
    R.tick(11)
    for k in range(1, TEAM_S):
        S.got(sa.at[(t.s + TEAM_S - k) % TEAM_S], r["sr"].at[1, k])
    sb[t.q] = jnp.sum(sa[...].astype(F32), axis=0).astype(BF)
    for k, (qq, d) in enumerate(((t.qx, t.nb[0]), (t.qy, t.nb[1]), (t.qd, t.diag))):
        S.go(sb.at[t.q], sb.at[t.q], r["ss"].at[2, k], r["sr"].at[2, k], d)
    last = max(ENTRY) + STAGES
    R.tick(12)
    for k, qq in enumerate((t.qx, t.qy, t.qd)):
        S.got(sb.at[qq], r["sr"].at[2, k])
    small_fin[...] = jnp.sum(sb[...].astype(F32), axis=0)
    for n in range(13, last):
        R.tick(n)
    R.sent()
    S.sent()
    out2.wait()


def layer(seg_start, seg_parent, bucket, gains, bias, hid, enc, dy, weights, shards):
    trees = seg_start.shape[0]
    tokens = trees * TREE
    V, D = pltpu.VMEM, pltpu.SemaphoreType.DMA
    act = lambda: V((tokens, SQ), BF)
    n, p = len(CHUNKS), len(PHASES)
    scratch = dict(
        sq=V((8, NZ, 2, 96, SQ), BF), gu=V((2, NZ, 2, 2, 48, FFN), BF), dn=V((NZ, 2, 4, 64, SQ), BF),
        rc0=V((4, NZ, 96, SQ), BF), rc1=V((2, NZ, 2, 48, LAND[1]), BF), rc2=V((NZ, 4, 64, SQ), BF),
        hid=act(), enc=act(), dy=act(), local=D((20,)),
        small=V((8, 16, 128), BF), small_out=V((8, 16, 128), BF), small_a=V((8, 16, 128), BF), small_b=V((4, 16, 128), BF),
        ss=D((3, 8)), sr=D((3, 8)), mix=V((16, 128), F32),
    )
    for i in range(3):
        scratch["ra%d" % i] = V((2, 2, NZ, ROWS[i], LAND[i] // 2), BF)
        scratch["rb%d" % i] = V((2, NZ, ROWS[i], LAND[i] // 2), BF)
        scratch["rz%d" % i] = V((NZ - 1, ROWS[i], LAND[i]), BF)
    for i in range(12):
        scratch["g%d" % i] = D((p, 16)) if i == 10 else D((p,)) if i == 11 else D((p, NZ))
    for i, shape in enumerate([(n,), (n,), (n, 2, 2), (n, 2, 2), (n, 2), (n, 2), (n, NZ), (n, NZ), (n, 4), (n, 4)]):
        scratch["r%d" % i] = D(shape)
    scratch.update(layer_scratch(trees))
    hbm, vmem, smem = (pl.BlockSpec(memory_space=m) for m in (pltpu.HBM, pltpu.VMEM, pltpu.SMEM))
    sd = jax.ShapeDtypeStruct
    return pl.pallas_call(
        functools.partial(layer_kernel, list(scratch), shards, trees),
        out_shape=[sd((tokens, SQ), BF)] * 3
        + [sd((4, 96, SQ), BF), sd((4, 96, SQ), BF), sd((4, 48, FFN), BF), sd((4, 64, SQ), BF), sd((16, 128), F32)],
        in_specs=[smem, smem] + [vmem] * 5 + [hbm] * 14,
        out_specs=[hbm] * 3 + [vmem] * 5,
        scratch_shapes=list(scratch.values()),
        compiler_params=pltpu.CompilerParams(collective_id=0, has_side_effects=True, vmem_limit_bytes=64 * 2**20 - 65536),
        name="decoder_layer",
    )(seg_start, seg_parent, bucket, *gains, bias, hid, enc, dy, *weights)


def finish_kernel(lo, gh, ge, f0, f1, f2, f3, small, *refs):
    o_lo, o_gh, o_ge = refs[:3]
    squares, gate, up, down = refs[3:11], refs[11], refs[12], refs[13]
    norms, table = refs[14:17], refs[17]
    a0, a1, a2, b0, b1, b2, b3, w0, w1, w2, w3, sem_in, sem_out = refs[18:]
    pairs = ((f0, b0), (f1, b1), (f2, b2), (f3, b3), (lo, a0), (gh, a1), (ge, a2))
    ins = [pltpu.make_async_copy(a, b, sem_in.at[i]) for i, (a, b) in enumerate(pairs)]
    for cp in ins:
        cp.start()
    for i in range(3):
        norms[i][...] = small[i:i + 1, :96]
    table[...] = small[4:8, :H]
    outs = []

    def out(src, dst):
        cp = pltpu.make_async_copy(src, dst, sem_out.at[len(outs)])
        cp.start()
        outs.append(cp)

    for n, (b, w) in enumerate(((b0, w0), (b1, w1))):
        ins[n].wait()
        for i in range(4):
            w[i] = b[i].astype(F32)
            out(w.at[i], squares[4 * n + i])
    ins[2].wait()
    for i, dst in enumerate((gate, up)):
        w2[i] = b2[2 * i:2 * i + 2].reshape(96, FFN).astype(F32)
        out(w2.at[i], dst)
    ins[3].wait()
    w3[...] = b3[...].reshape(256, SQ).astype(F32)
    out(w3, down)
    for i, dst in enumerate((o_lo, o_gh, o_ge)):
        ins[4 + i].wait()
        out((a0, a1, a2)[i], dst)
    for cp in outs:
        cp.wait()


def finish(outs):
    hbm, vmem = pl.BlockSpec(memory_space=pltpu.HBM), pl.BlockSpec(memory_space=pltpu.VMEM)
    V, sd = pltpu.VMEM, jax.ShapeDtypeStruct
    res = pl.pallas_call(
        finish_kernel,
        out_shape=[sd(o.shape, BF) for o in outs[:3]] + [sd((96, SQ), F32)] * 8 + [sd((96, FFN), F32)] * 2
        + [sd((256, SQ), F32)] + [sd((1, 96), F32)] * 3 + [sd((4, H), F32)],
        in_specs=[hbm] * 7 + [vmem],
        out_specs=[hbm] * 14 + [vmem] * 4,
        scratch_shapes=[V(o.shape, BF) for o in outs[:7]]
        + [V((4, 96, SQ), F32), V((4, 96, SQ), F32), V((2, 96, FFN), F32), V((256, SQ), F32)]
        + [pltpu.SemaphoreType.DMA((7,)), pltpu.SemaphoreType.DMA((14,))],
        compiler_params=pltpu.CompilerParams(vmem_limit_bytes=63 * 2**20),
        name="finish",
    )(*outs)
    return (*res[:3], res[3:11], res[11], res[12], res[13], res[14:17], res[17])


def team_rows(weight, fold):
    if fold == 1:
        return weight
    groups = [[a * fold + b for b in range(fold)] for a in range(TEAM_S)]
    return lax.all_gather(weight, "shard", axis=0, tiled=True, axis_index_groups=groups)


def team_sum(grad, fold, teams_r):
    if fold > 1:
        groups = [[a * fold + b for b in range(fold)] for a in range(TEAM_S)]
        grad = lax.psum_scatter(grad, "shard", scatter_dimension=0, tiled=True, axis_index_groups=groups)
    if teams_r > 1:
        groups = [[a * TEAM_R + b for a in range(teams_r)] for b in range(TEAM_R)]
        grad = lax.psum(grad, "replica", axis_index_groups=groups)
    return grad


def body(
    replicas, shards,
    hidden, encoded, out_grad, seg_start, seg_parent, bucket_of_distance,
    norm_self, self_query, self_key, self_value, self_out, rel_bias,
    norm_cross, cross_query, cross_key, cross_value, cross_out,
    norm_ff, ff_gate, ff_up, ff_down,
):
    fold, teams_r = shards // TEAM_S, replicas // TEAM_R
    big = (self_query, self_key, self_value, self_out, cross_query, cross_key, cross_value, cross_out, ff_gate, ff_up, ff_down)
    flat = lambda v: v.reshape(-1, v.shape[-1])
    outs = layer(
        flat(seg_start), flat(seg_parent), bucket_of_distance.reshape(2, 128),
        [team_rows(g, fold).reshape(1, -1) for g in (norm_self, norm_cross, norm_ff)], team_rows(rel_bias, fold),
        flat(hidden), flat(encoded), flat(out_grad), [team_rows(w, fold) for w in big], shards,
    )
    lo, gh, ge, squares, gate, up, down, norms, table = finish(outs)
    squares = [team_sum(v, fold, teams_r) for v in squares]
    gate, up, down, table = (team_sum(v, fold, teams_r) for v in (gate, up, down, table))
    norms = [team_sum(v.reshape(-1), fold, teams_r) for v in norms]
    lo, gh, ge = (v.reshape(hidden.shape) for v in (lo, gh, ge))
    return (
        lo, gh, ge, norms[0], *squares[:4], table, norms[1], *squares[4:], norms[2], gate, up, down,
    )


def solution(mesh):
    placed = (
        P(None, ("replica", "shard"), None, None),
        P(None, ("replica", "shard"), None, None),
        P(None, ("replica", "shard"), None, None),
        P(None, ("replica", "shard"), None),
        P(None, ("replica", "shard"), None),
        P(),
        P("shard"),
        P("shard", None),
        P("shard", None),
        P("shard", None),
        P("shard", None),
        P("shard", None),
        P("shard"),
        P("shard", None),
        P("shard", None),
        P("shard", None),
        P("shard", None),
        P("shard"),
        P("shard", None),
        P("shard", None),
        P("shard", None),
    )
    return jax.shard_map(
        functools.partial(body, mesh.shape["replica"], mesh.shape["shard"]),
        mesh=mesh,
        in_specs=placed,
        out_specs=(
            P(None, ("replica", "shard"), None, None),
            P(None, ("replica", "shard"), None, None),
            P(None, ("replica", "shard"), None, None),
            P("shard"),
            P("shard", None),
            P("shard", None),
            P("shard", None),
            P("shard", None),
            P("shard", None),
            P("shard"),
            P("shard", None),
            P("shard", None),
            P("shard", None),
            P("shard", None),
            P("shard"),
            P("shard", None),
            P("shard", None),
            P("shard", None),
        ),
        check_vma=False,
    )
```

```python
import functools
import math

import jax
import jax.numpy as jnp
from jax import lax
from jax.experimental import pallas as pl
from jax.experimental.pallas import tpu as pltpu
from jax.sharding import PartitionSpec as P

SQ, FFN, H, DH, TREE, NSEG, NB = 768, 2048, 12, 64, 256, 13, 32
TRUNK, BRANCH, LEAF = 64, 16, 16
BF, F32 = jnp.bfloat16, jnp.float32
EPSILON, NEGATIVE = 1e-6, -1e9
DEPTHS = 128
SEG_LEN = (TRUNK,) + (BRANCH,) * 4 + (LEAF,) * 8
SEG_DEPTH = (0,) + (TRUNK,) * 4 + (TRUNK + BRANCH,) * 8

def nn(a, b): return lax.dot_general(a, b, (((1,), (0,)), ((), ())), preferred_element_type=F32)
def nt(a, b): return lax.dot_general(a, b, (((1,), (1,)), ((), ())), preferred_element_type=F32)
def tn(a, b): return lax.dot_general(a, b, (((0,), (0,)), ((), ())), preferred_element_type=F32)

class Layer:
    def __init__(self, refs, trees):
        self.__dict__.update(refs)
        self.trees = trees
        self.tokens = trees * TREE

    def layout(self):
        for t in range(self.trees):
            def place(shape, axis):
                pos = lax.broadcasted_iota(jnp.int32, shape, axis)
                dep, sid, pid, gid = pos, jnp.zeros_like(pos), jnp.zeros_like(pos), jnp.zeros_like(pos)
                for s in range(NSEG):
                    at = self.seg_start[t, s]
                    inside = (pos >= at) & (pos < at + SEG_LEN[s])
                    dep = dep + jnp.where(inside, SEG_DEPTH[s] - at, 0)
                    sid = jnp.where(inside, s, sid)
                    pid = jnp.where(inside, self.seg_parent[t, s], pid)
                    gid = jnp.where(inside, self.seg_parent[t, self.seg_parent[t, s]], gid)
                return dep, sid, pid, gid
            dep_j, sid_j, _, _ = place((TREE, 1), 0)
            dep_i, sid_i, pid_i, gid_i = place((1, TREE), 1)
            ok = ((sid_j == sid_i) | (sid_j == pid_i) | (sid_j == gid_i)) & (dep_j <= dep_i)
            self.mask[t] = jnp.where(ok, 0.0, NEGATIVE).astype(F32)
            lanes = lax.broadcasted_iota(jnp.int32, (TREE, DEPTHS), 1)
            self.hot[t] = jnp.where(lanes == dep_j, 1.0, 0.0).astype(BF)
            rows = lax.broadcasted_iota(jnp.int32, (DEPTHS, TREE), 0)
            self.hot_t[t] = jnp.where(rows == DEPTHS - 1 - dep_i, 1.0, 0.0).astype(BF)

    def bucket_hot(self):
        row = lax.broadcasted_iota(jnp.int32, (128, DEPTHS), 0)
        inner = row % 16
        bucket = jnp.where((inner >= 4) & (inner < 8), 4 * (row // 16) + inner - 4, -1)
        return jnp.where(self.bucket[...][:1] == bucket, 1.0, 0.0).astype(BF)

    def spread(self, s):
        i = lax.broadcasted_iota(jnp.int32, (128, SQ), 0)
        j = lax.broadcasted_iota(jnp.int32, (128, SQ), 1)
        return jnp.where((j == i + 96 * s) & (i < 96), 1.0, 0.0).astype(BF)

    def small_params(self):
        total = jnp.zeros((16, SQ), F32)
        for s in range(8):
            total = total + nn(self.small[s], self.spread(s))
        self.gains[...] = total
        table = tn(self.small[...].reshape(128, 128), self.bucket_hot())
        for h in range(H):
            row = jnp.broadcast_to(table[h:h + 1], (DEPTHS, DEPTHS))
            self.toep[h] = pltpu.roll(row, 0, 1, stride=1, stride_axis=0).astype(BF)
        self.gain_grads[...] = jnp.zeros_like(self.gain_grads)
        self.bias_grads[...] = jnp.zeros_like(self.bias_grads)

    def small_grads(self):
        hot = self.bucket_hot()
        sums = self.bias_grads[...]
        high = sums.astype(BF)
        low = (sums - high.astype(F32)).astype(BF)
        out = nt(hot, high) + nt(hot, low)
        gains = self.gain_grads[...].astype(BF)
        for s in range(8):
            self.small_out[s] = (out[16 * s:16 * s + 16] + nt(gains, self.spread(s))).astype(BF)

    def norm(self, src, dst, gain):
        g = self.gains[gain:gain + 1, :]
        @pl.loop(0, self.tokens // 64, unroll=4)
        def _(b):
            rows = pl.ds(b * 64, 64)
            v = src[rows, :].astype(F32)
            r = lax.rsqrt(jnp.mean(v * v, axis=-1, keepdims=True) + EPSILON)
            dst[rows, :] = (v * r * g).astype(BF)

    def norm_back(self, src, gain, store):
        g = self.gains[gain:gain + 1, :]
        @pl.loop(0, self.tokens // 64, unroll=4)
        def _(b):
            rows = pl.ds(b * 64, 64)
            v = src[rows, :].astype(F32)
            r = lax.rsqrt(jnp.mean(v * v, axis=-1, keepdims=True) + EPSILON)
            n = v * r
            dh = self.gn[rows, :]
            dg = dh * g
            self.gain_grads[gain:gain + 1, :] += jnp.sum(dh * n, axis=0, keepdims=True)
            store(rows, r * (dg - n * jnp.mean(dg * n, axis=-1, keepdims=True)))

    def wsq(self, w): return self.sq[w].reshape(SQ, SQ)
    def project(self, src, w, dst, first=0, last=3):
        @pl.loop(first, last, unroll=last - first)
        def _(n):
            cols = pl.ds(pl.multiple_of(n * 256, 256), 256)
            wt = self.sq[w, :, :, :, cols].reshape(SQ, 256)
            for t in range(self.trees):
                rows = pl.ds(t * TREE, TREE)
                dst[rows, cols] = nn(src[rows, :], wt).astype(BF)
    def project_add(self, src, w, base, dst):
        @pl.loop(0, 3, unroll=3)
        def _(n):
            cols = pl.ds(pl.multiple_of(n * 256, 256), 256)
            wt = self.sq[w, :, :, :, cols].reshape(SQ, 256)
            for t in range(self.trees):
                rows = pl.ds(t * TREE, TREE)
                dst[rows, cols] = base[rows, cols].astype(F32) + nn(src[rows, :], wt)
    def back(self, pairs, dst, dtype):
        @pl.loop(0, 2, unroll=2)
        def _(n):
            cols = pl.ds(pl.multiple_of(n * 384, 384), 384)
            for t in range(self.trees):
                rows = pl.ds(t * TREE, TREE)
                total = None
                for src, w in pairs:
                    part = nt(src[rows, :], self.sq[w, pl.ds(n * 2, 2)].reshape(384, SQ))
                    total = part if total is None else total + part
                dst[rows, cols] = total.astype(dtype)
    def weight_grad(self, left, right, w):
        @pl.loop(0, 2, unroll=2)
        def _(n):
            cols = pl.ds(pl.multiple_of(n * 384, 384), 384)
            lt = left[:, cols]
            for m in range(3):
                part = tn(lt, right[:, m * 256:(m + 1) * 256])
                self.sq[w, pl.ds(n * 2, 2), :, :, m * 256:(m + 1) * 256] = part.astype(BF).reshape(2, 2, 96, 256)

    def lanes(self):
        low = lax.broadcasted_iota(jnp.int32, (TREE, 128), 1) < DH
        return low, jnp.logical_not(low)
    def block(self, n):
        rows, cols = slice((n % 2) * TREE, (n % 2) * TREE + TREE), slice((n // 2) * TREE, (n // 2) * TREE + TREE)
        return self.gn.at[rows, cols]
    def attend(self, q, k, v, ctx, probs, masked, first, last):
        halves = self.lanes()
        @pl.loop(first * self.trees // 6, last * self.trees // 6)
        def _(n):
            def place(u):
                i = n * 3 + u
                t, p = i % self.trees, i // self.trees
                return t, p, pl.ds(pl.multiple_of(t * TREE, TREE), TREE), pl.ds(pl.multiple_of(p * 128, 128), 128)
            for u in range(3):
                t, p, rows, cols = place(u)
                qp, kp = q[rows, cols], k[rows, cols]
                if masked:
                    hot = self.hot[t]
                    kp = jnp.concatenate([kp, hot], axis=1)
                for e in range(2):
                    qe = jnp.where(halves[e], qp, jnp.zeros_like(qp))
                    if masked:
                        qe = jnp.concatenate([qe, nt(hot, self.toep[2 * p + e]).astype(BF)], axis=1)
                    self.block(2 * u + e)[...] = nt(kp, qe)
            for u in range(3):
                t, p, rows, cols = place(u)
                for e in range(2):
                    s = self.block(2 * u + e)[...]
                    if masked:
                        s = s + self.mask[t]
                    x = jnp.exp(s - jnp.max(s, axis=0, keepdims=True))
                    probs[t * H + 2 * p + e] = (x * (1.0 / jnp.sum(x, axis=0, keepdims=True))).astype(BF)
            for u in range(3):
                t, p, rows, cols = place(u)
                vt = v[rows, cols].T
                outs = [nn(vt[e * DH:(e + 1) * DH], probs[t * H + 2 * p + e]) for e in range(2)]
                ctx[rows, cols] = jnp.concatenate(outs, axis=0).astype(BF).T
    def attend_back(self, q, k, v, dctx, probs, masked, first, last):
        halves = self.lanes()
        @pl.loop(first * self.trees // 6, last * self.trees // 6)
        def _(n):
            def place(u):
                i = n * 3 + u
                t, p = i % self.trees, i // self.trees
                return t, p, pl.ds(pl.multiple_of(t * TREE, TREE), TREE), pl.ds(pl.multiple_of(p * 128, 128), 128)
            for u in range(3):
                t, p, rows, cols = place(u)
                vp, dp = v[rows, cols], dctx[rows, cols]
                dv = []
                for e in range(2):
                    self.block(2 * u + e)[...] = nt(vp, jnp.where(halves[e], dp, jnp.zeros_like(dp)))
                    dv.append(nn(probs[t * H + 2 * p + e], dp))
                v[rows, cols] = jnp.where(halves[0], dv[0], dv[1]).astype(BF)
            for u in range(3):
                t, p, rows, cols = place(u)
                for e in range(2):
                    g = self.block(2 * u + e)[...]
                    prf = probs[t * H + 2 * p + e].astype(F32)
                    ds = prf * (g - jnp.sum(g * prf, axis=0, keepdims=True))
                    probs[t * H + 2 * p + e] = ds.astype(BF)
            for u in range(3):
                t, p, rows, cols = place(u)
                qp, kt = q[rows, cols], k[rows, cols].T
                dq, dk = [], []
                for e in range(2):
                    ds = probs[t * H + 2 * p + e]
                    dq.append(nn(kt[e * DH:(e + 1) * DH], ds))
                    dk.append(nn(ds, qp))
                    if masked:
                        m = nn(nn(self.hot_t[t], ds).astype(BF), self.hot[t])
                        m = pltpu.roll(m, 1, 1, stride=1, stride_axis=0)
                        self.bias_grads[pl.ds(2 * p + e, 1), :] += jnp.sum(m, axis=0, keepdims=True)
                q[rows, cols] = jnp.concatenate(dq, axis=0).astype(BF).T
                k[rows, cols] = jnp.where(halves[0], dk[0], dk[1]).astype(BF)

    def feed_forward(self, m):
        base = pl.multiple_of(m * 512, 512)
        for hf in range(2):
            cols = pl.ds(pl.multiple_of(base + hf * 256, 256), 256)
            wg = self.gu[0, :, :, :, :, cols].reshape(SQ, 256)
            wu = self.gu[1, :, :, :, :, cols].reshape(SQ, 256)
            wd = self.dn[m, hf].reshape(256, SQ)
            here = slice(hf * 256, hf * 256 + 256)
            @pl.loop(0, self.trees, unroll=2)
            def _(t):
                rows = pl.ds(pl.multiple_of(t * TREE, TREE), TREE)
                x = self.nf[rows, :]
                g, u, gi = nn(x, wg), nn(x, wu), nt(self.dy[rows, :], wd)
                c = math.sqrt(2.0 / math.pi)
                th = jnp.tanh(c * (g + 0.044715 * (g * g * g)))
                half = 0.5 * (1.0 + th)
                gelu = g * half
                slope = half + 0.5 * g * (1.0 - th * th) * c * (1.0 + 3 * 0.044715 * (g * g))
                self.inner[rows, here] = (gelu * u).astype(BF)
                self.ggate[rows, here] = (gi * u * slope).astype(BF)
                self.gup[rows, here] = (gi * gelu).astype(BF)
        @pl.loop(0, 3, unroll=3)
        def _(n):
            cols = pl.ds(pl.multiple_of(n * 256, 256), 256)
            wd = self.dn[m, :, :, :, cols].reshape(512, 256)
            for t in range(self.trees):
                rows = pl.ds(t * TREE, TREE)
                self.oacc[rows, cols] += nn(self.inner[rows, :], wd)
        @pl.loop(0, 2, unroll=2)
        def _(n):
            cols = pl.ds(pl.multiple_of(n * 384, 384), 384)
            hid = pl.ds(base, 512)
            wg = self.gu[0, pl.ds(n * 2, 2), :, :, :, hid].reshape(384, 512)
            wu = self.gu[1, pl.ds(n * 2, 2), :, :, :, hid].reshape(384, 512)
            for t in range(self.trees):
                rows = pl.ds(t * TREE, TREE)
                self.gn[rows, cols] += nt(self.ggate[rows, :], wg) + nt(self.gup[rows, :], wu)
        @pl.loop(0, 2, unroll=2)
        def _(n):
            hid = pl.ds(base, 512)
            cols = pl.ds(pl.multiple_of(n * 384, 384), 384)
            lt = self.nf[:, cols]
            self.gu[0, pl.ds(n * 2, 2), :, :, :, hid] = tn(lt, self.ggate[...]).astype(BF).reshape(2, 2, 2, 48, 512)
            self.gu[1, pl.ds(n * 2, 2), :, :, :, hid] = tn(lt, self.gup[...]).astype(BF).reshape(2, 2, 2, 48, 512)
        @pl.loop(0, 3, unroll=3)
        def _(n):
            cols = pl.ds(pl.multiple_of(n * 256, 256), 256)
            self.dn[m, :, :, :, cols] = tn(self.inner[...], self.dy[:, cols]).astype(BF).reshape(2, 4, 64, 256)

    def start_ff(self):
        self.norm(self.after_cross, self.nf, 2)
        self.oacc[...] = self.after_cross[...]
        self.gn[...] = jnp.zeros_like(self.gn)
    def end_ff(self):
        self.stage[...] = self.oacc[...].astype(BF)
    def back_ff_norm(self):
        def store(rows, dv):
            total = self.dy[rows, :].astype(F32) + dv
            self.oacc[rows, :] = total
            self.gb[rows, :] = total.astype(BF)
        self.norm_back(self.after_cross, 2, store)
    def back_cross_a(self):
        self.weight_grad_after(self.cctx, self.gb, 7, self.cctx)
    def weight_grad_after(self, ctx, grad, w, dst):
        self.back([(grad, w)], self.stage, BF)
        self.weight_grad(ctx, grad, w)
        dst[...] = self.stage[...]
    def back_cross_norm(self):
        def store(rows, dv):
            total = self.oacc[rows, :] + dv
            self.oacc[rows, :] = total
            self.gb[rows, :] = total.astype(BF)
        self.norm_back(self.after_self, 1, store)
    def back_self_a(self):
        self.weight_grad_after(self.ctx, self.gb, 3, self.ctx)
    def back_self_norm(self):
        def store(rows, dv):
            self.gb[rows, :] = (self.oacc[rows, :] + dv).astype(BF)
        self.norm_back(self.hid, 0, store)

def layer_scratch(trees):
    T = trees * TREE
    V = pltpu.VMEM
    b = lambda: V((T, SQ), BF)
    f = lambda: V((T, SQ), F32)
    d = {k: b() for k in ("ns", "q", "k", "v", "ctx", "nc", "cq", "ck", "cv", "cctx", "nf", "gb", "stage")}
    d.update({k: f() for k in ("after_self", "after_cross", "oacc", "gn")})
    d.update(ps=V((trees * H, TREE, TREE), BF), pc=V((trees * H, TREE, TREE), BF),
             mask=V((trees, TREE, TREE), F32), hot=V((trees, TREE, DEPTHS), BF), hot_t=V((trees, DEPTHS, TREE), BF),
             toep=V((H, DEPTHS, DEPTHS), BF), gains=V((16, SQ), F32), gain_grads=V((16, SQ), F32),
             bias_grads=V((128, 128), F32), inner=V((T, 512), BF), ggate=V((T, 512), BF), gup=V((T, 512), BF))
    return d


MESH = pl.DeviceIdType.MESH
TEAM_R, TEAM_S = 4, 8
NZ = TEAM_S // 2


class Team:
    def __init__(self, shard_count):
        self.fold = shard_count // TEAM_S
        r = lax.axis_index("replica")
        s = lax.axis_index("shard")
        self.base_r = (r // TEAM_R) * TEAM_R
        self.q = r % TEAM_R
        self.off_s = s % self.fold
        self.s = s // self.fold
        self.z = self.s // 2
        self.c = self.s % 2
        self.qx = self.q + 1 - 2 * (self.q % 2)
        self.qy = self.q + 2 - 4 * (self.q // 2)
        self.qd = 3 - self.q
        self.sib = self.dev(self.q, self.z * 2 + 1 - self.c)
        self.nb = (self.dev(self.qx, self.s), self.dev(self.qy, self.s))
        self.diag = self.dev(self.qd, self.s)
        self.qn = (self.qx, self.qy)

    def dev(self, q, s):
        return (self.base_r + q, s * self.fold + self.off_s)

    def zdev(self, k):
        return self.dev(self.q, ((self.z + k) % NZ) * 2 + self.c)

    def zsrc(self, k):
        return (self.z + NZ - k) % NZ


def rcopy(src, dst, send_sem, recv_sem, device):
    return pltpu.make_async_remote_copy(
        src_ref=src, dst_ref=dst, send_sem=send_sem, recv_sem=recv_sem, device_id=device, device_id_type=MESH
    )


class Sender:
    def __init__(self, team):
        self.t = team
        self.sends = {}

    def go(self, src, dst, send_sem, recv_sem, device, key=0):
        cp = rcopy(src, dst, send_sem, recv_sem, device)
        cp.start()
        self.sends.setdefault(key, []).append(cp)

    def got(self, ref, sem):
        rcopy(ref, ref, sem, sem, self.t.sib).wait_recv()

    def sent(self, key=0):
        for cp in self.sends.pop(key, ()):
            cp.wait_send()


PHASES = (
    ("sq", 0, 0, 256), ("sq", 0, 256, 512), ("sq", 4, 0, SQ), ("gu", 0, 0, 1024), ("dn", 0, 0, SQ), ("gu", 0, 1024, 1024),
)
AHEAD = 1


class Gather(Sender):
    def __init__(self, team, bufs, sems):
        super().__init__(team)
        self.done = [0, 0, 0]
        self.sq, self.gu, self.dn = bufs
        (self.zs, self.zr, self.xs, self.xr, self.ys, self.yr, self.dxs, self.dxr, self.dys, self.dyr, self.cs, self.cr) = sems

    def piece(self, p, q, z, half=None):
        kind, first, col, n = PHASES[p]
        c = self.t.c
        lo = col if half is None else col + half * (n // 2)
        w = n if half is None else n // 2
        if kind == "sq":
            ref = self.sq.at[first + q, z, c]
        elif kind == "gu":
            ref = self.gu.at[q // 2, z, c, q % 2]
        else:
            ref = self.dn.at[z, c, q]
        return ref.at[:, pl.ds(lo, w)]

    def all_of(self, p, z, c):
        kind, first, col, n = PHASES[p]
        cols = pl.ds(col, n)
        if kind == "sq":
            return self.sq.at[pl.ds(first, 4), z, c, :, cols]
        if kind == "gu":
            return self.gu.at[:, z, c, :, :, cols]
        return self.dn.at[z, c, :, :, cols]

    def begin(self, p):
        t = self.t
        ref = self.piece(p, t.q, t.z)
        for k in range(1, NZ):
            self.go(ref, ref, self.zs.at[p, k], self.zr.at[p, k], t.zdev(k), p)
        own = self.all_of(p, t.z, t.c)
        self.go(own, own, self.cs.at[p, 0], self.cr.at[p], t.sib, p)

    def zstep(self, p, k):
        t = self.t
        ref = self.piece(p, t.q, t.zsrc(k))
        self.got(ref, self.zr.at[p, k])
        self.go(ref, ref, self.xs.at[p, k], self.xr.at[p, k], t.nb[0], p)
        self.go(ref, ref, self.ys.at[p, k], self.yr.at[p, k], t.nb[1], p)
        self.go(ref, ref, self.cs.at[p, 5 * k - 4], self.cr.at[p], t.sib, p)

    def xystep(self, p, k):
        t = self.t
        z = t.zsrc(k)
        ref = self.piece(p, t.qx, z)
        self.got(ref, self.xr.at[p, k])
        h = self.piece(p, t.qx, z, 0)
        self.go(h, h, self.dys.at[p, k], self.dyr.at[p, k], t.nb[1], p)
        self.go(ref, ref, self.cs.at[p, 5 * k - 3], self.cr.at[p], t.sib, p)
        ref = self.piece(p, t.qy, z)
        self.got(ref, self.yr.at[p, k])
        h = self.piece(p, t.qy, z, 1)
        self.go(h, h, self.dxs.at[p, k], self.dxr.at[p, k], t.nb[0], p)
        self.go(ref, ref, self.cs.at[p, 5 * k - 2], self.cr.at[p], t.sib, p)

    def dstep(self, p, k):
        t = self.t
        z = t.zsrc(k)
        for half, sem, i in ((0, self.dyr, 1), (1, self.dxr, 0)):
            h = self.piece(p, t.qd, z, half)
            self.got(h, sem.at[p, k])
            self.go(h, h, self.cs.at[p, 5 * k - i], self.cr.at[p], t.sib, p)

    def run(self, nz, nx, nd):
        for i in range(max(self.done[0], nz)):
            for step, (what, upto) in enumerate(((self.zstep, nz), (self.xystep, nx), (self.dstep, nd))):
                n = self.done[step]
                if n < upto:
                    p, k = n // (NZ - 1), n % (NZ - 1) + 1
                    what(p, k)
                    self.done[step] += 1
                    if step == 0 and k == 1 and p + AHEAD < len(PHASES):
                        self.begin(p + AHEAD)

    def whole(self, p):
        self.got(self.all_of(p, slice(None), 1 - self.t.c), self.cr.at[p])


CHUNKS = (
    ("gu", 0, 0, 48, 0, 512),
    ("gu", 0, 0, 48, 512, 512),
    ("gu", 0, 0, 48, 1024, 512),
    ("gu", 0, 0, 48, 1536, 512),
    ("dn", 0, 0, 64, 0, SQ),
    ("sq", 4, 0, 48, 0, SQ),
    ("sq", 4, 48, 48, 0, SQ),
    ("sq", 0, 0, 48, 0, SQ),
    ("sq", 0, 48, 48, 0, SQ),
)
ENTRY = (0, 2, 3, 4, 5, 7, 8, 10, 11)
KINDS = {"sq": 0, "gu": 1, "dn": 2}
ROWS = (96, 48, 64)
LAND = (SQ, 1536, SQ)
STAGES = 7


class Reduce(Sender):
    def __init__(self, team, bufs, rc, r1, r2, rz, fin, sems):
        super().__init__(team)
        self.sq, self.gu, self.dn = bufs
        self.rc, self.r1, self.r2, self.rz, self.fin = rc, r1, r2, rz, fin
        (self.s_c, self.r_c, self.s_1, self.r_1, self.s_2, self.r_2, self.s_z, self.r_z, self.s_f, self.r_f) = sems

    def rows(self, ch):
        return pl.ds(ch[2], ch[3])

    def cols(self, ch, h=None):
        if h is None:
            return pl.ds(ch[4], ch[5])
        return pl.ds(ch[4] + h * (ch[5] // 2), ch[5] // 2)

    def land(self, ch):
        return pl.ds((ch[4] % LAND[KINDS[ch[0]]]) // 2, ch[5] // 2)

    def spot(self, ch):
        return pl.ds(ch[4] % LAND[KINDS[ch[0]]], ch[5])

    def view(self, ch, q, z, c, h=None):
        kind, w = ch[0], ch[1]
        rows, cols = self.rows(ch), self.cols(ch, h)
        if kind == "sq":
            return self.sq.at[w + q, z, c, rows, cols]
        if kind == "gu":
            return self.gu.at[q // 2, z, c, q % 2, rows, cols]
        return self.dn.at[z, c, q, rows, cols]

    def half(self, ch, c):
        kind, w = ch[0], ch[1]
        rows, cols = self.rows(ch), self.cols(ch)
        if kind == "sq":
            return self.sq.at[pl.ds(w, 4), :, c, rows, cols]
        if kind == "gu":
            return self.gu.at[:, :, c, :, rows, cols]
        return self.dn.at[:, c, :, rows, cols]

    def from_core(self, ch, q=None, z=None):
        b = self.rc[KINDS[ch[0]]]
        rows, cols = self.rows(ch), self.spot(ch)
        if ch[0] == "sq":
            return b.at[:, :, rows, cols] if q is None else b.at[q, z, rows, cols]
        if ch[0] == "gu":
            return b.at[:, :, :, rows, cols] if q is None else b.at[q // 2, z, q % 2, rows, cols]
        return b.at[:, :, rows, cols] if q is None else b.at[z, q, rows, cols]

    def final(self, ch):
        return self.fin[0 if ch[1] == 0 else 1] if ch[0] == "sq" else self.fin[1 + KINDS[ch[0]]]

    def stage(self, st, i):
        t, ch = self.t, CHUNKS[i]
        q, z, c = t.q, t.z, t.c
        kd = KINDS[ch[0]]
        rows, land = self.rows(ch), self.land(ch)
        if st == 0:
            self.go(self.half(ch, 1 - c), self.from_core(ch), self.s_c.at[i], self.r_c.at[i], t.sib)
        elif st == 1:
            self.got(self.from_core(ch), self.r_c.at[i])

            @pl.loop(0, 4 * NZ, unroll=4)
            def _(j):
                a, b = self.view(ch, j // NZ, j % NZ, c), self.from_core(ch, j // NZ, j % NZ)
                a[...] = a[...] + b[...]

            for h in range(2):
                for m, qq in enumerate((t.qn[h], t.qd)):
                    slot = (qq // 2) if h == 0 else (qq % 2)
                    self.go(
                        self.view(ch, qq, slice(None), c, h), self.r1[kd].at[h, slot, :, rows, land],
                        self.s_1.at[i, h, m], self.r_1.at[i, h, m], t.nb[h],
                    )
        elif st == 2:
            for h in range(2):
                for m, qq in ((1, t.qn[1 - h]), (0, q)):
                    slot = (qq // 2) if h == 0 else (qq % 2)
                    self.got(self.r1[kd].at[h, slot, :, rows, land], self.r_1.at[i, h, m])

                    @pl.loop(0, NZ, unroll=NZ)
                    def _(j):
                        a = self.view(ch, qq, j, c, h)
                        a[...] = a[...] + self.r1[kd][h, slot, j, rows, land]

            for h in range(2):
                self.go(
                    self.view(ch, t.qn[1 - h], slice(None), c, h), self.r2[kd].at[h, :, rows, land],
                    self.s_2.at[i, h], self.r_2.at[i, h], t.nb[1 - h],
                )
        elif st == 3:
            for h in range(2):
                self.got(self.r2[kd].at[h, :, rows, land], self.r_2.at[i, h])

                @pl.loop(0, NZ, unroll=NZ)
                def _(j):
                    a = self.view(ch, q, j, c, h)
                    a[...] = a[...] + self.r2[kd][h, j, rows, land]

            for k in range(1, NZ):
                self.go(
                    self.view(ch, q, (z + k) % NZ, c), self.rz[kd].at[k - 1, rows, self.spot(ch)],
                    self.s_z.at[i, k], self.r_z.at[i, k], t.zdev(k),
                )
        elif st == 4:
            v = self.view(ch, q, z, c)[...].astype(F32)
            for k in range(1, NZ):
                self.got(self.rz[kd].at[k - 1, rows, self.spot(ch)], self.r_z.at[i, k])
                v = v + self.rz[kd][k - 1, rows, self.spot(ch)].astype(F32)
            f = self.final(ch).at[q, rows, self.cols(ch)]
            f[...] = v.astype(BF)
            for h in range(2):
                self.go(f, f, self.s_f.at[i, h], self.r_f.at[i, h], t.nb[h])
        elif st == 5:
            for h in range(2):
                self.got(self.final(ch).at[t.qn[h], rows, self.cols(ch)], self.r_f.at[i, h])
                f = self.final(ch).at[t.qn[h], rows, self.cols(ch, h)]
                self.go(f, f, self.s_f.at[i, 2 + h], self.r_f.at[i, 2 + h], t.nb[1 - h])
        else:
            for h in range(2):
                self.got(self.final(ch).at[t.qd, rows, self.cols(ch, h)], self.r_f.at[i, 2 + h])

    def tick(self, n):
        for st in (1, 0, 6, 5, 4, 3, 2):
            for i, entry in enumerate(ENTRY):
                if n - entry == st:
                    self.stage(st, i)


def layer_kernel(names, shards, trees, *refs):
    seg_start, seg_parent, bucket, *gains_in, bias_in, hid_in, enc_in, dy_in = refs[:10]
    weights = refs[10:21]
    lo, gh, ge, f0, f1, f2, f3, small_fin = refs[21:29]
    r = dict(zip(names, refs[29:]))
    bufs = (r["sq"], r["gu"], r["dn"])
    t = Team(shards)
    L = Layer(dict(r, seg_start=seg_start, seg_parent=seg_parent, bucket=bucket), trees)
    G = Gather(t, bufs, [r["g%d" % i] for i in range(12)])
    R = Reduce(
        t, bufs, [r["rc0"], r["rc1"], r["rc2"]], [r["ra0"], r["ra1"], r["ra2"]], [r["rb0"], r["rb1"], r["rb2"]],
        [r["rz0"], r["rz1"], r["rz2"]], (f0, f1, f2, f3), [r["r%d" % i] for i in range(10)],
    )
    S = Sender(t)

    loc, lsem = [], r["local"]

    def fetch(src, dst):
        cp = pltpu.make_async_copy(src, dst, lsem.at[len(loc)])
        cp.start()
        loc.append(cp)

    z, c = t.z, t.c
    for i in range(8):
        fetch(weights[i], r["sq"].at[i, z, c])
    for i in range(2):
        for h in range(2):
            fetch(weights[8 + i].at[pl.ds(h * 48, 48)], r["gu"].at[i, z, c, h])
    for h in range(4):
        fetch(weights[10].at[pl.ds(h * 64, 64)], r["dn"].at[z, c, h])
    fetch(hid_in, r["hid"])
    fetch(enc_in, r["enc"])
    fetch(dy_in, r["dy"])

    others = [t.dev(t.q, (t.s + k) % TEAM_S) for k in range(1, TEAM_S)]
    greet = others + list(t.nb) + [t.diag]
    barrier = pltpu.get_barrier_semaphore()
    for d in greet:
        pl.semaphore_signal(barrier, inc=1, device_id=d, device_id_type=MESH)
    pl.semaphore_wait(barrier, len(greet))
    for cp in loc[:4]:
        cp.wait()
    for p in range(AHEAD):
        G.begin(p)

    small, mix = r["small"], r["mix"]
    mix[...] = jnp.zeros_like(mix)
    for i in range(3):
        mix[i:i + 1, :96] = gains_in[i][...].astype(F32)
    mix[4:8, :H] = bias_in[...].astype(F32)
    small[t.s] = mix[...].astype(BF)
    for k in range(1, TEAM_S):
        S.go(small.at[t.s], small.at[t.s], r["ss"].at[0, k], r["sr"].at[0, k], others[k - 1])
    L.layout()
    for cp in loc[4:]:
        cp.wait()
    G.run(1, 0, 0)
    for k in range(1, TEAM_S):
        S.got(small.at[(t.s + TEAM_S - k) % TEAM_S], r["sr"].at[0, k])
    L.small_params()
    G.run(2, 1, 0)
    L.norm(r["hid"], r["ns"], 0)
    G.run(3, 2, 1)
    G.run(4, 3, 2)
    G.run(5, 4, 3)
    own = (r["q"], r["k"], r["v"], r["ctx"], r["ps"], True)
    cross = (r["cq"], r["ck"], r["cv"], r["cctx"], r["pc"], False)
    G.whole(0)
    for w in range(3):
        L.project(r["ns"], w, own[w], 0, 1)
    G.run(6, 5, 4)
    L.attend(*own, 0, 3)
    G.run(7, 6, 5)
    G.run(8, 7, 6)
    G.run(9, 7, 6)
    G.whole(1)
    for w in range(3):
        L.project(r["ns"], w, own[w], 1, 3)
    L.attend(*own, 3, 6)
    G.run(10, 8, 6)
    L.attend(*own, 6, 12)
    G.run(11, 9, 7)
    L.project_add(r["ctx"], 3, r["hid"], r["after_self"])
    L.norm(r["after_self"], r["nc"], 1)
    G.run(12, 10, 8)
    G.run(13, 11, 9)
    G.whole(2)
    for w, src in enumerate((r["nc"], r["enc"], r["enc"])):
        L.project(src, 4 + w, cross[w])
    G.run(14, 12, 10)
    L.attend(*cross, 0, 6)
    G.run(15, 13, 11)
    L.attend(*cross, 6, 12)
    G.run(16, 14, 12)
    L.project_add(r["cctx"], 7, r["after_self"], r["after_cross"])
    L.start_ff()
    G.run(17, 15, 13)
    G.run(18, 16, 14)
    G.run(18, 17, 15)
    for p in (3, 4):
        G.whole(p)
        G.sent(p)

    L.feed_forward(0)
    G.run(18, 18, 17)
    R.tick(0)
    G.run(18, 18, 18)
    R.tick(1)
    L.feed_forward(1)
    R.tick(2)
    G.whole(5)
    for p in (5, 0, 1, 2):
        G.sent(p)
    S.sent()
    for m in (2, 3):
        L.feed_forward(m)
        R.tick(m + 1)
    L.end_ff()
    out0 = pltpu.make_async_copy(r["stage"], lo, lsem.at[0])
    out0.start()
    L.back_ff_norm()
    out0.wait()
    L.back_cross_a()
    R.tick(5)
    L.attend_back(*cross, 0, 6)
    R.tick(6)
    L.attend_back(*cross, 6, 12)
    L.back([(r["ck"], 5), (r["cv"], 6)], r["stage"], BF)
    out1 = pltpu.make_async_copy(r["stage"], ge, lsem.at[1])
    out1.start()
    L.back([(r["cq"], 4)], r["gn"], F32)
    L.weight_grad(r["nc"], r["cq"], 4)
    L.weight_grad(r["enc"], r["ck"], 5)
    L.weight_grad(r["enc"], r["cv"], 6)
    R.tick(7)
    L.back_cross_norm()
    out1.wait()
    L.back_self_a()
    L.attend_back(*own, 0, 3)
    R.tick(8)
    L.attend_back(*own, 3, 9)
    R.tick(9)
    L.attend_back(*own, 9, 12)
    L.back([(r["q"], 0), (r["k"], 1), (r["v"], 2)], r["gn"], F32)
    L.weight_grad(r["ns"], r["q"], 0)
    L.weight_grad(r["ns"], r["k"], 1)
    L.weight_grad(r["ns"], r["v"], 2)
    R.tick(10)
    L.back_self_norm()
    out2 = pltpu.make_async_copy(r["gb"], gh, lsem.at[2])
    out2.start()
    L.small_grads()
    so, sa, sb = r["small_out"], r["small_a"], r["small_b"]
    for k in range(1, TEAM_S):
        S.go(so.at[(t.s + k) % TEAM_S], sa.at[t.s], r["ss"].at[1, k], r["sr"].at[1, k], others[k - 1])
    sa[t.s] = so[t.s]
    R.tick(11)
    for k in range(1, TEAM_S):
        S.got(sa.at[(t.s + TEAM_S - k) % TEAM_S], r["sr"].at[1, k])
    sb[t.q] = jnp.sum(sa[...].astype(F32), axis=0).astype(BF)
    for k, (qq, d) in enumerate(((t.qx, t.nb[0]), (t.qy, t.nb[1]), (t.qd, t.diag))):
        S.go(sb.at[t.q], sb.at[t.q], r["ss"].at[2, k], r["sr"].at[2, k], d)
    last = max(ENTRY) + STAGES
    R.tick(12)
    for k, qq in enumerate((t.qx, t.qy, t.qd)):
        S.got(sb.at[qq], r["sr"].at[2, k])
    small_fin[...] = jnp.sum(sb[...].astype(F32), axis=0)
    for n in range(13, last):
        R.tick(n)
    R.sent()
    S.sent()
    out2.wait()


def layer(seg_start, seg_parent, bucket, gains, bias, hid, enc, dy, weights, shards):
    trees = seg_start.shape[0]
    tokens = trees * TREE
    V, D = pltpu.VMEM, pltpu.SemaphoreType.DMA
    act = lambda: V((tokens, SQ), BF)
    n, p = len(CHUNKS), len(PHASES)
    scratch = dict(
        sq=V((8, NZ, 2, 96, SQ), BF), gu=V((2, NZ, 2, 2, 48, FFN), BF), dn=V((NZ, 2, 4, 64, SQ), BF),
        rc0=V((4, NZ, 96, SQ), BF), rc1=V((2, NZ, 2, 48, LAND[1]), BF), rc2=V((NZ, 4, 64, SQ), BF),
        hid=act(), enc=act(), dy=act(), local=D((20,)),
        small=V((8, 16, 128), BF), small_out=V((8, 16, 128), BF), small_a=V((8, 16, 128), BF), small_b=V((4, 16, 128), BF),
        ss=D((3, 8)), sr=D((3, 8)), mix=V((16, 128), F32),
    )
    for i in range(3):
        scratch["ra%d" % i] = V((2, 2, NZ, ROWS[i], LAND[i] // 2), BF)
        scratch["rb%d" % i] = V((2, NZ, ROWS[i], LAND[i] // 2), BF)
        scratch["rz%d" % i] = V((NZ - 1, ROWS[i], LAND[i]), BF)
    for i in range(12):
        scratch["g%d" % i] = D((p, 16)) if i == 10 else D((p,)) if i == 11 else D((p, NZ))
    for i, shape in enumerate([(n,), (n,), (n, 2, 2), (n, 2, 2), (n, 2), (n, 2), (n, NZ), (n, NZ), (n, 4), (n, 4)]):
        scratch["r%d" % i] = D(shape)
    scratch.update(layer_scratch(trees))
    hbm, vmem, smem = (pl.BlockSpec(memory_space=m) for m in (pltpu.HBM, pltpu.VMEM, pltpu.SMEM))
    sd = jax.ShapeDtypeStruct
    return pl.pallas_call(
        functools.partial(layer_kernel, list(scratch), shards, trees),
        out_shape=[sd((tokens, SQ), BF)] * 3
        + [sd((4, 96, SQ), BF), sd((4, 96, SQ), BF), sd((4, 48, FFN), BF), sd((4, 64, SQ), BF), sd((16, 128), F32)],
        in_specs=[smem, smem] + [vmem] * 5 + [hbm] * 14,
        out_specs=[hbm] * 3 + [vmem] * 5,
        scratch_shapes=list(scratch.values()),
        compiler_params=pltpu.CompilerParams(collective_id=0, has_side_effects=True, vmem_limit_bytes=64 * 2**20 - 65536),
        name="decoder_layer",
    )(seg_start, seg_parent, bucket, *gains, bias, hid, enc, dy, *weights)


def finish_kernel(lo, gh, ge, f0, f1, f2, f3, small, *refs):
    o_lo, o_gh, o_ge = refs[:3]
    squares, gate, up, down = refs[3:11], refs[11], refs[12], refs[13]
    norms, table = refs[14:17], refs[17]
    a0, a1, a2, b0, b1, b2, b3, w0, w1, w2, w3, sem_in, sem_out = refs[18:]
    pairs = ((f0, b0), (f1, b1), (f2, b2), (f3, b3), (lo, a0), (gh, a1), (ge, a2))
    ins = [pltpu.make_async_copy(a, b, sem_in.at[i]) for i, (a, b) in enumerate(pairs)]
    for cp in ins:
        cp.start()
    for i in range(3):
        norms[i][...] = small[i:i + 1, :96]
    table[...] = small[4:8, :H]
    outs = []

    def out(src, dst):
        cp = pltpu.make_async_copy(src, dst, sem_out.at[len(outs)])
        cp.start()
        outs.append(cp)

    for n, (b, w) in enumerate(((b0, w0), (b1, w1))):
        ins[n].wait()
        for i in range(4):
            w[i] = b[i].astype(F32)
            out(w.at[i], squares[4 * n + i])
    ins[2].wait()
    for i, dst in enumerate((gate, up)):
        w2[i] = b2[2 * i:2 * i + 2].reshape(96, FFN).astype(F32)
        out(w2.at[i], dst)
    ins[3].wait()
    w3[...] = b3[...].reshape(256, SQ).astype(F32)
    out(w3, down)
    for i, dst in enumerate((o_lo, o_gh, o_ge)):
        ins[4 + i].wait()
        out((a0, a1, a2)[i], dst)
    for cp in outs:
        cp.wait()


def finish(outs):
    hbm, vmem = pl.BlockSpec(memory_space=pltpu.HBM), pl.BlockSpec(memory_space=pltpu.VMEM)
    V, sd = pltpu.VMEM, jax.ShapeDtypeStruct
    res = pl.pallas_call(
        finish_kernel,
        out_shape=[sd(o.shape, BF) for o in outs[:3]] + [sd((96, SQ), F32)] * 8 + [sd((96, FFN), F32)] * 2
        + [sd((256, SQ), F32)] + [sd((1, 96), F32)] * 3 + [sd((4, H), F32)],
        in_specs=[hbm] * 7 + [vmem],
        out_specs=[hbm] * 14 + [vmem] * 4,
        scratch_shapes=[V(o.shape, BF) for o in outs[:7]]
        + [V((4, 96, SQ), F32), V((4, 96, SQ), F32), V((2, 96, FFN), F32), V((256, SQ), F32)]
        + [pltpu.SemaphoreType.DMA((7,)), pltpu.SemaphoreType.DMA((14,))],
        compiler_params=pltpu.CompilerParams(vmem_limit_bytes=63 * 2**20),
        name="finish",
    )(*outs)
    return (*res[:3], res[3:11], res[11], res[12], res[13], res[14:17], res[17])


def team_rows(weight, fold):
    if fold == 1:
        return weight
    groups = [[a * fold + b for b in range(fold)] for a in range(TEAM_S)]
    return lax.all_gather(weight, "shard", axis=0, tiled=True, axis_index_groups=groups)


def team_sum(grad, fold, teams_r):
    if fold > 1:
        groups = [[a * fold + b for b in range(fold)] for a in range(TEAM_S)]
        grad = lax.psum_scatter(grad, "shard", scatter_dimension=0, tiled=True, axis_index_groups=groups)
    if teams_r > 1:
        groups = [[a * TEAM_R + b for a in range(teams_r)] for b in range(TEAM_R)]
        grad = lax.psum(grad, "replica", axis_index_groups=groups)
    return grad


def body(
    replicas, shards,
    hidden, encoded, out_grad, seg_start, seg_parent, bucket_of_distance,
    norm_self, self_query, self_key, self_value, self_out, rel_bias,
    norm_cross, cross_query, cross_key, cross_value, cross_out,
    norm_ff, ff_gate, ff_up, ff_down,
):
    fold, teams_r = shards // TEAM_S, replicas // TEAM_R
    big = (self_query, self_key, self_value, self_out, cross_query, cross_key, cross_value, cross_out, ff_gate, ff_up, ff_down)
    flat = lambda v: v.reshape(-1, v.shape[-1])
    outs = layer(
        flat(seg_start), flat(seg_parent), bucket_of_distance.reshape(2, 128),
        [team_rows(g, fold).reshape(1, -1) for g in (norm_self, norm_cross, norm_ff)], team_rows(rel_bias, fold),
        flat(hidden), flat(encoded), flat(out_grad), [team_rows(w, fold) for w in big], shards,
    )
    lo, gh, ge, squares, gate, up, down, norms, table = finish(outs)
    squares = [team_sum(v, fold, teams_r) for v in squares]
    gate, up, down, table = (team_sum(v, fold, teams_r) for v in (gate, up, down, table))
    norms = [team_sum(v.reshape(-1), fold, teams_r) for v in norms]
    lo, gh, ge = (v.reshape(hidden.shape) for v in (lo, gh, ge))
    return (
        lo, gh, ge, norms[0], *squares[:4], table, norms[1], *squares[4:], norms[2], gate, up, down,
    )


def solution(mesh):
    placed = (
        P(None, ("replica", "shard"), None, None),
        P(None, ("replica", "shard"), None, None),
        P(None, ("replica", "shard"), None, None),
        P(None, ("replica", "shard"), None),
        P(None, ("replica", "shard"), None),
        P(),
        P("shard"),
        P("shard", None),
        P("shard", None),
        P("shard", None),
        P("shard", None),
        P("shard", None),
        P("shard"),
        P("shard", None),
        P("shard", None),
        P("shard", None),
        P("shard", None),
        P("shard"),
        P("shard", None),
        P("shard", None),
        P("shard", None),
    )
    return jax.shard_map(
        functools.partial(body, mesh.shape["replica"], mesh.shape["shard"]),
        mesh=mesh,
        in_specs=placed,
        out_specs=(
            P(None, ("replica", "shard"), None, None),
            P(None, ("replica", "shard"), None, None),
            P(None, ("replica", "shard"), None, None),
            P("shard"),
            P("shard", None),
            P("shard", None),
            P("shard", None),
            P("shard", None),
            P("shard", None),
            P("shard"),
            P("shard", None),
            P("shard", None),
            P("shard", None),
            P("shard", None),
            P("shard"),
            P("shard", None),
            P("shard", None),
            P("shard", None),
        ),
        check_vma=False,
    )
```
